32 devices in a mesh: dp: 4 (over y, x), head: 8 (over z, core).
Axes of the slice: x: 2, y: 2, z: 4, core: 2. Of those that a mesh axis runs over, the one named last changes fastest.
Arguments:
- query_latent: bfloat16 [1024, 1536], P('dp'), may hold values from -384 to 384
- kv_latent: bfloat16 [1024, 576], P('dp'), may hold values from -48 to 48
- out_grad: bfloat16 [1024, 4096], P('dp', 'head'), may hold values from -20 to 20
- query_up: bfloat16 [1536, 6144], P(None, 'head'), may hold values from -1 to 1
- key_up: bfloat16 [512, 4096], P(None, 'head'), may hold values from -0.25 to 0.25
- value_up: bfloat16 [512, 4096], P(None, 'head'), may hold values from -0.25 to 0.25
Outputs:
- query_latent_grad: float32 [1024, 1536], P(('dp', 'head'))
- kv_latent_grad: float32 [1024, 576], P(('dp', 'head'))
- query_up_grad: bfloat16 [1536, 6144], P(None, 'head')
- key_up_grad: bfloat16 [512, 4096], P(None, 'head')
- value_up_grad: bfloat16 [512, 4096], P(None, 'head')
The draws below stay inside these ranges and needn't reach their ends.
All inputs are finite; a program needn't handle non-finite values.
Results may differ from the reference program's by a relative error of at most 0.035.
Values may be sent and summed in bfloat16 or wider, within the bound.
No kernel may reach another device: no remote copies, remote signals or barrier semaphores. Data moves between devices by JAX's collectives and lax.ppermute only.
A program may use at most 64 MiB of HBM per device.

```python
import math
import jax
import jax.numpy as jnp
from jax import lax

QL = 1536
KL = 512
DN = 128
DR = 64
HD_DEV = 4
LENGTH = 256
HEADS = 32
ROWS = 1024
N_DP = 4
N_HEAD = 8


def base_field(key, shape):
    return jnp.clip(jax.random.normal(key, shape, jnp.float32), -6.0, 6.0)


def up_weights(key):
    weight_key = jax.random.fold_in(key, 202)
    raw_field = base_field(weight_key, (QL, HEADS * (DN + DR)))
    weights = (raw_field / math.sqrt(QL)).astype(jnp.bfloat16).astype(jnp.float32)
    return weights


def draw_query_up(key, part):
    return up_weights(key).astype(jnp.bfloat16)


def draw_out_grad(key, part):
    grad_key = jax.random.fold_in(key, 505)
    raw_field = base_field(grad_key, (ROWS, HEADS * DN))
    head_index = (jnp.arange(HEADS * DN, dtype=jnp.int32) // DN).astype(jnp.float32)
    rise = math.sqrt(10.0)
    gain = rise ** (head_index / max(HEADS - 1, 1))
    return (raw_field * gain[None, :]).astype(jnp.bfloat16)


def draw_query_latent(key, part):
    latent_key = jax.random.fold_in(key, 303)
    raw_field = base_field(latent_key, (ROWS, QL))
    return raw_field.astype(jnp.bfloat16)


def draw_kv_latent(key, part):
    kv_key = jax.random.fold_in(key, 404)
    raw_field = base_field(kv_key, (ROWS, KL + DR))
    return raw_field.astype(jnp.bfloat16)


def shard_levels(key, shape, pieces, least, largest):
    level = 1.0
    for position, blocks in pieces:
        heights = jax.random.uniform(jax.random.fold_in(jax.random.fold_in(key, 6), position), (blocks,), jnp.float32, least / len(pieces), largest / len(pieces))
        level = level * jnp.repeat(jnp.exp(heights), shape[position] // blocks).reshape((-1,) + (1,) * (len(shape) - 1 - position))
    return level


def scatter_about(key, shape, scale, reach, cuts=(), kind=jnp.bfloat16):
    values = scale * jax.random.normal(key, shape, jnp.float32)
    if cuts:
        values = values * shard_levels(key, shape, cuts, -0.22, 0.18)
    return jnp.clip(values, -reach, reach).astype(kind)


def setup_inputs(seed: int = 0) -> dict:
    arg_keys = jax.random.split(jax.random.key(seed), 7)
    query_latent = draw_query_latent(jax.random.fold_in(arg_keys[6], 71), 0)
    kv_latent = draw_kv_latent(jax.random.fold_in(arg_keys[6], 71), 0)
    out_grad = draw_out_grad(jax.random.fold_in(arg_keys[6], 71), 0)
    query_up = draw_query_up(jax.random.fold_in(arg_keys[6], 71), 0)
    key_up = scatter_about(arg_keys[4], (KL, HEADS * DN), KL ** -0.5, 0.25, ((1, 8),))
    value_up = scatter_about(arg_keys[5], (KL, HEADS * DN), KL ** -0.5, 0.25, ((1, 8),))
    return {"query_latent": query_latent, "kv_latent": kv_latent, "out_grad": out_grad, "query_up": query_up, "key_up": key_up, "value_up": value_up}


max_rms = 1.0
eps = 1e-06

def rotate(values, length):
    half = values.shape[-1] // 2
    freqs = 10000.0 ** (-2.0 * jnp.arange(half, dtype=jnp.float32) / values.shape[-1])
    angle = jnp.arange(length, dtype=jnp.float32)[:, None] * freqs[None, :]
    cosine = jnp.cos(angle)[:, None, :]
    sine = jnp.sin(angle)[:, None, :]
    first = values[..., :half]
    second = values[..., half:]
    return jnp.concatenate([first * cosine - second * sine, second * cosine + first * sine], axis=-1)

def attend(q_plain, q_rot, keys, key_rot, values):
    length = q_plain.shape[0]
    q_rope = rotate(q_rot.astype(jnp.float32), length).astype(jnp.bfloat16)
    scale = 1.0 / (q_plain.shape[-1] + q_rot.shape[-1]) ** 0.5
    scores = jnp.einsum('shd,thd->hst', q_plain, keys, preferred_element_type=jnp.float32)
    scores = scores + jnp.einsum('shd,thd->hst', q_rope, key_rot, preferred_element_type=jnp.float32)
    scores = scores * scale
    positions = jnp.arange(length)
    allowed = positions[None, :] <= positions[:, None]
    scores = jnp.where(allowed[None], scores, -jnp.inf)
    top = lax.stop_gradient(lax.optimization_barrier(jnp.max(scores, axis=-1, keepdims=True)))
    weights = jnp.exp(scores - top)
    probs = (weights / lax.optimization_barrier(jnp.sum(weights, axis=-1, keepdims=True))).astype(jnp.bfloat16)
    return jnp.einsum('hst,thd->shd', probs, values, preferred_element_type=jnp.float32)

def local_grads(query_latent, kv_latent, out_grad, query_up, key_up, value_up):
    length = query_latent.shape[0]
    heads = key_up.shape[1] // DN
    queries = jnp.dot(query_latent, query_up, preferred_element_type=jnp.float32).astype(jnp.bfloat16)
    queries = queries.reshape(length, heads, DN + DR)
    plain_latent = kv_latent[:, :KL]
    keys = jnp.dot(plain_latent, key_up, preferred_element_type=jnp.float32).astype(jnp.bfloat16).reshape(length, heads, DN)
    values = jnp.dot(plain_latent, value_up, preferred_element_type=jnp.float32).astype(jnp.bfloat16).reshape(length, heads, DN)
    key_rot = jnp.broadcast_to(kv_latent[:, None, KL:], (length, heads, DR))
    attn, pull = jax.vjp(attend, queries[..., :DN], queries[..., DN:], keys, key_rot, values)
    grad_plain, grad_rot, key_grad, rot_grad, value_grad = pull(out_grad.reshape(length, heads, DN).astype(jnp.float32))
    q_grad = jnp.concatenate([grad_plain, grad_rot], axis=-1).reshape(length, heads * (DN + DR))
    rot_sum = lax.optimization_barrier(jnp.sum(rot_grad.astype(jnp.float32), axis=1))
    return (q_grad, key_grad.reshape(length, heads * DN), value_grad.reshape(length, heads * DN), rot_sum)

def transposed(left, right):
    return lax.dot_general(left, right, (((1,), (1,)), ((), ())), preferred_element_type=jnp.float32)

def reference(query_latent, kv_latent, out_grad, query_up, key_up, value_up):
    width_q = HD_DEV * (DN + DR)
    width_k = HD_DEV * DN
    wq_blocks = query_up.reshape(QL, N_HEAD, width_q).transpose(1, 0, 2)
    wk_blocks = key_up.reshape(KL, N_HEAD, width_k).transpose(1, 0, 2)
    wv_blocks = value_up.reshape(KL, N_HEAD, width_k).transpose(1, 0, 2)
    cq_groups = query_latent.reshape(N_DP, LENGTH, QL)
    kv_groups = kv_latent.reshape(N_DP, LENGTH, KL + DR)
    do_groups = out_grad.reshape(N_DP, LENGTH, N_HEAD, width_k).transpose(0, 2, 1, 3)

    def per_group(carry, xs):
        cq_g, kv_g, do_g = xs

        def per_block(block_xs):
            wq_h, wk_h, wv_h, do_h = block_xs
            q_grad, key_grad, value_grad, rot_sum = local_grads(cq_g, kv_g, do_h, wq_h, wk_h, wv_h)
            plain_latent = kv_g[:, :KL]
            grad_wq = jnp.dot(cq_g.T, q_grad, preferred_element_type=jnp.float32)
            grad_wk = jnp.dot(plain_latent.T, key_grad, preferred_element_type=jnp.float32)
            grad_wv = jnp.dot(plain_latent.T, value_grad, preferred_element_type=jnp.float32)
            term_q = transposed(q_grad, wq_h)
            term_kv = transposed(key_grad, wk_h) + transposed(value_grad, wv_h)
            return (grad_wq, grad_wk, grad_wv, term_q, term_kv, rot_sum)
        grad_wq, grad_wk, grad_wv, term_q, term_kv, rot_sum = lax.map(per_block, (wq_blocks, wk_blocks, wv_blocks, do_g))
        carry = (carry[0] + grad_wq, carry[1] + grad_wk, carry[2] + grad_wv)
        latent_q = lax.optimization_barrier(jnp.sum(term_q, axis=0))
        latent_kv = jnp.concatenate([lax.optimization_barrier(jnp.sum(term_kv, axis=0)), lax.optimization_barrier(jnp.sum(rot_sum, axis=0))], axis=1)
        return (carry, (latent_q, latent_kv))
    start = (jnp.zeros((N_HEAD, QL, width_q), jnp.float32), jnp.zeros((N_HEAD, KL, width_k), jnp.float32), jnp.zeros((N_HEAD, KL, width_k), jnp.float32))
    sums, latents = lax.scan(per_group, start, (cq_groups, kv_groups, do_groups))
    grad_wq = sums[0].transpose(1, 0, 2).reshape(QL, N_HEAD * width_q)
    grad_wk = sums[1].transpose(1, 0, 2).reshape(KL, N_HEAD * width_k)
    grad_wv = sums[2].transpose(1, 0, 2).reshape(KL, N_HEAD * width_k)
    total = jnp.sum(grad_wq * grad_wq) + jnp.sum(grad_wk * grad_wk) + jnp.sum(grad_wv * grad_wv)
    count = QL * N_HEAD * width_q + 2 * KL * N_HEAD * width_k
    factor = jnp.minimum(1.0, max_rms * count ** 0.5 / jnp.sqrt(total + eps))
    query_latent_grad = latents[0].reshape(ROWS, QL)
    kv_latent_grad = latents[1].reshape(ROWS, KL + DR)
    return (query_latent_grad, kv_latent_grad, (grad_wq * factor).astype(jnp.bfloat16), (grad_wk * factor).astype(jnp.bfloat16), (grad_wv * factor).astype(jnp.bfloat16))
```

```python
import functools

import jax
import jax.numpy as jnp
import numpy as np
from jax import lax
from jax.experimental import pallas as pl
from jax.experimental.pallas import tpu as pltpu
from jax.sharding import PartitionSpec as P

QL = 1536
KL = 512
DN = 128
DR = 64
TILE = 128
WIDTH = DN + DR
PAIR = 2 * WIDTH
LATENT = QL + KL + DR

max_rms = 1.0
eps = 1e-06
VMEM_LIMIT = 48 * 2**20

NT = (((1,), (1,)), ((), ()))
TN = (((0,), (0,)), ((), ()))


def dot(left, right, dims=(((1,), (0,)), ((), ()))):
    return lax.dot_general(left, right, dims, preferred_element_type=jnp.float32)


def rotary_tables(length):
    half = DR // 2
    freqs = np.float32(10000.0) ** (
        np.float32(-2.0) * np.arange(half, dtype=np.float32) / np.float32(DR)
    )
    angle = np.arange(length, dtype=np.float32)[:, None] * freqs.astype(np.float32)[None, :]
    cosine, sine = np.cos(angle), np.sin(angle)
    ones, zeros = np.ones((length, DR), np.float32), np.zeros((length, DR), np.float32)
    rot_cos = np.concatenate([cosine, cosine], axis=1)
    rot_sin = np.concatenate([-sine, sine], axis=1)
    return np.concatenate([rot_cos, ones, ones, rot_cos, rot_sin, zeros, zeros, rot_sin], axis=1)


def swap_halves(tile):
    lane = lax.broadcasted_iota(jnp.int32, tile.shape, 1)
    first = lane % DR < DR // 2
    return jnp.where(
        first, pltpu.roll(tile, TILE - DR // 2, 1), pltpu.roll(tile, DR // 2, 1)
    )


def rounded(values):
    return values.astype(jnp.bfloat16).astype(jnp.float32)


def backward(xq, xkv, grad, wq, wk, wv, table, gq, gk, gv):
    length = xq.shape[0]
    heads = wk.shape[1] // DN
    scale = 1.0 / (DN + DR) ** 0.5
    low = lax.broadcasted_iota(jnp.int32, (length, TILE), 1) < DR
    token = lax.broadcasted_iota(jnp.int32, (length, length), 0)
    query = lax.broadcasted_iota(jnp.int32, (length, length), 1)
    allowed = token <= query
    cos_tiles = [table[:, 0:TILE], table[:, TILE : 2 * TILE]]
    sin_tiles = [table[:, 2 * TILE : 3 * TILE], table[:, 3 * TILE : 4 * TILE]]
    latent = xkv[:, :KL]
    rot = jnp.concatenate(
        [xkv[:, KL : KL + DR].astype(jnp.float32), jnp.zeros((length, DR), jnp.float32)], axis=1
    )
    rot_high = pltpu.roll(rot, DR, 1)
    rot_sum = jnp.zeros((length, TILE), jnp.float32)
    for pair in range(heads // 2):
        queries = rounded(dot(xq[...], wq[:, PAIR * pair : PAIR * (pair + 1)]))
        tiles = [queries[:, :TILE]]
        for i in range(2):
            part = queries[:, (i + 1) * TILE : (i + 2) * TILE]
            tiles.append(part * cos_tiles[i] + swap_halves(part) * sin_tiles[i])
        tiles = [tile.astype(jnp.bfloat16) for tile in tiles]
        columns = slice(2 * DN * pair, 2 * DN * (pair + 1))
        keys = dot(latent, wk[:, columns])
        values = dot(latent, wv[:, columns]).astype(jnp.bfloat16)
        odd = pltpu.roll(keys[:, DN:], DR, 1)
        key_windows = (
            jnp.concatenate([keys[:, :DN], rot], axis=1).astype(jnp.bfloat16),
            jnp.concatenate([jnp.where(low, 0.0, odd), jnp.where(low, odd, rot_high)], axis=1).astype(
                jnp.bfloat16
            ),
        )
        query_parts = []
        for side in range(2):
            head = slice((2 * pair + side) * DN, (2 * pair + side + 1) * DN)
            query_window = jnp.concatenate(tiles[side : side + 2], axis=1)
            key_window = key_windows[side]
            scores = dot(key_window, query_window, NT) * scale
            scores = jnp.where(allowed, scores, -jnp.inf)
            weights = jnp.exp(scores - jnp.max(scores, axis=0, keepdims=True))
            probs = weights * (1.0 / jnp.sum(weights, axis=0, keepdims=True))
            grad_head = grad[:, head]
            grad_probs = rounded(dot(values[:, DN * side : DN * (side + 1)], grad_head, NT))
            mean = jnp.sum(grad_probs * probs, axis=0, keepdims=True)
            grad_scores = (probs * (grad_probs - mean) * scale).astype(jnp.bfloat16)
            gv[:, head] = dot(probs.astype(jnp.bfloat16), grad_head).astype(jnp.bfloat16)
            key_part = dot(grad_scores, query_window)
            query_parts.append(dot(grad_scores, key_window, TN))
            if side == 0:
                gk[:, head] = key_part[:, :TILE].astype(jnp.bfloat16)
                rot_sum = rot_sum + rounded(key_part[:, TILE:])
            else:
                turned = pltpu.roll(key_part[:, TILE:], DR, 1)
                gk[:, head] = jnp.where(low, pltpu.roll(key_part[:, :TILE], DR, 1), turned).astype(
                    jnp.bfloat16
                )
                rot_sum = rot_sum + rounded(turned)
        even, uneven = query_parts
        parts = [even[:, :TILE], even[:, TILE:] + uneven[:, :TILE], uneven[:, TILE:]]
        for i in range(2):
            part = rounded(parts[i + 1])
            parts[i + 1] = part * cos_tiles[i] - swap_halves(part) * sin_tiles[i]
        for i in range(3):
            start = PAIR * pair + i * TILE
            gq[:, start : start + TILE] = parts[i].astype(jnp.bfloat16)
    return rot_sum


def raw_grads(xq, xkv, gq, gk, gv, sums, previous, squares):
    total = jnp.zeros((8, TILE), jnp.float32)
    blocks = [(xq, gq, i) for i in range(QL // 512)] + [(xkv, gk, 0), (xkv, gv, 0)]
    for index, (left, right, i) in enumerate(blocks):
        which = max(index - QL // 512 + 1, 0)
        rows = slice(i * 512, (i + 1) * 512)
        product = dot(left[:, rows], right[...], TN)
        if previous is not None:
            product = product + previous[which][rows, :]
        sums[which][rows, :] = product
        if squares is not None:
            square = product * product
            square = jnp.sum(square.reshape(512 // 8, 8, square.shape[1]), axis=0)
            for column in range(0, square.shape[1], TILE):
                total = total + square[:, column : column + TILE]
    if squares is not None:
        squares[...] = total


def own_kernel(n_head, place, xq, xkv, grad, wq, wk, wv, table, sq, sk, sv, keep, send, gq, gk, gv, term):
    rot_sum = backward(xq, xkv, grad, wq, wk, wv, table, gq, gk, gv)
    term[:, :QL] = dot(gq[...], wq[...], NT)
    term[:, QL : QL + KL] = dot(gk[...], wk[...], NT) + dot(gv[...], wv[...], NT)
    term[:, QL + KL :] = rot_sum
    rows = xq.shape[0] // n_head
    chip, core = place[0], place[1]
    for k in range(n_head // 2):
        mine = 2 * jnp.bitwise_xor(chip, k) + core
        other = 2 * jnp.bitwise_xor(chip, k) + 1 - core
        here = slice(k * rows, (k + 1) * rows)
        keep[here, :] = term[pl.ds(pl.multiple_of(mine * rows, rows), rows), :LATENT]
        send[here, :] = term[pl.ds(pl.multiple_of(other * rows, rows), rows), :LATENT]
    raw_grads(xq, xkv, gq, gk, gv, (sq, sk, sv), None, None)


def far_kernel(n_seq, last, place, *refs):
    packed, refs = refs[: 4 * n_seq], refs[4 * n_seq :]
    wq, wk, wv, table, pq, pk, pv, sq, sk, sv, *refs = refs
    squares = refs[0] if last else None
    xq, xkv, grad, gq, gk, gv = refs[-6:]
    quarter = packed[0].shape[0]
    length = 4 * quarter
    core = place[1]
    for s in range(n_seq):
        for part in range(2):
            mine, other = packed[4 * s + part], packed[4 * s + 2 + part]
            for source, half in ((mine, core), (other, 1 - core)):
                start = pl.multiple_of(half * 2 * quarter + part * quarter, quarter)
                rows = pl.ds(s * length + start, quarter)
                xq[rows, :] = source[:, :QL]
                xkv[rows, :] = source[:, QL + 2 * grad.shape[1] :]
            for half in range(2):
                start = s * length + half * 2 * quarter + part * quarter
                columns = slice(QL + half * grad.shape[1], QL + (half + 1) * grad.shape[1])
                grad[start : start + quarter, :] = mine[:, columns]
        rows = pl.ds(s * length, length)
        views = [ref.at[rows] for ref in (xq, xkv, grad)]
        outs = [ref.at[rows] for ref in (gq, gk, gv)]
        backward(*views, wq, wk, wv, table, *outs)
    raw_grads(xq, xkv, gq, gk, gv, (sq, sk, sv), (pq, pk, pv), squares)


def scale_kernel(n_head, limit, *refs):
    parts, (sq, sk, sv, oq, ok, ov) = refs[:n_head], refs[n_head:]
    total = parts[0][...]
    for part in parts[1:]:
        total = total + part[...]
    total = jnp.sum(total, keepdims=True)
    factor = jnp.minimum(1.0, limit / jnp.sqrt(total + eps))
    for source, out in ((sq, oq), (sk, ok), (sv, ov)):
        out[...] = (source[...] * factor).astype(jnp.bfloat16)


def vmem(count):
    return [pl.BlockSpec(memory_space=pltpu.VMEM)] * count


def params():
    return pltpu.CompilerParams(vmem_limit_bytes=VMEM_LIMIT)


def cost(flops, moved):
    return pl.CostEstimate(flops=int(flops), bytes_accessed=int(moved), transcendentals=0)


def struct(shape, dtype):
    return jax.ShapeDtypeStruct(shape, dtype)


def exchange(value, axis, size, k):
    return lax.ppermute(value, axis, [(i, i ^ k) for i in range(size)])


def per_device(n_dp, n_head, query_latent, kv_latent, out_grad, query_up, key_up, value_up):
    length = query_latent.shape[0]
    quarter = length // 4
    wide_q, wide_k = query_up.shape[1], key_up.shape[1]
    index = lax.axis_index("head")
    chip, core = index // 2, index % 2
    place = jnp.stack([chip, core]).astype(jnp.int32)
    table = jnp.asarray(rotary_tables(length))
    weights = (query_up, key_up, value_up)

    half_q = lax.dynamic_slice_in_dim(query_latent, core * 2 * quarter, 2 * quarter, 0)
    half_kv = lax.dynamic_slice_in_dim(kv_latent, core * 2 * quarter, 2 * quarter, 0)
    packed = jnp.concatenate(
        [half_q, out_grad[: 2 * quarter], out_grad[2 * quarter :], half_kv], axis=1
    )
    received = {0: (packed[:quarter], packed[quarter:])}
    for k in range(1, n_dp):
        first, final = k & -k, 1 << (k.bit_length() - 1)
        received[k] = (
            exchange(received[k ^ first][0], "dp", n_dp, first),
            exchange(received[k ^ final][1], "dp", n_dp, final),
        )
    swapped = {
        k: tuple(exchange(part, "head", n_head, 1) for part in received[k]) for k in range(1, n_dp)
    }

    sums_shape = (
        struct((QL, wide_q), jnp.float32),
        struct((KL, wide_k), jnp.float32),
        struct((KL, wide_k), jnp.float32),
    )
    work = 2 * length * (QL * wide_q + 2 * KL * wide_k)

    def scratch(rows):
        return [
            pltpu.VMEM((rows, wide_q), jnp.bfloat16),
            pltpu.VMEM((rows, wide_k), jnp.bfloat16),
            pltpu.VMEM((rows, wide_k), jnp.bfloat16),
        ]

    halves = struct((length // 2, LATENT), jnp.float32)
    *sums, keep, send = pl.pallas_call(
        functools.partial(own_kernel, n_head),
        out_shape=(*sums_shape, halves, halves),
        in_specs=[pl.BlockSpec(memory_space=pltpu.SMEM)] + vmem(7),
        out_specs=vmem(5),
        scratch_shapes=scratch(length) + [pltpu.VMEM((length, QL + KL + TILE), jnp.float32)],
        compiler_params=params(),
        cost_estimate=cost(5 * work, 2**24),
        name="own",
    )(place, query_latent, kv_latent, out_grad, *weights, table)

    both = keep + exchange(send, "head", n_head, 1)
    rows = length // n_head
    latent_rows = both[:rows]
    for k in range(1, n_head // 2):
        block = both[k * rows : (k + 1) * rows].astype(jnp.bfloat16)
        latent_rows = latent_rows + exchange(block, "head", n_head, 2 * k).astype(jnp.float32)

    groups = [(1, 2)] + [(k,) for k in range(3, n_dp)]
    for group in groups:
        last = group is groups[-1]
        n_seq = len(group)
        blocks = [part for k in group for part in (*received[k], *swapped[k])]
        outs = sums_shape + ((struct((8, TILE), jnp.float32),) if last else ())
        sums = pl.pallas_call(
            functools.partial(far_kernel, n_seq, last),
            out_shape=outs,
            in_specs=[pl.BlockSpec(memory_space=pltpu.SMEM)] + vmem(len(blocks) + 7),
            out_specs=vmem(len(outs)),
            scratch_shapes=[
                pltpu.VMEM((n_seq * length, QL), jnp.bfloat16),
                pltpu.VMEM((n_seq * length, KL + DR), jnp.bfloat16),
                pltpu.VMEM((n_seq * length, wide_k), jnp.bfloat16),
            ]
            + scratch(n_seq * length),
            compiler_params=params(),
            cost_estimate=cost(4 * n_seq * work, 2**24),
            name="last" if last else "far",
        )(place, *blocks, *weights, table, *sums)
    *sums, squares = sums

    count = (QL * wide_q + 2 * KL * wide_k) * n_head
    limit = max_rms * count**0.5
    parts = [squares] + [exchange(squares, "head", n_head, k) for k in range(1, n_head)]
    scaled = pl.pallas_call(
        functools.partial(scale_kernel, n_head, limit),
        out_shape=tuple(struct(s.shape, jnp.bfloat16) for s in sums_shape),
        in_specs=vmem(n_head + 3),
        out_specs=vmem(3),
        compiler_params=params(),
        cost_estimate=cost(0, 2**23),
        name="scale",
    )(*parts, *sums)
    return (latent_rows[:, :QL], latent_rows[:, QL:], *scaled)


def solution(mesh):
    placed = (
        P("dp", None),
        P("dp", None),
        P("dp", "head"),
        P(None, "head"),
        P(None, "head"),
        P(None, "head"),
    )
    return jax.shard_map(
        functools.partial(per_device, mesh.shape["dp"], mesh.shape["head"]),
        mesh=mesh,
        in_specs=placed,
        out_specs=(
            P(("dp", "head"), None),
            P(("dp", "head"), None),
            P(None, "head"),
            P(None, "head"),
            P(None, "head"),
        ),
        check_vma=False,
    )
```

```python
import functools

import jax
import jax.numpy as jnp
import numpy as np
from jax import lax
from jax.experimental import pallas as pl
from jax.experimental.pallas import tpu as pltpu
from jax.sharding import PartitionSpec as P

QL = 1536
KL = 512
DN = 128
DR = 64
TILE = 128
WIDTH = DN + DR
PAIR = 2 * WIDTH
LATENT = QL + KL + DR

max_rms = 1.0
eps = 1e-06
VMEM_LIMIT = 32 * 2**20

NT = (((1,), (1,)), ((), ()))
TN = (((0,), (0,)), ((), ()))


def dot(left, right, dims=(((1,), (0,)), ((), ()))):
    return lax.dot_general(left, right, dims, preferred_element_type=jnp.float32)


def rotary_tables(length):
    half = DR // 2
    freqs = np.float32(10000.0) ** (
        np.float32(-2.0) * np.arange(half, dtype=np.float32) / np.float32(DR)
    )
    angle = np.arange(length, dtype=np.float32)[:, None] * freqs.astype(np.float32)[None, :]
    cosine, sine = np.cos(angle), np.sin(angle)
    ones, zeros = np.ones((length, DR), np.float32), np.zeros((length, DR), np.float32)
    rot_cos = np.concatenate([cosine, cosine], axis=1)
    rot_sin = np.concatenate([-sine, sine], axis=1)
    return np.concatenate([rot_cos, ones, ones, rot_cos, rot_sin, zeros, zeros, rot_sin], axis=1)


def swap_halves(tile):
    lane = lax.broadcasted_iota(jnp.int32, tile.shape, 1)
    first = lane % DR < DR // 2
    return jnp.where(
        first, pltpu.roll(tile, TILE - DR // 2, 1), pltpu.roll(tile, DR // 2, 1)
    )


def rounded(values):
    return values.astype(jnp.bfloat16).astype(jnp.float32)


def backward(xq, xkv, grad, wq, wk, wv, table, gq, gk, gv):
    length = xq.shape[0]
    heads = wk.shape[1] // DN
    scale = 1.0 / (DN + DR) ** 0.5
    low = lax.broadcasted_iota(jnp.int32, (length, TILE), 1) < DR
    token = lax.broadcasted_iota(jnp.int32, (length, length), 0)
    query = lax.broadcasted_iota(jnp.int32, (length, length), 1)
    allowed = token <= query
    cos_tiles = [table[:, 0:TILE], table[:, TILE : 2 * TILE]]
    sin_tiles = [table[:, 2 * TILE : 3 * TILE], table[:, 3 * TILE : 4 * TILE]]
    latent = xkv[:, :KL]
    rot = jnp.concatenate(
        [xkv[:, KL : KL + DR].astype(jnp.float32), jnp.zeros((length, DR), jnp.float32)], axis=1
    )
    rot_high = pltpu.roll(rot, DR, 1)
    rot_sum = jnp.zeros((length, TILE), jnp.float32)
    for pair in range(heads // 2):
        queries = rounded(dot(xq[...], wq[:, PAIR * pair : PAIR * (pair + 1)]))
        tiles = [queries[:, :TILE]]
        for i in range(2):
            part = queries[:, (i + 1) * TILE : (i + 2) * TILE]
            tiles.append(part * cos_tiles[i] + swap_halves(part) * sin_tiles[i])
        tiles = [tile.astype(jnp.bfloat16) for tile in tiles]
        columns = slice(2 * DN * pair, 2 * DN * (pair + 1))
        keys = dot(latent, wk[:, columns])
        values = dot(latent, wv[:, columns]).astype(jnp.bfloat16)
        odd = pltpu.roll(keys[:, DN:], DR, 1)
        key_windows = (
            jnp.concatenate([keys[:, :DN], rot], axis=1).astype(jnp.bfloat16),
            jnp.concatenate([jnp.where(low, 0.0, odd), jnp.where(low, odd, rot_high)], axis=1).astype(
                jnp.bfloat16
            ),
        )
        query_parts = []
        for side in range(2):
            head = slice((2 * pair + side) * DN, (2 * pair + side + 1) * DN)
            query_window = jnp.concatenate(tiles[side : side + 2], axis=1)
            key_window = key_windows[side]
            scores = dot(key_window, query_window, NT) * scale
            scores = jnp.where(allowed, scores, -jnp.inf)
            weights = jnp.exp(scores - jnp.max(scores, axis=0, keepdims=True))
            probs = weights * (1.0 / jnp.sum(weights, axis=0, keepdims=True))
            grad_head = grad[:, head]
            grad_probs = rounded(dot(values[:, DN * side : DN * (side + 1)], grad_head, NT))
            mean = jnp.sum(grad_probs * probs, axis=0, keepdims=True)
            grad_scores = (probs * (grad_probs - mean) * scale).astype(jnp.bfloat16)
            gv[:, head] = dot(probs.astype(jnp.bfloat16), grad_head).astype(jnp.bfloat16)
            key_part = dot(grad_scores, query_window)
            query_parts.append(dot(grad_scores, key_window, TN))
            if side == 0:
                gk[:, head] = key_part[:, :TILE].astype(jnp.bfloat16)
                rot_sum = rot_sum + rounded(key_part[:, TILE:])
            else:
                turned = pltpu.roll(key_part[:, TILE:], DR, 1)
                gk[:, head] = jnp.where(low, pltpu.roll(key_part[:, :TILE], DR, 1), turned).astype(
                    jnp.bfloat16
                )
                rot_sum = rot_sum + rounded(turned)
        even, uneven = query_parts
        parts = [even[:, :TILE], even[:, TILE:] + uneven[:, :TILE], uneven[:, TILE:]]
        for i in range(2):
            part = rounded(parts[i + 1])
            parts[i + 1] = part * cos_tiles[i] - swap_halves(part) * sin_tiles[i]
        for i in range(3):
            start = PAIR * pair + i * TILE
            gq[:, start : start + TILE] = parts[i].astype(jnp.bfloat16)
    return rot_sum


def raw_grads(xq, xkv, gq, gk, gv, sums, previous, squares):
    total = jnp.zeros((8, TILE), jnp.float32)
    blocks = [(xq, gq, i) for i in range(QL // 512)] + [(xkv, gk, 0), (xkv, gv, 0)]
    for index, (left, right, i) in enumerate(blocks):
        which = max(index - QL // 512 + 1, 0)
        rows = slice(i * 512, (i + 1) * 512)
        product = dot(left[:, rows], right[...], TN)
        if previous is not None:
            product = product + previous[which][rows, :]
        sums[which][rows, :] = product
        if squares is not None:
            square = product * product
            square = jnp.sum(square.reshape(512 // 8, 8, square.shape[1]), axis=0)
            for column in range(0, square.shape[1], TILE):
                total = total + square[:, column : column + TILE]
    if squares is not None:
        squares[...] = total


def load_kernel(place, xq, kvt, grad, xq_out, kv_out, grad_out, packed, sem):
    half = packed.shape[0]
    copies = [
        pltpu.make_async_copy(xq, xq_out, sem.at[0]),
        pltpu.make_async_copy(grad, grad_out, sem.at[1]),
    ]
    for copy in copies:
        copy.start()
    for start in range(0, KL + DR, TILE):
        stop = min(start + TILE, KL + DR)
        kv_out[:, start:stop] = kvt[start:stop, :].T
    for copy in copies:
        copy.wait()
    rows = pl.ds(pl.multiple_of(place[1] * half, half), half)
    wide = grad.shape[1]
    packed[:, :QL] = xq_out[rows, :]
    packed[:, QL : QL + wide] = grad_out[:half, :]
    packed[:, QL + wide : QL + 2 * wide] = grad_out[half:, :]
    packed[:, QL + 2 * wide :] = kv_out[rows, :]


def own_kernel(n_head, place, xq, xkv, grad, wq_in, wk_in, wv_in, table, *refs):
    wq, wk, wv, sq, sk, sv, keep, send, gq, gk, gv, term, sem = refs
    copies = [
        pltpu.make_async_copy(source, target, sem.at[i])
        for i, (source, target) in enumerate(((wq_in, wq), (wk_in, wk), (wv_in, wv)))
    ]
    for copy in copies:
        copy.start()
    for copy in copies:
        copy.wait()
    rot_sum = backward(xq, xkv, grad, wq, wk, wv, table, gq, gk, gv)
    term[:, :QL] = dot(gq[...], wq[...], NT)
    term[:, QL : QL + KL] = dot(gk[...], wk[...], NT) + dot(gv[...], wv[...], NT)
    term[:, QL + KL :] = rot_sum
    rows = xq.shape[0] // n_head
    chip, core = place[0], place[1]
    for k in range(n_head // 2):
        mine = 2 * jnp.bitwise_xor(chip, k) + core
        other = 2 * jnp.bitwise_xor(chip, k) + 1 - core
        here = slice(k * rows, (k + 1) * rows)
        keep[here, :] = term[pl.ds(pl.multiple_of(mine * rows, rows), rows), :]
        send[here, :] = term[pl.ds(pl.multiple_of(other * rows, rows), rows), :]
    raw_grads(xq, xkv, gq, gk, gv, (sq, sk, sv), None, None)


def pair_kernel(keep, received, local, *blocks):
    rows = local.shape[0]
    local[...] = keep[:rows, :] + received[:rows, :]
    for k, block in enumerate(blocks):
        here = slice((k + 1) * rows, (k + 2) * rows)
        block[...] = (keep[here, :] + received[here, :]).astype(jnp.bfloat16)


def far_kernel(n_terms, place, mine, other, wq, wk, wv, table, pq, pk, pv, *refs):
    last = n_terms > 0
    terms, refs = refs[:n_terms], refs[n_terms:]
    sq, sk, sv, *refs = refs
    squares = None
    if last:
        squares, latent_q, latent_kv, *refs = refs
        total = terms[0][...]
        for part in terms[1:]:
            total = total + part[...].astype(jnp.float32)
        latent_q[...] = total[:, :QL]
        latent_kv[...] = total[:, QL:LATENT]
    xq, xkv, grad, gq, gk, gv = refs
    half, wide = mine.shape[0], grad.shape[1]
    core = place[1]
    for source, side in ((mine, core), (other, 1 - core)):
        rows = pl.ds(pl.multiple_of(side * half, half), half)
        xq[rows, :] = source[:, :QL]
        xkv[rows, :] = source[:, QL + 2 * wide :]
    grad[:half, :] = mine[:, QL : QL + wide]
    grad[half:, :] = mine[:, QL + wide : QL + 2 * wide]
    backward(xq, xkv, grad, wq, wk, wv, table, gq, gk, gv)
    raw_grads(xq, xkv, gq, gk, gv, (sq, sk, sv), (pq, pk, pv), squares)


def scale_kernel(limit, left, right, sq, sk, sv, oq, ok, ov, bq, bk, bv, sem):
    total = jnp.sum(left[...] + right[...], keepdims=True)
    factor = jnp.minimum(1.0, limit / jnp.sqrt(total + eps))
    copies = []
    for source, buffer, out in ((sq, bq, oq), (sk, bk, ok), (sv, bv, ov)):
        for start in range(0, source.shape[0], 256):
            rows = slice(start, start + 256)
            buffer[rows, :] = (source[rows, :] * factor).astype(jnp.bfloat16)
            copy = pltpu.make_async_copy(buffer.at[rows], out.at[rows], sem.at[len(copies)])
            copy.start()
            copies.append(copy)
    for copy in copies:
        copy.wait()


def vmem(count):
    return [pl.BlockSpec(memory_space=pltpu.VMEM)] * count


def anywhere(count):
    return [pl.BlockSpec(memory_space=pl.ANY)] * count


def params():
    return pltpu.CompilerParams(vmem_limit_bytes=VMEM_LIMIT)


def cost(flops, moved):
    return pl.CostEstimate(flops=int(flops), bytes_accessed=int(moved), transcendentals=0)


def struct(shape, dtype):
    return jax.ShapeDtypeStruct(shape, dtype)


def exchange(value, axis, size, k):
    return lax.ppermute(value, axis, [(i, i ^ k) for i in range(size)])


def relay(low, high, core, n_dp, n_head, k):
    first, final = k & -k, 1 << (k.bit_length() - 1)
    value = jnp.where(core == 0, low, high)
    pairs = []
    for d in range(n_dp):
        for h in range(n_head):
            pairs.append((d * n_head + h, (d ^ (final if h % 2 else first)) * n_head + h))
    return lax.ppermute(value, ("dp", "head"), pairs)


def per_device(n_dp, n_head, query_latent, kv_latent, out_grad, query_up, key_up, value_up):
    length = query_latent.shape[0]
    half = length // 2
    wide_q, wide_k = query_up.shape[1], key_up.shape[1]
    index = lax.axis_index("head")
    chip, core = index // 2, index % 2
    place = jnp.stack([chip, core]).astype(jnp.int32)
    table = jnp.asarray(rotary_tables(length))
    smem = [pl.BlockSpec(memory_space=pltpu.SMEM)]
    work = 2 * length * (QL * wide_q + 2 * KL * wide_k)

    xq, xkv, grad, packed = pl.pallas_call(
        load_kernel,
        out_shape=(
            pltpu.VMEM((length, QL), jnp.bfloat16),
            pltpu.VMEM((length, KL + DR), jnp.bfloat16),
            pltpu.VMEM((length, wide_k), jnp.bfloat16),
            struct((half, LATENT + 2 * wide_k), jnp.bfloat16),
        ),
        in_specs=smem + anywhere(1) + vmem(1) + anywhere(1),
        out_specs=vmem(4),
        scratch_shapes=[pltpu.SemaphoreType.DMA((2,))],
        compiler_params=params(),
        cost_estimate=cost(0, 2**22),
        name="load",
    )(place, query_latent, kv_latent.T, out_grad)

    received = {k: exchange(packed, "dp", n_dp, k) for k in range(1, n_dp) if k & (k - 1) == 0}

    sums_shape = (
        pltpu.VMEM((QL, wide_q), jnp.float32),
        pltpu.VMEM((KL, wide_k), jnp.float32),
        pltpu.VMEM((KL, wide_k), jnp.float32),
    )
    grads_scratch = [
        pltpu.VMEM((length, wide_q), jnp.bfloat16),
        pltpu.VMEM((length, wide_k), jnp.bfloat16),
        pltpu.VMEM((length, wide_k), jnp.bfloat16),
    ]
    width = QL + KL + TILE
    halves = struct((half, width), jnp.float32)
    *outs, keep, send = pl.pallas_call(
        functools.partial(own_kernel, n_head),
        out_shape=(
            pltpu.VMEM((QL, wide_q), jnp.bfloat16),
            pltpu.VMEM((KL, wide_k), jnp.bfloat16),
            pltpu.VMEM((KL, wide_k), jnp.bfloat16),
            *sums_shape,
            halves,
            halves,
        ),
        in_specs=smem + vmem(3) + anywhere(3) + vmem(1),
        out_specs=vmem(8),
        scratch_shapes=grads_scratch
        + [pltpu.VMEM((length, width), jnp.float32), pltpu.SemaphoreType.DMA((3,))],
        compiler_params=params(),
        cost_estimate=cost(5 * work, 2**24),
        name="own",
    )(place, xq, xkv, grad, query_up, key_up, value_up, table)
    weights, sums = outs[:3], outs[3:]

    rows = length // n_head
    n_chip = n_head // 2
    local, *blocks = pl.pallas_call(
        pair_kernel,
        out_shape=(struct((rows, width), jnp.float32),)
        + (struct((rows, width), jnp.bfloat16),) * (n_chip - 1),
        in_specs=vmem(2),
        out_specs=vmem(n_chip),
        compiler_params=params(),
        cost_estimate=cost(0, 2**21),
        name="pair",
    )(keep, exchange(send, "head", n_head, 1))
    terms = [local] + [
        exchange(block, "head", n_head, 2 * (k + 1)) for k, block in enumerate(blocks)
    ]

    *values, keep = lax.optimization_barrier((*received.values(), keep))
    received = dict(zip(received, values))
    for k in range(3, n_dp):
        if k not in received:
            low, high = received[k ^ (k & -k)], received[k ^ (1 << (k.bit_length() - 1))]
            received[k] = relay(low, high, core, n_dp, n_head, k)

    for k in range(1, n_dp):
        last = k == n_dp - 1
        mine = received[k]
        other = exchange(mine, "head", n_head, 1)
        extra_out, extra_in = (), []
        if last:
            extra_in = terms
            extra_out = (
                struct((8, TILE), jnp.float32),
                struct((rows, QL), jnp.float32),
                struct((rows, KL + DR), jnp.float32),
            )
        sums = pl.pallas_call(
            functools.partial(far_kernel, len(extra_in)),
            out_shape=(*sums_shape, *extra_out),
            in_specs=smem + vmem(9 + len(extra_in)),
            out_specs=vmem(3 + len(extra_out)),
            scratch_shapes=[
                pltpu.VMEM((length, QL), jnp.bfloat16),
                pltpu.VMEM((length, KL + DR), jnp.bfloat16),
                pltpu.VMEM((length, wide_k), jnp.bfloat16),
            ]
            + grads_scratch,
            input_output_aliases={7: 0, 8: 1, 9: 2},
            compiler_params=params(),
            cost_estimate=cost(4 * work, 2**24),
            name="last" if last else "far",
        )(place, mine, other, *weights, table, *sums, *extra_in)
    *sums, squares, latent_q, latent_kv = sums

    count = (QL * wide_q + 2 * KL * wide_k) * n_head
    limit = max_rms * count**0.5
    bits = [1 << i for i in range(n_head.bit_length() - 1)]
    for bit in bits[:-1]:
        squares = squares + exchange(squares, "head", n_head, bit)
    scaled_shape = tuple(struct(w.shape, jnp.bfloat16) for w in weights)
    scaled = pl.pallas_call(
        functools.partial(scale_kernel, limit),
        out_shape=scaled_shape,
        in_specs=vmem(5),
        out_specs=anywhere(3),
        scratch_shapes=[pltpu.VMEM(w.shape, jnp.bfloat16) for w in weights]
        + [pltpu.SemaphoreType.DMA(((QL + 2 * KL) // 256,))],
        compiler_params=params(),
        cost_estimate=cost(0, 2**23),
        name="scale",
    )(squares, exchange(squares, "head", n_head, bits[-1]), *sums)
    return (latent_q, latent_kv, *scaled)


def solution(mesh):
    placed = (
        P("dp", None),
        P("dp", None),
        P("dp", "head"),
        P(None, "head"),
        P(None, "head"),
        P(None, "head"),
    )
    return jax.shard_map(
        functools.partial(per_device, mesh.shape["dp"], mesh.shape["head"]),
        mesh=mesh,
        in_specs=placed,
        out_specs=(
            P(("dp", "head"), None),
            P(("dp", "head"), None),
            P(None, "head"),
            P(None, "head"),
            P(None, "head"),
        ),
        check_vma=False,
    )
```

```python
import functools

import jax
import jax.numpy as jnp
import numpy as np
from jax import lax
from jax.experimental import pallas as pl
from jax.experimental.pallas import tpu as pltpu
from jax.sharding import PartitionSpec as P

QL = 1536
KL = 512
DN = 128
DR = 64
TILE = 128
WIDTH = DN + DR
PAIR = 2 * WIDTH
LATENT = QL + KL + DR

max_rms = 1.0
eps = 1e-06
VMEM_LIMIT = 32 * 2**20

NT = (((1,), (1,)), ((), ()))
TN = (((0,), (0,)), ((), ()))


def dot(left, right, dims=(((1,), (0,)), ((), ()))):
    return lax.dot_general(left, right, dims, preferred_element_type=jnp.float32)


def rotary_tables(length):
    half = DR // 2
    freqs = np.float32(10000.0) ** (
        np.float32(-2.0) * np.arange(half, dtype=np.float32) / np.float32(DR)
    )
    angle = np.arange(length, dtype=np.float32)[:, None] * freqs.astype(np.float32)[None, :]
    cosine, sine = np.cos(angle), np.sin(angle)
    ones, zeros = np.ones((length, DR), np.float32), np.zeros((length, DR), np.float32)
    rot_cos = np.concatenate([cosine, cosine], axis=1)
    rot_sin = np.concatenate([-sine, sine], axis=1)
    return np.concatenate([rot_cos, ones, ones, rot_cos, rot_sin, zeros, zeros, rot_sin], axis=1)


def swap_halves(tile):
    lane = lax.broadcasted_iota(jnp.int32, tile.shape, 1)
    first = lane % DR < DR // 2
    return jnp.where(
        first, pltpu.roll(tile, TILE - DR // 2, 1), pltpu.roll(tile, DR // 2, 1)
    )


def rounded(values):
    return values.astype(jnp.bfloat16).astype(jnp.float32)


def backward(xq, xkv, grad, wq, wk, wv, table, gq, gk, gv):
    length = xq.shape[0]
    heads = wk.shape[1] // DN
    scale = 1.0 / (DN + DR) ** 0.5
    low = lax.broadcasted_iota(jnp.int32, (length, TILE), 1) < DR
    token = lax.broadcasted_iota(jnp.int32, (length, length), 0)
    query = lax.broadcasted_iota(jnp.int32, (length, length), 1)
    allowed = token <= query
    cos_tiles = [table[:, 0:TILE], table[:, TILE : 2 * TILE]]
    sin_tiles = [table[:, 2 * TILE : 3 * TILE], table[:, 3 * TILE : 4 * TILE]]
    latent = xkv[:, :KL]
    rot = jnp.concatenate(
        [xkv[:, KL : KL + DR].astype(jnp.float32), jnp.zeros((length, DR), jnp.float32)], axis=1
    )
    rot_high = pltpu.roll(rot, DR, 1)
    rot_sum = jnp.zeros((length, TILE), jnp.float32)
    for pair in range(heads // 2):
        queries = rounded(dot(xq[...], wq[:, PAIR * pair : PAIR * (pair + 1)]))
        tiles = [queries[:, :TILE]]
        for i in range(2):
            part = queries[:, (i + 1) * TILE : (i + 2) * TILE]
            tiles.append(part * cos_tiles[i] + swap_halves(part) * sin_tiles[i])
        tiles = [tile.astype(jnp.bfloat16) for tile in tiles]
        columns = slice(2 * DN * pair, 2 * DN * (pair + 1))
        keys = dot(latent, wk[:, columns])
        values = dot(latent, wv[:, columns]).astype(jnp.bfloat16)
        odd = pltpu.roll(keys[:, DN:], DR, 1)
        key_windows = (
            jnp.concatenate([keys[:, :DN], rot], axis=1).astype(jnp.bfloat16),
            jnp.concatenate([jnp.where(low, 0.0, odd), jnp.where(low, odd, rot_high)], axis=1).astype(
                jnp.bfloat16
            ),
        )
        query_parts = []
        for side in range(2):
            head = slice((2 * pair + side) * DN, (2 * pair + side + 1) * DN)
            query_window = jnp.concatenate(tiles[side : side + 2], axis=1)
            key_window = key_windows[side]
            scores = dot(key_window, query_window, NT) * scale
            scores = jnp.where(allowed, scores, -jnp.inf)
            weights = jnp.exp(scores - jnp.max(scores, axis=0, keepdims=True))
            probs = weights * (1.0 / jnp.sum(weights, axis=0, keepdims=True))
            grad_head = grad[:, head]
            grad_probs = rounded(dot(values[:, DN * side : DN * (side + 1)], grad_head, NT))
            mean = jnp.sum(grad_probs * probs, axis=0, keepdims=True)
            grad_scores = (probs * (grad_probs - mean) * scale).astype(jnp.bfloat16)
            gv[:, head] = dot(probs.astype(jnp.bfloat16), grad_head).astype(jnp.bfloat16)
            key_part = dot(grad_scores, query_window)
            query_parts.append(dot(grad_scores, key_window, TN))
            if side == 0:
                gk[:, head] = key_part[:, :TILE].astype(jnp.bfloat16)
                rot_sum = rot_sum + rounded(key_part[:, TILE:])
            else:
                turned = pltpu.roll(key_part[:, TILE:], DR, 1)
                gk[:, head] = jnp.where(low, pltpu.roll(key_part[:, :TILE], DR, 1), turned).astype(
                    jnp.bfloat16
                )
                rot_sum = rot_sum + rounded(turned)
        even, uneven = query_parts
        parts = [even[:, :TILE], even[:, TILE:] + uneven[:, :TILE], uneven[:, TILE:]]
        for i in range(2):
            part = rounded(parts[i + 1])
            parts[i + 1] = part * cos_tiles[i] - swap_halves(part) * sin_tiles[i]
        for i in range(3):
            start = PAIR * pair + i * TILE
            gq[:, start : start + TILE] = parts[i].astype(jnp.bfloat16)
    return rot_sum


def raw_grads(xq, xkv, gq, gk, gv, sums, previous, squares):
    total = jnp.zeros((8, TILE), jnp.float32)
    blocks = [(xq, gq, i) for i in range(QL // 512)] + [(xkv, gk, 0), (xkv, gv, 0)]
    for index, (left, right, i) in enumerate(blocks):
        which = max(index - QL // 512 + 1, 0)
        rows = slice(i * 512, (i + 1) * 512)
        product = dot(left[:, rows], right[...], TN)
        if previous is not None:
            product = product + previous[which][rows, :]
        sums[which][rows, :] = product
        if squares is not None:
            square = product * product
            square = jnp.sum(square.reshape(512 // 8, 8, square.shape[1]), axis=0)
            for column in range(0, square.shape[1], TILE):
                total = total + square[:, column : column + TILE]
    if squares is not None:
        squares[...] = total


def load_kernel(place, xq, kvt, grad, xq_out, kv_out, grad_out, packed, sem):
    half = packed.shape[0]
    copies = [
        pltpu.make_async_copy(xq, xq_out, sem.at[0]),
        pltpu.make_async_copy(grad, grad_out, sem.at[1]),
    ]
    for copy in copies:
        copy.start()
    for start in range(0, KL + DR, TILE):
        stop = min(start + TILE, KL + DR)
        kv_out[:, start:stop] = kvt[start:stop, :].T
    for copy in copies:
        copy.wait()
    rows = pl.ds(pl.multiple_of(place[1] * half, half), half)
    wide = grad.shape[1]
    packed[:, :QL] = xq_out[rows, :]
    packed[:, QL : QL + wide] = grad_out[:half, :]
    packed[:, QL + wide : QL + 2 * wide] = grad_out[half:, :]
    packed[:, QL + 2 * wide : QL + 2 * wide + KL + DR] = kv_out[rows, :]
    packed[:, QL + 2 * wide + KL + DR :] = jnp.zeros((half, DR), jnp.bfloat16)


def own_kernel(n_head, place, xq, xkv, grad, wq_in, wk_in, wv_in, table, *refs):
    wq, wk, wv, sq, sk, sv, keep, send, gq, gk, gv, term, sem = refs
    copies = [
        pltpu.make_async_copy(source, target, sem.at[i])
        for i, (source, target) in enumerate(((wq_in, wq), (wk_in, wk), (wv_in, wv)))
    ]
    for copy in copies:
        copy.start()
    for copy in copies:
        copy.wait()
    rot_sum = backward(xq, xkv, grad, wq, wk, wv, table, gq, gk, gv)
    term[:, :QL] = dot(gq[...], wq[...], NT)
    term[:, QL : QL + KL] = dot(gk[...], wk[...], NT) + dot(gv[...], wv[...], NT)
    term[:, QL + KL :] = rot_sum
    rows = xq.shape[0] // n_head
    chip, core = place[0], place[1]
    for k in range(n_head // 2):
        mine = 2 * jnp.bitwise_xor(chip, k) + core
        other = 2 * jnp.bitwise_xor(chip, k) + 1 - core
        here = slice(k * rows, (k + 1) * rows)
        keep[here, :] = term[pl.ds(pl.multiple_of(mine * rows, rows), rows), :]
        send[here, :] = term[pl.ds(pl.multiple_of(other * rows, rows), rows), :]
    raw_grads(xq, xkv, gq, gk, gv, (sq, sk, sv), None, None)


def pair_kernel(keep, received, local, *blocks):
    rows = local.shape[0]
    local[...] = keep[:rows, :] + received[:rows, :]
    for k, block in enumerate(blocks):
        here = slice((k + 1) * rows, (k + 2) * rows)
        block[...] = (keep[here, :] + received[here, :]).astype(jnp.bfloat16)


def far_kernel(n_terms, place, mine, other, wq, wk, wv, table, pq, pk, pv, *refs):
    last = n_terms > 0
    terms, refs = refs[:n_terms], refs[n_terms:]
    sq, sk, sv, *refs = refs
    squares = None
    if last:
        squares, latent_q, latent_kv, *refs = refs
        total = terms[0][...]
        for part in terms[1:]:
            total = total + part[...].astype(jnp.float32)
        latent_q[...] = total[:, :QL]
        latent_kv[...] = total[:, QL:LATENT]
    xq, xkv, grad, gq, gk, gv = refs
    half, wide = mine.shape[0], grad.shape[1]
    core = place[1]
    for source, side in ((mine, core), (other, 1 - core)):
        rows = pl.ds(pl.multiple_of(side * half, half), half)
        xq[rows, :] = source[:, :QL]
        xkv[rows, :] = source[:, QL + 2 * wide : QL + 2 * wide + KL + DR]
    grad[:half, :] = mine[:, QL : QL + wide]
    grad[half:, :] = mine[:, QL + wide : QL + 2 * wide]
    backward(xq, xkv, grad, wq, wk, wv, table, gq, gk, gv)
    raw_grads(xq, xkv, gq, gk, gv, (sq, sk, sv), (pq, pk, pv), squares)


def scale_kernel(limit, left, right, sq, sk, sv, oq, ok, ov, bq, bk, bv, sem):
    total = jnp.sum(left[...] + right[...], keepdims=True)
    factor = jnp.minimum(1.0, limit / jnp.sqrt(total + eps))
    copies = []
    for source, buffer, out in ((sq, bq, oq), (sk, bk, ok), (sv, bv, ov)):
        for start in range(0, source.shape[0], 256):
            rows = slice(start, start + 256)
            buffer[rows, :] = (source[rows, :] * factor).astype(jnp.bfloat16)
            copy = pltpu.make_async_copy(buffer.at[rows], out.at[rows], sem.at[len(copies)])
            copy.start()
            copies.append(copy)
    for copy in copies:
        copy.wait()


def pick_kernel(place, low, high, out):
    @pl.when(place[1] == 0)
    def _():
        out[...] = low[...]

    @pl.when(place[1] != 0)
    def _():
        out[...] = high[...]


def add_kernel(left, right, out):
    out[...] = left[...] + right[...]


def vmem(count):
    return [pl.BlockSpec(memory_space=pltpu.VMEM)] * count


def hbm(count):
    return [pl.BlockSpec(memory_space=pltpu.HBM)] * count


def params():
    return pltpu.CompilerParams(vmem_limit_bytes=VMEM_LIMIT)


def cost(flops, moved):
    return pl.CostEstimate(flops=int(flops), bytes_accessed=int(moved), transcendentals=0)


def struct(shape, dtype):
    return jax.ShapeDtypeStruct(shape, dtype)


def exchange(value, axis, size, k):
    return lax.ppermute(value, axis, [(i, i ^ k) for i in range(size)])


def simple(kernel, like, *args, scalars=0):
    size = like.size * like.dtype.itemsize
    return pl.pallas_call(
        kernel,
        out_shape=struct(like.shape, like.dtype),
        in_specs=[pl.BlockSpec(memory_space=pltpu.SMEM)] * scalars + vmem(len(args) - scalars),
        out_specs=pl.BlockSpec(memory_space=pltpu.VMEM),
        compiler_params=pltpu.CompilerParams(vmem_limit_bytes=2**22 + 4 * size),
        cost_estimate=cost(0, 2 * size),
        name=kernel.__name__.split("_")[0],
    )(*args)


def far_away(value):
    return pltpu.with_memory_space_constraint(value, pltpu.HBM)


def relay(place, low, high, n_dp, n_head, k):
    first, final = k & -k, 1 << (k.bit_length() - 1)
    value = simple(pick_kernel, low, place, low, high, scalars=1)
    pairs = []
    for d in range(n_dp):
        for h in range(n_head):
            pairs.append((d * n_head + h, (d ^ (final if h % 2 else first)) * n_head + h))
    return lax.ppermute(value, ("dp", "head"), pairs)


def per_device(n_dp, n_head, query_latent, kv_latent, out_grad, query_up, key_up, value_up):
    length = query_latent.shape[0]
    half = length // 2
    wide_q, wide_k = query_up.shape[1], key_up.shape[1]
    index = lax.axis_index("head")
    chip, core = index // 2, index % 2
    place = jnp.stack([chip, core]).astype(jnp.int32)
    table = jnp.asarray(rotary_tables(length))
    smem = [pl.BlockSpec(memory_space=pltpu.SMEM)]
    work = 2 * length * (QL * wide_q + 2 * KL * wide_k)

    xq, xkv, grad, packed = pl.pallas_call(
        load_kernel,
        out_shape=(
            pltpu.VMEM((length, QL), jnp.bfloat16),
            pltpu.VMEM((length, KL + DR), jnp.bfloat16),
            pltpu.VMEM((length, wide_k), jnp.bfloat16),
            struct((half, QL + KL + TILE + 2 * wide_k), jnp.bfloat16),
        ),
        in_specs=smem + hbm(1) + vmem(1) + hbm(1),
        out_specs=vmem(4),
        scratch_shapes=[pltpu.SemaphoreType.DMA((2,))],
        compiler_params=params(),
        cost_estimate=cost(0, 2**22),
        name="load",
    )(place, far_away(query_latent), far_away(kv_latent.T), far_away(out_grad))

    received = {k: exchange(packed, "dp", n_dp, k) for k in range(1, n_dp) if k & (k - 1) == 0}

    sums_shape = (
        pltpu.VMEM((QL, wide_q), jnp.float32),
        pltpu.VMEM((KL, wide_k), jnp.float32),
        pltpu.VMEM((KL, wide_k), jnp.float32),
    )
    grads_scratch = [
        pltpu.VMEM((length, wide_q), jnp.bfloat16),
        pltpu.VMEM((length, wide_k), jnp.bfloat16),
        pltpu.VMEM((length, wide_k), jnp.bfloat16),
    ]
    width = QL + KL + TILE
    halves = struct((half, width), jnp.float32)
    *outs, keep, send = pl.pallas_call(
        functools.partial(own_kernel, n_head),
        out_shape=(
            pltpu.VMEM((QL, wide_q), jnp.bfloat16),
            pltpu.VMEM((KL, wide_k), jnp.bfloat16),
            pltpu.VMEM((KL, wide_k), jnp.bfloat16),
            *sums_shape,
            halves,
            halves,
        ),
        in_specs=smem + vmem(3) + hbm(3) + vmem(1),
        out_specs=vmem(8),
        scratch_shapes=grads_scratch
        + [pltpu.VMEM((length, width), jnp.float32), pltpu.SemaphoreType.DMA((3,))],
        compiler_params=params(),
        cost_estimate=cost(5 * work, 2**24),
        name="own",
    )(place, xq, xkv, grad, *[far_away(w) for w in (query_up, key_up, value_up)], table)
    weights, sums = outs[:3], outs[3:]

    rows = length // n_head
    n_chip = n_head // 2
    local, *blocks = pl.pallas_call(
        pair_kernel,
        out_shape=(struct((rows, width), jnp.float32),)
        + (struct((rows, width), jnp.bfloat16),) * (n_chip - 1),
        in_specs=vmem(2),
        out_specs=vmem(n_chip),
        compiler_params=params(),
        cost_estimate=cost(0, 2**21),
        name="pair",
    )(keep, exchange(send, "head", n_head, 1))
    terms = [local] + [
        exchange(block, "head", n_head, 2 * (k + 1)) for k, block in enumerate(blocks)
    ]

    *values, sums[2] = lax.optimization_barrier((*received.values(), sums[2]))
    received = dict(zip(received, values))
    for k in range(3, n_dp):
        if k not in received:
            low, high = received[k ^ (k & -k)], received[k ^ (1 << (k.bit_length() - 1))]
            received[k] = relay(place, low, high, n_dp, n_head, k)

    for k in range(1, n_dp):
        last = k == n_dp - 1
        if 1 < k < n_dp - 1:
            received[k], received[k + 1], sums[2] = lax.optimization_barrier(
                (received[k], received[k + 1], sums[2])
            )
        mine = received[k]
        other = exchange(mine, "head", n_head, 1)
        extra_out, extra_in = (), []
        if last:
            extra_in = terms
            extra_out = (
                struct((8, TILE), jnp.float32),
                struct((rows, QL), jnp.float32),
                struct((rows, KL + DR), jnp.float32),
            )
        sums = pl.pallas_call(
            functools.partial(far_kernel, len(extra_in)),
            out_shape=(*sums_shape, *extra_out),
            in_specs=smem + vmem(9 + len(extra_in)),
            out_specs=vmem(3 + len(extra_out)),
            scratch_shapes=[
                pltpu.VMEM((length, QL), jnp.bfloat16),
                pltpu.VMEM((length, KL + DR), jnp.bfloat16),
                pltpu.VMEM((length, wide_k), jnp.bfloat16),
            ]
            + grads_scratch,
            input_output_aliases={7: 0, 8: 1, 9: 2},
            compiler_params=params(),
            cost_estimate=cost(4 * work, 2**24),
            name="last" if last else "far",
        )(place, mine, other, *weights, table, *sums, *extra_in)
        sums = list(sums)
    *sums, squares, latent_q, latent_kv = sums

    count = (QL * wide_q + 2 * KL * wide_k) * n_head
    limit = max_rms * count**0.5
    bits = [1 << i for i in range(n_head.bit_length() - 1)]
    for bit in bits[:-1]:
        squares = simple(add_kernel, squares, squares, exchange(squares, "head", n_head, bit))
    scaled_shape = tuple(struct(w.shape, jnp.bfloat16) for w in weights)
    scaled = pl.pallas_call(
        functools.partial(scale_kernel, limit),
        out_shape=scaled_shape,
        in_specs=vmem(5),
        out_specs=hbm(3),
        scratch_shapes=[pltpu.VMEM(w.shape, jnp.bfloat16) for w in weights]
        + [pltpu.SemaphoreType.DMA(((QL + 2 * KL) // 256,))],
        compiler_params=params(),
        cost_estimate=cost(0, 2**23),
        name="scale",
    )(squares, exchange(squares, "head", n_head, bits[-1]), *sums)
    return (latent_q, latent_kv, *scaled)


def solution(mesh):
    placed = (
        P("dp", None),
        P("dp", None),
        P("dp", "head"),
        P(None, "head"),
        P(None, "head"),
        P(None, "head"),
    )
    return jax.shard_map(
        functools.partial(per_device, mesh.shape["dp"], mesh.shape["head"]),
        mesh=mesh,
        in_specs=placed,
        out_specs=(
            P(("dp", "head"), None),
            P(("dp", "head"), None),
            P(None, "head"),
            P(None, "head"),
            P(None, "head"),
        ),
        check_vma=False,
    )
```

```python
import functools

import jax
import jax.numpy as jnp
import numpy as np
from jax import lax
from jax.experimental import pallas as pl
from jax.experimental.pallas import tpu as pltpu
from jax.sharding import PartitionSpec as P

QL = 1536
KL = 512
DN = 128
DR = 64
TILE = 128
WIDTH = DN + DR
PAIR = 2 * WIDTH
LATENT = QL + KL + DR

max_rms = 1.0
eps = 1e-06
VMEM_LIMIT = 32 * 2**20

NT = (((1,), (1,)), ((), ()))
TN = (((0,), (0,)), ((), ()))


def dot(left, right, dims=(((1,), (0,)), ((), ()))):
    return lax.dot_general(left, right, dims, preferred_element_type=jnp.float32)


def rotary_tables(length):
    half = DR // 2
    freqs = np.float32(10000.0) ** (
        np.float32(-2.0) * np.arange(half, dtype=np.float32) / np.float32(DR)
    )
    angle = np.arange(length, dtype=np.float32)[:, None] * freqs.astype(np.float32)[None, :]
    cosine, sine = np.cos(angle), np.sin(angle)
    ones, zeros = np.ones((length, DR), np.float32), np.zeros((length, DR), np.float32)
    return np.concatenate([cosine, cosine, ones, -sine, sine, zeros], axis=1)


def swap_halves(tile):
    lane = lax.broadcasted_iota(jnp.int32, tile.shape, 1)
    first = lane % DR < DR // 2
    return jnp.where(
        first, pltpu.roll(tile, TILE - DR // 2, 1), pltpu.roll(tile, DR // 2, 1)
    )


def rounded(values):
    return values.astype(jnp.bfloat16).astype(jnp.float32)


def softmax_grads(scores, grad_probs):
    length = scores.shape[0]
    block = length // 2
    scale = 1.0 / (DN + DR) ** 0.5
    key = lax.broadcasted_iota(jnp.int32, (block, block), 0)
    query = lax.broadcasted_iota(jnp.int32, (block, block), 1)
    allowed = key <= query
    grad_probs = rounded(grad_probs)
    probs_columns, grads_columns = [], []
    for column in range(2):
        columns = slice(column * block, (column + 1) * block)
        parts = [scores[:block, columns], scores[block:, columns]][: column + 1]
        parts[-1] = jnp.where(allowed, parts[-1], -jnp.inf)
        tops = [jnp.max(part, axis=0, keepdims=True) for part in parts]
        top = tops[0] if column == 0 else jnp.maximum(*tops)
        parts = [jnp.exp((part - top) * scale) for part in parts]
        sums = [jnp.sum(part, axis=0, keepdims=True) for part in parts]
        inverse = 1.0 / (sums[0] if column == 0 else sums[0] + sums[1])
        parts = [part * inverse for part in parts]
        grads = [grad_probs[:block, columns], grad_probs[block:, columns]][: column + 1]
        means = [jnp.sum(g * p, axis=0, keepdims=True) for g, p in zip(grads, parts)]
        mean = means[0] if column == 0 else means[0] + means[1]
        grads = [(p * (g - mean) * scale).astype(jnp.bfloat16) for g, p in zip(grads, parts)]
        parts = [p.astype(jnp.bfloat16) for p in parts]
        if column == 0:
            parts.append(jnp.zeros((block, block), jnp.bfloat16))
            grads.append(jnp.zeros((block, block), jnp.bfloat16))
        probs_columns.append(jnp.concatenate(parts, axis=0))
        grads_columns.append(jnp.concatenate(grads, axis=0))
    return jnp.concatenate(probs_columns, axis=1), jnp.concatenate(grads_columns, axis=1)


def backward(length, xq, xkv, grad, weights, table, gq, gkv, qw, kw, vw, rot_out, ready):
    wq, wk, wv = weights
    n_seq = xq.shape[0] // length
    wide = wk.shape[1]
    heads = wide // DN
    low = lax.broadcasted_iota(jnp.int32, (length, TILE), 1) < DR
    cos_low, sin_low = table[:, :TILE], table[:, TILE:]
    cos_tiles = (cos_low, pltpu.roll(cos_low, DR, 1))
    sin_tiles = (sin_low, pltpu.roll(sin_low, DR, 1))
    spans = [slice(s * length, (s + 1) * length) for s in range(n_seq)]

    ready[0]()
    latent = xkv[:, :KL]
    for pair in range(heads // 2):
        columns = slice(2 * DN * pair, 2 * DN * (pair + 1))
        keys = dot(latent, wk[:, columns])
        vw[:, columns] = dot(latent, wv[:, columns]).astype(jnp.bfloat16)
        for span in spans:
            rot = jnp.concatenate(
                [xkv[span, KL : KL + DR].astype(jnp.float32), jnp.zeros((length, DR), jnp.float32)],
                axis=1,
            )
            odd = pltpu.roll(keys[span, DN:], DR, 1)
            tiles = (
                keys[span, :DN],
                rot,
                jnp.where(low, 0.0, odd),
                jnp.where(low, odd, pltpu.roll(rot, DR, 1)),
            )
            for i, tile in enumerate(tiles):
                start = (4 * pair + i) * TILE
                kw[span, start : start + TILE] = tile.astype(jnp.bfloat16)
    ready[1]()
    for pair in range(heads // 2):
        queries = dot(xq[...], wq[:, PAIR * pair : PAIR * (pair + 1)])
        for span in spans:
            for i in range(3):
                part = rounded(queries[span, i * TILE : (i + 1) * TILE])
                if i > 0:
                    part = part * cos_tiles[i - 1] + swap_halves(part) * sin_tiles[i - 1]
                start = PAIR * pair + i * TILE
                qw[span, start : start + TILE] = part.astype(jnp.bfloat16)

    items = [(span, head) for span in spans for head in range(heads)]

    def windows(span, head):
        start = PAIR * (head // 2) + TILE * (head % 2)
        return (
            qw[span, start : start + 2 * TILE],
            kw[span, 2 * TILE * head : 2 * TILE * (head + 1)],
            slice(head * DN, (head + 1) * DN),
        )

    def first_products(span, head):
        query_window, key_window, columns = windows(span, head)
        return (
            dot(key_window, query_window, NT),
            dot(vw[span, columns], grad[span, columns], NT),
        )

    rot_sums = [jnp.zeros((length, TILE), jnp.float32) for _ in spans]
    pending = first_products(*items[0])
    even_part = None
    for index, (span, head) in enumerate(items):
        products = pending
        if index + 1 < len(items):
            pending = first_products(*items[index + 1])
        probs, grad_scores = softmax_grads(*products)
        query_window, key_window, columns = windows(span, head)
        gkv[span, wide + head * DN : wide + (head + 1) * DN] = dot(probs, grad[span, columns]).astype(
            jnp.bfloat16
        )
        key_part = dot(grad_scores, query_window)
        query_part = dot(grad_scores, key_window, TN)
        seq = index // heads
        if head % 2 == 0:
            gkv[span, columns] = key_part[:, :TILE].astype(jnp.bfloat16)
            if rot_out is not None:
                rot_sums[seq] = rot_sums[seq] + rounded(key_part[:, TILE:])
            even_part = query_part
            continue
        turned = pltpu.roll(key_part[:, TILE:], DR, 1)
        gkv[span, columns] = jnp.where(low, pltpu.roll(key_part[:, :TILE], DR, 1), turned).astype(
            jnp.bfloat16
        )
        if rot_out is not None:
            rot_sums[seq] = rot_sums[seq] + rounded(turned)
        parts = [
            even_part[:, :TILE],
            even_part[:, TILE:] + query_part[:, :TILE],
            query_part[:, TILE:],
        ]
        for i in range(3):
            part = parts[i]
            if i > 0:
                part = rounded(part)
                part = part * cos_tiles[i - 1] - swap_halves(part) * sin_tiles[i - 1]
            start = PAIR * (head // 2) + i * TILE
            gq[span, start : start + TILE] = part.astype(jnp.bfloat16)
    if rot_out is not None:
        rot_out[...] = rot_sums[0]


def raw_grads(xq, xkv, gq, gkv, sums, previous, squares):
    wide = sums[1].shape[1]
    total = jnp.zeros((8, TILE), jnp.float32)
    step = KL
    for block in range(QL // step + 1):
        if block < QL // step:
            rows = slice(block * step, (block + 1) * step)
            targets = ((0, rows, dot(xq[:, rows], gq[...], TN)),)
        else:
            rows = slice(0, KL)
            product = dot(xkv[:, :KL], gkv[...], TN)
            targets = ((1, rows, product[:, :wide]), (2, rows, product[:, wide:]))
        for which, rows, product in targets:
            if previous is not None:
                product = product + previous[which][rows, :]
            sums[which][rows, :] = product
            if squares is None:
                continue
            folded = jnp.zeros((8, product.shape[1]), jnp.float32)
            for start in range(rows.start, rows.stop, 64):
                part = sums[which][start : start + 64, :]
                folded = folded + jnp.sum((part * part).reshape(8, 8, part.shape[1]), axis=0)
            for column in range(0, product.shape[1], TILE):
                total = total + folded[:, column : column + TILE]
    if squares is not None:
        for start in range(0, squares.shape[0], 8):
            squares[start : start + 8, :] = total


def load_kernel(place, xq, kvt, grad, packed, kv_rows, sem):
    half, wide = packed.shape[0], grad.shape[1]
    start = pl.multiple_of(place[1] * half, half)
    rows = pl.ds(start, half)
    pieces = (
        (kvt.at[:, rows], kv_rows),
        (xq.at[rows], packed.at[:, :QL]),
        (grad.at[:half], packed.at[:, QL : QL + wide]),
        (grad.at[half:], packed.at[:, QL + wide : QL + 2 * wide]),
    )
    copies = [pltpu.make_async_copy(*piece, sem.at[i]) for i, piece in enumerate(pieces)]
    for copy in copies:
        copy.start()
    copies[0].wait()
    for block in range(0, KL + DR, TILE):
        stop = min(block + TILE, KL + DR)
        first = QL + 2 * wide + block
        packed[:, first : first + stop - block] = kv_rows[block:stop, :].T
    packed[:, QL + 2 * wide + KL + DR :] = jnp.zeros((half, DR), jnp.bfloat16)
    for copy in copies[1:]:
        copy.wait()


def own_kernel(n_head, place, xq_in, kvt_in, grad_in, wq_in, wk_in, wv_in, table, *refs):
    wq, wk, wv, sq, sk, sv, keep, send_a, send_b, *refs = refs
    xq, kvt, xkv, grad, gq, gkv, qw, kw, vw, term, sem = refs
    pieces = (
        (kvt_in, kvt),
        (wk_in, wk),
        (wv_in, wv),
        (xq_in, xq),
        (wq_in, wq),
        (grad_in, grad),
    )
    copies = [pltpu.make_async_copy(*piece, sem.at[i]) for i, piece in enumerate(pieces)]
    for copy in copies:
        copy.start()

    def latents_ready():
        for copy in copies[:3]:
            copy.wait()
        for block in range(0, KL + DR, TILE):
            stop = min(block + TILE, KL + DR)
            xkv[:, block:stop] = kvt[block:stop, :].T

    def queries_ready():
        for copy in copies[3:]:
            copy.wait()

    length = xq.shape[0]
    rot = term.at[:, QL + KL :]
    ready = (latents_ready, queries_ready)
    backward(length, xq, xkv, grad, (wq, wk, wv), table, gq, gkv, qw, kw, vw, rot, ready)
    wide = wk.shape[1]
    term[:, :QL] = dot(gq[...], wq[...], NT)
    term[:, QL : QL + KL] = dot(gkv[:, :wide], wk[...], NT) + dot(gkv[:, wide:], wv[...], NT)
    rows = length // n_head
    chip, core = place[0], place[1]
    for k in range(n_head // 2):
        mine = 2 * jnp.bitwise_xor(chip, k) + core
        other = 2 * jnp.bitwise_xor(chip, k) + 1 - core
        here = slice(k * rows, (k + 1) * rows)
        keep[here, :] = term[pl.ds(pl.multiple_of(mine * rows, rows), rows), :]
        send, start = (send_a, k * rows), (send_b, k * rows - send_a.shape[0])
        send, start = send if k * rows < send_a.shape[0] else start
        send[start : start + rows, :] = term[pl.ds(pl.multiple_of(other * rows, rows), rows), :]
    raw_grads(xq, xkv, gq, gkv, (sq, sk, sv), None, None)


def pair_kernel(keep, first, second, local, *blocks):
    rows = local.shape[0]
    for k, block in enumerate((local, *blocks)):
        received, start = (first, k * rows) if k * rows < first.shape[0] else (second, k * rows - first.shape[0])
        total = keep[k * rows : (k + 1) * rows, :] + received[start : start + rows, :]
        block[...] = total.astype(block.dtype)


def far_kernel(n_seq, n_terms, place, *refs):
    packed, refs = refs[: 2 * n_seq], refs[2 * n_seq :]
    wq, wk, wv, table, pq, pk, pv, *refs = refs
    terms, refs = refs[:n_terms], refs[n_terms:]
    sq, sk, sv, *refs = refs
    squares = None
    if n_terms > 0:
        squares, latent_q, latent_kv, *refs = refs
        total = terms[0][...]
        for part in terms[1:]:
            total = total + part[...].astype(jnp.float32)
        latent_q[...] = total[:, :QL]
        latent_kv[...] = total[:, QL:LATENT]
    xq, xkv, grad, gq, gkv, qw, kw, vw = refs
    half, wide = packed[0].shape[0], grad.shape[1]
    length = 2 * half
    core = place[1]
    for s in range(n_seq):
        mine, other = packed[2 * s], packed[2 * s + 1]
        for source, side in ((mine, core), (other, 1 - core)):
            rows = pl.ds(pl.multiple_of(s * length + side * half, half), half)
            xq[rows, :] = source[:, :QL]
            xkv[rows, :] = source[:, QL + 2 * wide : QL + 2 * wide + KL + DR]
        start = s * length
        grad[start : start + half, :] = mine[:, QL : QL + wide]
        grad[start + half : start + length, :] = mine[:, QL + wide : QL + 2 * wide]
    ready = (lambda: None, lambda: None)
    backward(length, xq, xkv, grad, (wq, wk, wv), table, gq, gkv, qw, kw, vw, None, ready)
    raw_grads(xq, xkv, gq, gkv, (sq, sk, sv), (pq, pk, pv), squares)


def scale_kernel(limit, parts, sq, sk, sv, oq, ok, ov, bq, bk, bv, sem):
    total = jnp.sum(parts[...], keepdims=True)
    factor = jnp.minimum(1.0, limit / jnp.sqrt(total + eps))
    copies = []
    for source, buffer, out in ((sq, bq, oq), (sk, bk, ok), (sv, bv, ov)):
        for start in range(0, source.shape[0], 256):
            rows = slice(start, start + 256)
            buffer[rows, :] = (source[rows, :] * factor).astype(jnp.bfloat16)
            copy = pltpu.make_async_copy(buffer.at[rows], out.at[rows], sem.at[len(copies)])
            copy.start()
            copies.append(copy)
    for copy in copies:
        copy.wait()


def pick_kernel(place, low, high, out):
    @pl.when(place[1] == 0)
    def _():
        out[...] = low[...]

    @pl.when(place[1] != 0)
    def _():
        out[...] = high[...]


def vmem(count):
    return [pl.BlockSpec(memory_space=pltpu.VMEM)] * count


def hbm(count):
    return [pl.BlockSpec(memory_space=pltpu.HBM)] * count


def params():
    return pltpu.CompilerParams(vmem_limit_bytes=VMEM_LIMIT)


def cost(flops, moved):
    return pl.CostEstimate(flops=int(flops), bytes_accessed=int(moved), transcendentals=0)


def struct(shape, dtype):
    return jax.ShapeDtypeStruct(shape, dtype)


def exchange(value, axis, size, k):
    return lax.ppermute(value, axis, [(i, i ^ k) for i in range(size)])


def simple(kernel, like, *args, scalars=0):
    size = like.size * like.dtype.itemsize
    return pl.pallas_call(
        kernel,
        out_shape=struct(like.shape, like.dtype),
        in_specs=[pl.BlockSpec(memory_space=pltpu.SMEM)] * scalars + vmem(len(args) - scalars),
        out_specs=pl.BlockSpec(memory_space=pltpu.VMEM),
        compiler_params=pltpu.CompilerParams(vmem_limit_bytes=2**22 + 4 * size),
        cost_estimate=cost(0, 2 * size),
        name=kernel.__name__.split("_")[0],
    )(*args)


def far_away(value):
    return pltpu.with_memory_space_constraint(value, pltpu.HBM)


def relay(place, low, high, n_dp, n_head, k):
    first, final = k & -k, 1 << (k.bit_length() - 1)
    value = simple(pick_kernel, low, place, low, high, scalars=1)
    pairs = []
    for d in range(n_dp):
        for h in range(n_head):
            pairs.append((d * n_head + h, (d ^ (final if h % 2 else first)) * n_head + h))
    return lax.ppermute(value, ("dp", "head"), pairs)


def per_device(n_dp, n_head, query_latent, kv_latent, out_grad, query_up, key_up, value_up):
    length = query_latent.shape[0]
    half = length // 2
    wide_q, wide_k = query_up.shape[1], key_up.shape[1]
    heads = wide_k // DN
    index = lax.axis_index("head")
    chip, core = index // 2, index % 2
    place = jnp.stack([chip, core]).astype(jnp.int32)
    table = jnp.asarray(rotary_tables(length))
    smem = [pl.BlockSpec(memory_space=pltpu.SMEM)]
    work = 2 * length * (QL * wide_q + 2 * KL * wide_k)
    inputs = [far_away(value) for value in (query_latent, kv_latent.T, out_grad)]

    packed = pl.pallas_call(
        load_kernel,
        out_shape=pltpu.VMEM((half, QL + KL + TILE + 2 * wide_k), jnp.bfloat16),
        in_specs=smem + hbm(3),
        out_specs=pl.BlockSpec(memory_space=pltpu.VMEM),
        scratch_shapes=[pltpu.VMEM((KL + DR, half), jnp.bfloat16), pltpu.SemaphoreType.DMA((4,))],
        compiler_params=params(),
        cost_estimate=cost(0, 2**21),
        name="load",
    )(place, *inputs)

    received = {k: exchange(packed, "dp", n_dp, k) for k in range(1, n_dp) if k & (k - 1) == 0}

    sums_shape = (
        pltpu.VMEM((QL, wide_q), jnp.float32),
        pltpu.VMEM((KL, wide_k), jnp.float32),
        pltpu.VMEM((KL, wide_k), jnp.float32),
    )

    def scratch(rows):
        widths = (wide_q, 2 * wide_k, wide_q, 2 * TILE * heads, wide_k)
        return [pltpu.VMEM((rows, width), jnp.bfloat16) for width in widths]

    def rows_scratch(rows):
        return [pltpu.VMEM((rows, width), jnp.bfloat16) for width in (QL, KL + DR, wide_k)]

    width = QL + KL + TILE
    quarters = struct((half // 2, width), jnp.float32)
    *outs, keep, send_a, send_b = pl.pallas_call(
        functools.partial(own_kernel, n_head),
        out_shape=(
            pltpu.VMEM((QL, wide_q), jnp.bfloat16),
            pltpu.VMEM((KL, wide_k), jnp.bfloat16),
            pltpu.VMEM((KL, wide_k), jnp.bfloat16),
            *sums_shape,
            struct((half, width), jnp.float32),
            quarters,
            quarters,
        ),
        in_specs=smem + hbm(6) + vmem(1),
        out_specs=vmem(9),
        scratch_shapes=[
            pltpu.VMEM((length, QL), jnp.bfloat16),
            pltpu.VMEM((KL + DR, length), jnp.bfloat16),
            pltpu.VMEM((length, KL + DR), jnp.bfloat16),
            pltpu.VMEM((length, wide_k), jnp.bfloat16),
        ]
        + scratch(length)
        + [pltpu.VMEM((length, width), jnp.float32), pltpu.SemaphoreType.DMA((6,))],
        compiler_params=params(),
        cost_estimate=cost(5 * work, 2**24),
        name="own",
    )(place, *inputs, *[far_away(w) for w in (query_up, key_up, value_up)], table)
    weights, sums = outs[:3], outs[3:]

    rows = length // n_head
    n_chip = n_head // 2
    local, *blocks = pl.pallas_call(
        pair_kernel,
        out_shape=(struct((rows, width), jnp.float32),)
        + (struct((rows, width), jnp.bfloat16),) * (n_chip - 1),
        in_specs=vmem(3),
        out_specs=vmem(n_chip),
        compiler_params=params(),
        cost_estimate=cost(0, 2**21),
        name="pair",
    )(keep, exchange(send_a, "head", n_head, 1), exchange(send_b, "head", n_head, 1))
    terms = [local] + [
        exchange(block, "head", n_head, 2 * (k + 1)) for k, block in enumerate(blocks)
    ]

    *values, sums[2] = lax.optimization_barrier((*received.values(), sums[2]))
    *values, terms[0] = lax.optimization_barrier((*values, terms[0]))
    received = dict(zip(received, values))
    for k in range(3, n_dp):
        if k not in received:
            low, high = received[k ^ (k & -k)], received[k ^ (1 << (k.bit_length() - 1))]
            received[k] = relay(place, low, high, n_dp, n_head, k)

    groups = [(1, 2)] + [(k,) for k in range(3, n_dp)]
    for group in groups:
        last = group is groups[-1]
        n_seq = len(group)
        if len(group) == 1:
            received[group[0]], sums[2], *terms = lax.optimization_barrier(
                (received[group[0]], sums[2], *terms)
            )
        blocks = []
        for k in group:
            blocks += [received[k], exchange(received[k], "head", n_head, 1)]
        extra_out, extra_in = (), []
        if last:
            extra_in = terms
            extra_out = (
                struct((8 * n_head, TILE), jnp.float32),
                struct((rows, QL), jnp.float32),
                struct((rows, KL + DR), jnp.float32),
            )
        first = 1 + len(blocks) + 4
        sums = pl.pallas_call(
            functools.partial(far_kernel, n_seq, len(extra_in)),
            out_shape=(*sums_shape, *extra_out),
            in_specs=smem + vmem(len(blocks) + 7 + len(extra_in)),
            out_specs=vmem(3 + len(extra_out)),
            scratch_shapes=rows_scratch(n_seq * length) + scratch(n_seq * length),
            input_output_aliases={first: 0, first + 1: 1, first + 2: 2},
            compiler_params=params(),
            cost_estimate=cost(4 * n_seq * work, 2**24),
            name="last" if last else "far",
        )(place, *blocks, *weights, table, *sums, *extra_in)
        sums = list(sums)
    *sums, squares, latent_q, latent_kv = sums

    count = (QL * wide_q + 2 * KL * wide_k) * n_head
    limit = max_rms * count**0.5
    parts = lax.all_to_all(squares, "head", 0, 0, tiled=True)
    scaled_shape = tuple(struct(w.shape, jnp.bfloat16) for w in weights)
    scaled = pl.pallas_call(
        functools.partial(scale_kernel, limit),
        out_shape=scaled_shape,
        in_specs=vmem(4),
        out_specs=hbm(3),
        scratch_shapes=[pltpu.VMEM(w.shape, jnp.bfloat16) for w in weights]
        + [pltpu.SemaphoreType.DMA(((QL + 2 * KL) // 256,))],
        compiler_params=params(),
        cost_estimate=cost(0, 2**23),
        name="scale",
    )(parts, *sums)
    return (latent_q, latent_kv, *scaled)


def solution(mesh):
    placed = (
        P("dp", None),
        P("dp", None),
        P("dp", "head"),
        P(None, "head"),
        P(None, "head"),
        P(None, "head"),
    )
    return jax.shard_map(
        functools.partial(per_device, mesh.shape["dp"], mesh.shape["head"]),
        mesh=mesh,
        in_specs=placed,
        out_specs=(
            P(("dp", "head"), None),
            P(("dp", "head"), None),
            P(None, "head"),
            P(None, "head"),
            P(None, "head"),
        ),
        check_vma=False,
    )
```

```python
import functools

import jax
import jax.numpy as jnp
import numpy as np
from jax import lax
from jax.experimental import pallas as pl
from jax.experimental.pallas import tpu as pltpu
from jax.sharding import PartitionSpec as P

QL = 1536
KL = 512
DN = 128
DR = 64
TILE = 128
WIDTH = DN + DR
PAIR = 2 * WIDTH
LATENT = QL + KL + DR

max_rms = 1.0
eps = 1e-06
VMEM_LIMIT = 32 * 2**20

NT = (((1,), (1,)), ((), ()))
TN = (((0,), (0,)), ((), ()))


def dot(left, right, dims=(((1,), (0,)), ((), ()))):
    return lax.dot_general(left, right, dims, preferred_element_type=jnp.float32)


def rotary_tables(length):
    half = DR // 2
    freqs = np.float32(10000.0) ** (
        np.float32(-2.0) * np.arange(half, dtype=np.float32) / np.float32(DR)
    )
    angle = np.arange(length, dtype=np.float32)[:, None] * freqs.astype(np.float32)[None, :]
    cosine, sine = np.cos(angle), np.sin(angle)
    ones, zeros = np.ones((length, DR), np.float32), np.zeros((length, DR), np.float32)
    return np.concatenate([cosine, cosine, ones, -sine, sine, zeros], axis=1)


def swap_halves(tile):
    lane = lax.broadcasted_iota(jnp.int32, tile.shape, 1)
    first = lane % DR < DR // 2
    return jnp.where(
        first, pltpu.roll(tile, TILE - DR // 2, 1), pltpu.roll(tile, DR // 2, 1)
    )


def rounded(values):
    return values.astype(jnp.bfloat16).astype(jnp.float32)


def softmax_grads(scores, grad_probs):
    length = scores.shape[0]
    block = length // 2
    scale = 1.0 / (DN + DR) ** 0.5
    key = lax.broadcasted_iota(jnp.int32, (block, block), 0)
    query = lax.broadcasted_iota(jnp.int32, (block, block), 1)
    allowed = key <= query
    grad_probs = rounded(grad_probs)
    probs_columns, grads_columns = [], []
    for column in range(2):
        columns = slice(column * block, (column + 1) * block)
        parts = [scores[:block, columns], scores[block:, columns]][: column + 1]
        parts[-1] = jnp.where(allowed, parts[-1], -jnp.inf)
        tops = [jnp.max(part, axis=0, keepdims=True) for part in parts]
        top = tops[0] if column == 0 else jnp.maximum(*tops)
        parts = [jnp.exp((part - top) * scale) for part in parts]
        sums = [jnp.sum(part, axis=0, keepdims=True) for part in parts]
        inverse = 1.0 / (sums[0] if column == 0 else sums[0] + sums[1])
        parts = [part * inverse for part in parts]
        grads = [grad_probs[:block, columns], grad_probs[block:, columns]][: column + 1]
        means = [jnp.sum(g * p, axis=0, keepdims=True) for g, p in zip(grads, parts)]
        mean = means[0] if column == 0 else means[0] + means[1]
        grads = [(p * (g - mean) * scale).astype(jnp.bfloat16) for g, p in zip(grads, parts)]
        parts = [p.astype(jnp.bfloat16) for p in parts]
        if column == 0:
            parts.append(jnp.zeros((block, block), jnp.bfloat16))
            grads.append(jnp.zeros((block, block), jnp.bfloat16))
        probs_columns.append(jnp.concatenate(parts, axis=0))
        grads_columns.append(jnp.concatenate(grads, axis=0))
    return jnp.concatenate(probs_columns, axis=1), jnp.concatenate(grads_columns, axis=1)


def backward(length, xq, xkv, grad, weights, table, gq, gkv, qw, kw, vw, rot_out, ready):
    wq, wk, wv = weights
    n_seq = xq.shape[0] // length
    wide = wk.shape[1]
    heads = wide // DN
    low = lax.broadcasted_iota(jnp.int32, (length, TILE), 1) < DR
    cos_low, sin_low = table[:, :TILE], table[:, TILE:]
    cos_tiles = (cos_low, pltpu.roll(cos_low, DR, 1))
    sin_tiles = (sin_low, pltpu.roll(sin_low, DR, 1))
    spans = [slice(s * length, (s + 1) * length) for s in range(n_seq)]

    ready[0]()
    latent = xkv[:, :KL]
    for pair in range(heads // 2):
        columns = slice(2 * DN * pair, 2 * DN * (pair + 1))
        keys = dot(latent, wk[:, columns])
        vw[:, columns] = dot(latent, wv[:, columns]).astype(jnp.bfloat16)
        for span in spans:
            rot = jnp.concatenate(
                [xkv[span, KL : KL + DR].astype(jnp.float32), jnp.zeros((length, DR), jnp.float32)],
                axis=1,
            )
            odd = pltpu.roll(keys[span, DN:], DR, 1)
            tiles = (
                keys[span, :DN],
                rot,
                jnp.where(low, 0.0, odd),
                jnp.where(low, odd, pltpu.roll(rot, DR, 1)),
            )
            for i, tile in enumerate(tiles):
                start = (4 * pair + i) * TILE
                kw[span, start : start + TILE] = tile.astype(jnp.bfloat16)
    ready[1]()
    for pair in range(heads // 2):
        queries = dot(xq[...], wq[:, PAIR * pair : PAIR * (pair + 1)])
        for span in spans:
            for i in range(3):
                part = rounded(queries[span, i * TILE : (i + 1) * TILE])
                if i > 0:
                    part = part * cos_tiles[i - 1] + swap_halves(part) * sin_tiles[i - 1]
                start = PAIR * pair + i * TILE
                qw[span, start : start + TILE] = part.astype(jnp.bfloat16)

    items = [(span, head) for span in spans for head in range(heads)]

    def windows(span, head):
        start = PAIR * (head // 2) + TILE * (head % 2)
        return (
            qw[span, start : start + 2 * TILE],
            kw[span, 2 * TILE * head : 2 * TILE * (head + 1)],
            slice(head * DN, (head + 1) * DN),
        )

    def first_products(span, head):
        query_window, key_window, columns = windows(span, head)
        return (
            dot(key_window, query_window, NT),
            dot(vw[span, columns], grad[span, columns], NT),
        )

    rot_sums = [jnp.zeros((length, TILE), jnp.float32) for _ in spans]
    pending = first_products(*items[0])
    even_part = None
    for index, (span, head) in enumerate(items):
        products = pending
        if index + 1 < len(items):
            pending = first_products(*items[index + 1])
        probs, grad_scores = softmax_grads(*products)
        query_window, key_window, columns = windows(span, head)
        gkv[span, wide + head * DN : wide + (head + 1) * DN] = dot(probs, grad[span, columns]).astype(
            jnp.bfloat16
        )
        key_part = dot(grad_scores, query_window)
        query_part = dot(grad_scores, key_window, TN)
        seq = index // heads
        if head % 2 == 0:
            gkv[span, columns] = key_part[:, :TILE].astype(jnp.bfloat16)
            if rot_out is not None:
                rot_sums[seq] = rot_sums[seq] + rounded(key_part[:, TILE:])
            even_part = query_part
            continue
        turned = pltpu.roll(key_part[:, TILE:], DR, 1)
        gkv[span, columns] = jnp.where(low, pltpu.roll(key_part[:, :TILE], DR, 1), turned).astype(
            jnp.bfloat16
        )
        if rot_out is not None:
            rot_sums[seq] = rot_sums[seq] + rounded(turned)
        parts = [
            even_part[:, :TILE],
            even_part[:, TILE:] + query_part[:, :TILE],
            query_part[:, TILE:],
        ]
        for i in range(3):
            part = parts[i]
            if i > 0:
                part = rounded(part)
                part = part * cos_tiles[i - 1] - swap_halves(part) * sin_tiles[i - 1]
            start = PAIR * (head // 2) + i * TILE
            gq[span, start : start + TILE] = part.astype(jnp.bfloat16)
    if rot_out is not None:
        rot_out[...] = rot_sums[0]


def raw_grads(xq, xkv, gq, gkv, sums, previous, squares):
    wide = sums[1].shape[1]
    total = jnp.zeros((8, TILE), jnp.float32)
    step = KL
    for block in range(QL // step + 1):
        if block < QL // step:
            rows = slice(block * step, (block + 1) * step)
            targets = ((0, rows, dot(xq[:, rows], gq[...], TN)),)
        else:
            rows = slice(0, KL)
            product = dot(xkv[:, :KL], gkv[...], TN)
            targets = ((1, rows, product[:, :wide]), (2, rows, product[:, wide:]))
        for which, rows, product in targets:
            if previous is not None:
                product = product + previous[which][rows, :]
            sums[which][rows, :] = product
            if squares is None:
                continue
            folded = jnp.zeros((8, product.shape[1]), jnp.float32)
            for start in range(rows.start, rows.stop, 64):
                part = sums[which][start : start + 64, :]
                folded = folded + jnp.sum((part * part).reshape(8, 8, part.shape[1]), axis=0)
            for column in range(0, product.shape[1], TILE):
                total = total + folded[:, column : column + TILE]
    if squares is not None:
        for start in range(0, squares.shape[0], 8):
            squares[start : start + 8, :] = total


def load_kernel(place, xq, kvt, grad, packed, cotangent, kv_rows, sem):
    half = packed.shape[0]
    rows = pl.ds(pl.multiple_of(place[1] * half, half), half)
    pieces = ((kvt.at[:, rows], kv_rows), (xq.at[rows], packed.at[:, :QL]), (grad, cotangent))
    copies = [pltpu.make_async_copy(*piece, sem.at[i]) for i, piece in enumerate(pieces)]
    for copy in copies:
        copy.start()
    copies[0].wait()
    for block in range(0, KL + DR, TILE):
        stop = min(block + TILE, KL + DR)
        packed[:, QL + block : QL + stop] = kv_rows[block:stop, :].T
    packed[:, LATENT:] = jnp.zeros((half, TILE - DR), jnp.bfloat16)
    for copy in copies[1:]:
        copy.wait()


def own_kernel(n_head, place, xq_in, kvt_in, grad_in, wq_in, wk_in, wv_in, table, *refs):
    wq, wk, wv, xq, xkv, gq, gkv, keep, send_a, send_b, *refs = refs
    kvt, grad, qw, kw, vw, term, sem = refs
    pieces = (
        (kvt_in, kvt),
        (wk_in, wk),
        (wv_in, wv),
        (xq_in, xq),
        (wq_in, wq),
        (grad_in, grad),
    )
    copies = [pltpu.make_async_copy(*piece, sem.at[i]) for i, piece in enumerate(pieces)]
    for copy in copies:
        copy.start()

    def latents_ready():
        for copy in copies[:3]:
            copy.wait()
        for block in range(0, KL + DR, TILE):
            stop = min(block + TILE, KL + DR)
            xkv[:, block:stop] = kvt[block:stop, :].T

    def queries_ready():
        for copy in copies[3:]:
            copy.wait()

    length = xq.shape[0]
    rot = term.at[:, QL + KL :]
    ready = (latents_ready, queries_ready)
    backward(length, xq, xkv, grad, (wq, wk, wv), table, gq, gkv, qw, kw, vw, rot, ready)
    wide = wk.shape[1]
    term[:, :QL] = dot(gq[...], wq[...], NT)
    term[:, QL : QL + KL] = dot(gkv[:, :wide], wk[...], NT) + dot(gkv[:, wide:], wv[...], NT)
    rows = length // n_head
    chip, core = place[0], place[1]
    for k in range(n_head // 2):
        mask = turned_round(k, n_head // 2)
        mine = 2 * jnp.bitwise_xor(chip, mask) + core
        other = 2 * jnp.bitwise_xor(chip, mask) + 1 - core
        here = slice(k * rows, (k + 1) * rows)
        keep[here, :] = term[pl.ds(pl.multiple_of(mine * rows, rows), rows), :]
        send, start = (send_a, k * rows), (send_b, k * rows - send_a.shape[0])
        send, start = send if k * rows < send_a.shape[0] else start
        send[start : start + rows, :] = term[pl.ds(pl.multiple_of(other * rows, rows), rows), :]


def fold_kernel(n_received, keep, *refs):
    received, (stay, go) = refs[:n_received], refs[n_received:]
    start = 0
    for part in received:
        rows = slice(start, start + part.shape[0])
        total = keep[rows, :] + part[...].astype(jnp.float32)
        start = rows.stop
        if rows.stop <= stay.shape[0]:
            stay[rows, :] = total
        elif rows.start >= stay.shape[0]:
            go[rows.start - stay.shape[0] : rows.stop - stay.shape[0], :] = total.astype(go.dtype)
        else:
            stay[...] = total[: stay.shape[0], :]
            go[...] = total[stay.shape[0] :, :].astype(go.dtype)


def far_kernel(n_seq, place, *refs):
    blocks, refs = refs[: 3 * n_seq], refs[3 * n_seq :]
    wq, wk, wv, table, xq, xkv, gq, gkv, grad, qw, kw, vw = refs
    half = blocks[0].shape[0]
    length = 2 * half
    core = place[1]
    for s in range(n_seq):
        mine, other, cotangent = blocks[3 * s : 3 * s + 3]
        for source, side in ((mine, core), (other, 1 - core)):
            rows = pl.ds(pl.multiple_of(s * length + side * half, half), half)
            xq[rows, :] = source[:, :QL]
            xkv[rows, :] = source[:, QL:LATENT]
        grad[s * length : (s + 1) * length, :] = cotangent[...]
    ready = (lambda: None, lambda: None)
    backward(length, xq, xkv, grad, (wq, wk, wv), table, gq, gkv, qw, kw, vw, None, ready)


def sums_kernel(first, last, xq, xkv, gq, gkv, *refs):
    previous, refs = (None, refs) if first else (refs[:3], refs[3:])
    squares = None
    if last:
        local, received, *refs, squares, latent_q, latent_kv = refs
        total = local[...] + received[...].astype(jnp.float32)
        latent_q[...] = total[:, :QL]
        latent_kv[...] = total[:, QL:LATENT]
    raw_grads(xq, xkv, gq, gkv, refs, previous, squares)


def scale_kernel(limit, parts, sq, sk, sv, oq, ok, ov, bq, bk, bv, sem):
    total = jnp.sum(parts[...], keepdims=True)
    factor = jnp.minimum(1.0, limit / jnp.sqrt(total + eps))
    copies = []
    for source, buffer, out in ((sq, bq, oq), (sk, bk, ok), (sv, bv, ov)):
        for start in range(0, source.shape[0], 256):
            rows = slice(start, start + 256)
            buffer[rows, :] = (source[rows, :] * factor).astype(jnp.bfloat16)
            copy = pltpu.make_async_copy(buffer.at[rows], out.at[rows], sem.at[len(copies)])
            copy.start()
            copies.append(copy)
    for copy in copies:
        copy.wait()


def vmem(count):
    return [pl.BlockSpec(memory_space=pltpu.VMEM)] * count


def hbm(count):
    return [pl.BlockSpec(memory_space=pltpu.HBM)] * count


def params():
    return pltpu.CompilerParams(vmem_limit_bytes=VMEM_LIMIT)


def cost(flops, moved):
    return pl.CostEstimate(flops=int(flops), bytes_accessed=int(moved), transcendentals=0)


def struct(shape, dtype):
    return jax.ShapeDtypeStruct(shape, dtype)


def exchange(value, axis, size, k):
    return lax.ppermute(value, axis, [(i, i ^ k) for i in range(size)])


def far_away(value):
    return pltpu.with_memory_space_constraint(value, pltpu.HBM)


def turned_round(mask, n_dp):
    bits = n_dp.bit_length() - 1
    return sum(((mask >> i) & 1) << (bits - 1 - i) for i in range(bits))


def across(value, n_dp, n_head, mask):
    masks = (mask, turned_round(mask, n_dp))
    pairs = [
        (d * n_head + h, (d ^ masks[h % 2]) * n_head + h) for d in range(n_dp) for h in range(n_head)
    ]
    return lax.ppermute(value, ("dp", "head"), pairs)


def per_device(n_dp, n_head, query_latent, kv_latent, out_grad, query_up, key_up, value_up):
    length = query_latent.shape[0]
    half = length // 2
    wide_q, wide_k = query_up.shape[1], key_up.shape[1]
    heads = wide_k // DN
    index = lax.axis_index("head")
    place = jnp.stack([index // 2, index % 2]).astype(jnp.int32)
    table = jnp.asarray(rotary_tables(length))
    smem = [pl.BlockSpec(memory_space=pltpu.SMEM)]
    work = 2 * length * (QL * wide_q + 2 * KL * wide_k)
    inputs = [far_away(value) for value in (query_latent, kv_latent.T, out_grad)]
    width = QL + KL + TILE

    packed, cotangent = pl.pallas_call(
        load_kernel,
        out_shape=(
            pltpu.VMEM((half, width), jnp.bfloat16),
            pltpu.VMEM((length, wide_k), jnp.bfloat16),
        ),
        in_specs=smem + hbm(3),
        out_specs=vmem(2),
        scratch_shapes=[pltpu.VMEM((KL + DR, half), jnp.bfloat16), pltpu.SemaphoreType.DMA((3,))],
        compiler_params=params(),
        cost_estimate=cost(0, 0),
        name="load",
    )(place, *inputs)

    packed, place = lax.optimization_barrier((packed, place))
    singles = [1 << i for i in reversed(range(n_dp.bit_length() - 1))]
    cotangents = {k: across(cotangent, n_dp, n_head, k) for k in singles}
    latents = {k: across(packed, n_dp, n_head, k) for k in singles}

    def rows_shape(rows):
        widths = (QL, KL + DR, wide_q, 2 * wide_k)
        return tuple(pltpu.VMEM((rows, width), jnp.bfloat16) for width in widths)

    def scratch(rows):
        widths = (wide_k, wide_q, 2 * TILE * heads, wide_k)
        return [pltpu.VMEM((rows, width), jnp.bfloat16) for width in widths]

    weights_shape = tuple(
        pltpu.VMEM(shape, jnp.bfloat16) for shape in ((QL, wide_q), (KL, wide_k), (KL, wide_k))
    )
    sums_shape = tuple(pltpu.VMEM(w.shape, jnp.float32) for w in weights_shape)
    quarters = struct((half // 2, width), jnp.float32)
    *outs, keep, send_a, send_b = pl.pallas_call(
        functools.partial(own_kernel, n_head),
        out_shape=(
            *weights_shape,
            *rows_shape(length),
            struct((half, width), jnp.float32),
            quarters,
            quarters,
        ),
        in_specs=smem + hbm(6) + vmem(1),
        out_specs=vmem(10),
        scratch_shapes=[pltpu.VMEM((KL + DR, length), jnp.bfloat16)]
        + scratch(length)
        + [pltpu.VMEM((length, width), jnp.float32), pltpu.SemaphoreType.DMA((6,))],
        compiler_params=params(),
        cost_estimate=cost(0, 0),
        name="own",
    )(place, *inputs, *[far_away(w) for w in (query_up, key_up, value_up)], table)
    weights, found = outs[:3], outs[3:]

    rows = length // n_head

    def add_sums(found, sums, terms):
        extra_out = ()
        if terms:
            extra_out = (
                struct((8 * n_head, TILE), jnp.float32),
                struct((rows, QL), jnp.float32),
                struct((rows, KL + DR), jnp.float32),
            )
        return list(
            pl.pallas_call(
                functools.partial(sums_kernel, not sums, bool(terms)),
                out_shape=(*sums_shape, *extra_out),
                in_specs=vmem(4 + len(sums) + len(terms)),
                out_specs=vmem(3 + len(extra_out)),
                input_output_aliases={4: 0, 5: 1, 6: 2} if sums else {},
                compiler_params=params(),
                cost_estimate=cost(0, 0),
                name="sums_last" if terms else "sums",
            )(*found, *sums, *terms)
        )

    sums = add_sums(found, [], [])

    def fold(keep, *received):
        half_shape = (keep.shape[0] // 2, width)
        return pl.pallas_call(
            functools.partial(fold_kernel, len(received)),
            out_shape=(struct(half_shape, jnp.float32), struct(half_shape, jnp.bfloat16)),
            in_specs=vmem(1 + len(received)),
            out_specs=vmem(2),
            compiler_params=params(),
            cost_estimate=cost(0, 0),
            name="fold",
        )(keep, *received)

    stay, go = fold(keep, *[exchange(send, "head", n_head, 1) for send in (send_a, send_b)])
    bits = [2 << i for i in range(n_head.bit_length() - 2)]
    for bit in bits[:-2]:
        stay, go = fold(stay, exchange(go, "head", n_head, bit))
    came = exchange(go, "head", n_head, bits[-2])

    values = [latents[k] for k in singles] + [cotangents[k] for k in singles]
    *values, sums[2] = lax.optimization_barrier((*values, sums[2]))
    latents = dict(zip(singles, values))
    cotangents = dict(zip(singles, values[len(singles) :]))
    for k in range(3, n_dp):
        if k not in latents:
            latents[k] = across(latents[k & (k - 1)], n_dp, n_head, k & -k)
            cotangents[k] = across(cotangents[k & (k - 1)], n_dp, n_head, k & -k)
    def swapped(k):
        return exchange(latents[turned_round(k, n_dp)], "head", n_head, 1)

    groups = [(1, 2)] + [(k,) for k in range(3, n_dp)]
    for group in groups:
        n_seq = len(group)
        blocks = []
        for k in group:
            blocks += [latents[k], swapped(k), cotangents[k]]
        found = list(
            pl.pallas_call(
                functools.partial(far_kernel, n_seq),
                out_shape=rows_shape(n_seq * length),
                in_specs=smem + vmem(len(blocks) + 4),
                out_specs=vmem(4),
                scratch_shapes=scratch(n_seq * length),
                compiler_params=params(),
                cost_estimate=cost(0, 0),
                name="far",
            )(place, *blocks, *weights, table)
        )
        last = group is groups[-1]
        if not last:
            k = groups[groups.index(group) + 1][0]
            latents[k], found[3], came = lax.optimization_barrier((latents[k], found[3], came))
            if group is groups[0]:
                stay, go = fold(stay, came)
                terms = [stay, exchange(go, "head", n_head, bits[-1])]
        sums = add_sums(found, sums, terms if last else [])
    *sums, squares, latent_q, latent_kv = sums

    count = (QL * wide_q + 2 * KL * wide_k) * n_head
    limit = max_rms * count**0.5
    parts = lax.all_to_all(squares, "head", 0, 0, tiled=True)
    scaled = pl.pallas_call(
        functools.partial(scale_kernel, limit),
        out_shape=tuple(struct(w.shape, jnp.bfloat16) for w in weights),
        in_specs=vmem(4),
        out_specs=hbm(3),
        scratch_shapes=[pltpu.VMEM(w.shape, jnp.bfloat16) for w in weights]
        + [pltpu.SemaphoreType.DMA(((QL + 2 * KL) // 256,))],
        compiler_params=params(),
        cost_estimate=cost(0, 0),
        name="scale",
    )(parts, *sums)
    return (latent_q, latent_kv, *scaled)


def solution(mesh):
    placed = (
        P("dp", None),
        P("dp", None),
        P("dp", "head"),
        P(None, "head"),
        P(None, "head"),
        P(None, "head"),
    )
    return jax.shard_map(
        functools.partial(per_device, mesh.shape["dp"], mesh.shape["head"]),
        mesh=mesh,
        in_specs=placed,
        out_specs=(
            P(("dp", "head"), None),
            P(("dp", "head"), None),
            P(None, "head"),
            P(None, "head"),
            P(None, "head"),
        ),
        check_vma=False,
    )
```

```python
import functools

import jax
import jax.numpy as jnp
import numpy as np
from jax import lax
from jax.experimental import pallas as pl
from jax.experimental.pallas import tpu as pltpu
from jax.sharding import PartitionSpec as P

QL = 1536
KL = 512
DN = 128
DR = 64
TILE = 128
WIDTH = DN + DR
PAIR = 2 * WIDTH
LATENT = QL + KL + DR

max_rms = 1.0
eps = 1e-06
VMEM_LIMIT = 32 * 2**20

NT = (((1,), (1,)), ((), ()))
TN = (((0,), (0,)), ((), ()))


def dot(left, right, dims=(((1,), (0,)), ((), ()))):
    return lax.dot_general(left, right, dims, preferred_element_type=jnp.float32)


def rotary_tables(length):
    half = DR // 2
    freqs = np.float32(10000.0) ** (
        np.float32(-2.0) * np.arange(half, dtype=np.float32) / np.float32(DR)
    )
    angle = np.arange(length, dtype=np.float32)[:, None] * freqs.astype(np.float32)[None, :]
    cosine, sine = np.cos(angle), np.sin(angle)
    ones, zeros = np.ones((length, DR), np.float32), np.zeros((length, DR), np.float32)
    return np.concatenate([cosine, cosine, ones, -sine, sine, zeros], axis=1)


def swap_halves(tile):
    lane = lax.broadcasted_iota(jnp.int32, tile.shape, 1)
    first = lane % DR < DR // 2
    return jnp.where(
        first, pltpu.roll(tile, TILE - DR // 2, 1), pltpu.roll(tile, DR // 2, 1)
    )


def rounded(values):
    return values.astype(jnp.bfloat16).astype(jnp.float32)


def softmax_grads(scores, grad_probs):
    length = scores.shape[0]
    block = length // 2
    scale = 1.0 / (DN + DR) ** 0.5
    key = lax.broadcasted_iota(jnp.int32, (block, block), 0)
    query = lax.broadcasted_iota(jnp.int32, (block, block), 1)
    allowed = key <= query
    grad_probs = rounded(grad_probs)
    probs_columns, grads_columns = [], []
    for column in range(2):
        columns = slice(column * block, (column + 1) * block)
        parts = [scores[:block, columns], scores[block:, columns]][: column + 1]
        parts[-1] = jnp.where(allowed, parts[-1], -jnp.inf)
        tops = [jnp.max(part, axis=0, keepdims=True) for part in parts]
        top = tops[0] if column == 0 else jnp.maximum(*tops)
        parts = [jnp.exp((part - top) * scale) for part in parts]
        sums = [jnp.sum(part, axis=0, keepdims=True) for part in parts]
        inverse = 1.0 / (sums[0] if column == 0 else sums[0] + sums[1])
        parts = [part * inverse for part in parts]
        grads = [grad_probs[:block, columns], grad_probs[block:, columns]][: column + 1]
        means = [jnp.sum(g * p, axis=0, keepdims=True) for g, p in zip(grads, parts)]
        mean = means[0] if column == 0 else means[0] + means[1]
        grads = [(p * (g - mean) * scale).astype(jnp.bfloat16) for g, p in zip(grads, parts)]
        parts = [p.astype(jnp.bfloat16) for p in parts]
        if column == 0:
            parts.append(jnp.zeros((block, block), jnp.bfloat16))
            grads.append(jnp.zeros((block, block), jnp.bfloat16))
        probs_columns.append(jnp.concatenate(parts, axis=0))
        grads_columns.append(jnp.concatenate(grads, axis=0))
    return jnp.concatenate(probs_columns, axis=1), jnp.concatenate(grads_columns, axis=1)


def backward(length, xq, xkv, grad, weights, table, gq, gkv, qw, kw, vw, rot_out, ready):
    wq, wk, wv = weights
    n_seq = xq.shape[0] // length
    wide = wk.shape[1]
    heads = wide // DN
    low = lax.broadcasted_iota(jnp.int32, (length, TILE), 1) < DR
    spans = [slice(s * length, (s + 1) * length) for s in range(n_seq)]

    ready[0]()
    cos_low, sin_low = table[:, :TILE], table[:, TILE:]
    cos_tiles = (cos_low, pltpu.roll(cos_low, DR, 1))
    sin_tiles = (sin_low, pltpu.roll(sin_low, DR, 1))
    latent = xkv[:, :KL]
    for pair in range(heads // 2):
        columns = slice(2 * DN * pair, 2 * DN * (pair + 1))
        keys = dot(latent, wk[:, columns])
        vw[:, columns] = dot(latent, wv[:, columns]).astype(jnp.bfloat16)
        for span in spans:
            rot = jnp.concatenate(
                [xkv[span, KL : KL + DR].astype(jnp.float32), jnp.zeros((length, DR), jnp.float32)],
                axis=1,
            )
            odd = pltpu.roll(keys[span, DN:], DR, 1)
            tiles = (
                keys[span, :DN],
                rot,
                jnp.where(low, 0.0, odd),
                jnp.where(low, odd, pltpu.roll(rot, DR, 1)),
            )
            for i, tile in enumerate(tiles):
                start = (4 * pair + i) * TILE
                kw[span, start : start + TILE] = tile.astype(jnp.bfloat16)
    ready[1]()
    for pair in range(heads // 2):
        queries = dot(xq[...], wq[:, PAIR * pair : PAIR * (pair + 1)])
        for span in spans:
            for i in range(3):
                part = rounded(queries[span, i * TILE : (i + 1) * TILE])
                if i > 0:
                    part = part * cos_tiles[i - 1] + swap_halves(part) * sin_tiles[i - 1]
                start = PAIR * pair + i * TILE
                qw[span, start : start + TILE] = part.astype(jnp.bfloat16)

    items = [(span, head) for span in spans for head in range(heads)]

    def windows(span, head):
        start = PAIR * (head // 2) + TILE * (head % 2)
        return (
            qw[span, start : start + 2 * TILE],
            kw[span, 2 * TILE * head : 2 * TILE * (head + 1)],
            slice(head * DN, (head + 1) * DN),
        )

    def first_products(span, head):
        query_window, key_window, columns = windows(span, head)
        return (
            dot(key_window, query_window, NT),
            dot(vw[span, columns], grad[span, columns], NT),
        )

    rot_sums = [jnp.zeros((length, TILE), jnp.float32) for _ in spans]
    pending = first_products(*items[0])
    even_part = None
    for index, (span, head) in enumerate(items):
        products = pending
        if index + 1 < len(items):
            pending = first_products(*items[index + 1])
        probs, grad_scores = softmax_grads(*products)
        query_window, key_window, columns = windows(span, head)
        gkv[span, wide + head * DN : wide + (head + 1) * DN] = dot(probs, grad[span, columns]).astype(
            jnp.bfloat16
        )
        key_part = dot(grad_scores, query_window)
        query_part = dot(grad_scores, key_window, TN)
        seq = index // heads
        if head % 2 == 0:
            gkv[span, columns] = key_part[:, :TILE].astype(jnp.bfloat16)
            if rot_out is not None:
                rot_sums[seq] = rot_sums[seq] + rounded(key_part[:, TILE:])
            even_part = query_part
            continue
        turned = pltpu.roll(key_part[:, TILE:], DR, 1)
        gkv[span, columns] = jnp.where(low, pltpu.roll(key_part[:, :TILE], DR, 1), turned).astype(
            jnp.bfloat16
        )
        if rot_out is not None:
            rot_sums[seq] = rot_sums[seq] + rounded(turned)
        parts = [
            even_part[:, :TILE],
            even_part[:, TILE:] + query_part[:, :TILE],
            query_part[:, TILE:],
        ]
        for i in range(3):
            part = parts[i]
            if i > 0:
                part = rounded(part)
                part = part * cos_tiles[i - 1] - swap_halves(part) * sin_tiles[i - 1]
            start = PAIR * (head // 2) + i * TILE
            gq[span, start : start + TILE] = part.astype(jnp.bfloat16)
    if rot_out is not None:
        rot_out[...] = rot_sums[0]


def raw_grads(xq, xkv, gq, gkv, sums, previous, squares):
    wide = sums[1].shape[1]
    total = jnp.zeros((8, TILE), jnp.float32)
    step = KL
    for block in range(QL // step + 1):
        if block < QL // step:
            rows = slice(block * step, (block + 1) * step)
            targets = ((0, rows, dot(xq[:, rows], gq[...], TN)),)
        else:
            rows = slice(0, KL)
            product = dot(xkv[:, :KL], gkv[...], TN)
            targets = ((1, rows, product[:, :wide]), (2, rows, product[:, wide:]))
        for which, rows, product in targets:
            if previous is not None:
                product = product + previous[which][rows, :]
            sums[which][rows, :] = product
            if squares is None:
                continue
            folded = jnp.zeros((8, product.shape[1]), jnp.float32)
            for start in range(rows.start, rows.stop, 64):
                part = sums[which][start : start + 64, :]
                folded = folded + jnp.sum((part * part).reshape(8, 8, part.shape[1]), axis=0)
            for column in range(0, product.shape[1], TILE):
                total = total + folded[:, column : column + TILE]
    if squares is not None:
        squares[...] = total


def load_kernel(place, xq, kvt, grad, packed, cotangent, kv_rows, sem):
    half = packed.shape[0]
    rows = pl.ds(pl.multiple_of(place[1] * half, half), half)
    pieces = ((kvt.at[:, rows], kv_rows), (xq.at[rows], packed.at[:, :QL]), (grad, cotangent))
    copies = [pltpu.make_async_copy(*piece, sem.at[i]) for i, piece in enumerate(pieces)]
    for copy in copies:
        copy.start()
    copies[0].wait()
    for block in range(0, KL + DR, TILE):
        stop = min(block + TILE, KL + DR)
        packed[:, QL + block : QL + stop] = kv_rows[block:stop, :].T
    packed[:, LATENT:] = jnp.zeros((half, TILE - DR), jnp.bfloat16)
    for copy in copies[1:]:
        copy.wait()


def own_kernel(n_head, place, xq_in, kvt_in, grad_in, wq_in, wk_in, wv_in, table_in, *refs):
    wq, wk, wv, table, xq, xkv, gq, gkv, keep, send_stay, send_go, *refs = refs
    kvt, grad, qw, kw, vw, term, sem = refs
    pieces = (
        (kvt_in, kvt),
        (table_in, table),
        (wk_in, wk),
        (wv_in, wv),
        (xq_in, xq),
        (wq_in, wq),
        (grad_in, grad),
    )
    copies = [pltpu.make_async_copy(*piece, sem.at[i]) for i, piece in enumerate(pieces)]
    for copy in copies:
        copy.start()

    def latents_ready():
        for copy in copies[:4]:
            copy.wait()
        for block in range(0, KL + DR, TILE):
            stop = min(block + TILE, KL + DR)
            xkv[:, block:stop] = kvt[block:stop, :].T

    def queries_ready():
        for copy in copies[4:]:
            copy.wait()

    length = xq.shape[0]
    rot = term.at[:, QL + KL :]
    ready = (latents_ready, queries_ready)
    backward(length, xq, xkv, grad, (wq, wk, wv), table, gq, gkv, qw, kw, vw, rot, ready)
    wide = wk.shape[1]
    term[:, :QL] = dot(gq[...], wq[...], NT)
    term[:, QL : QL + KL] = dot(gkv[:, :wide], wk[...], NT) + dot(gkv[:, wide:], wv[...], NT)
    rows = length // n_head
    chip, core = place[0], place[1]
    masks = [turned_round(k, n_head // 2) for k in range(n_head // 2)]

    def chosen(which):
        starts = [(2 * jnp.bitwise_xor(chip, mask) + which) * rows for mask in masks]
        return jnp.concatenate([term[pl.ds(pl.multiple_of(i, rows), rows), :] for i in starts])

    keep[...] = chosen(core)
    send = chosen(1 - core).astype(jnp.bfloat16)
    send_stay[...] = send[: send_stay.shape[0], :]
    send_go[...] = send[send_stay.shape[0] :, :]


def fold_kernel(keep, *refs):
    received, (stay, go) = refs[:-2], refs[-2:]
    total = jnp.concatenate([part[...] for part in received]).astype(jnp.float32) + keep[...]
    stay[...] = total[: stay.shape[0], :]
    go[...] = total[stay.shape[0] :, :].astype(jnp.bfloat16)


def far_kernel(n_seq, place, *refs):
    blocks, refs = refs[: 3 * n_seq], refs[3 * n_seq :]
    wq, wk, wv, table, xq, xkv, gq, gkv, grad, qw, kw, vw = refs
    half = blocks[0].shape[0]
    length = 2 * half
    core = place[1]
    for s in range(n_seq):
        mine, other, cotangent = blocks[3 * s : 3 * s + 3]
        for source, side in ((mine, core), (other, 1 - core)):
            rows = pl.ds(pl.multiple_of(s * length + side * half, half), half)
            xq[rows, :] = source[:, :QL]
            xkv[rows, :] = source[:, QL:LATENT]
        grad[s * length : (s + 1) * length, :] = cotangent[...]
    ready = (lambda: None, lambda: None)
    backward(length, xq, xkv, grad, (wq, wk, wv), table, gq, gkv, qw, kw, vw, None, ready)


def sums_kernel(first, last, xq, xkv, gq, gkv, *refs):
    previous, refs = (None, refs) if first else (refs[:3], refs[3:])
    squares = None
    if last:
        local, received, *refs, squares, latent_q, latent_kv = refs
        total = local[...] + received[...].astype(jnp.float32)
        latent_q[...] = total[:, :QL]
        latent_kv[...] = total[:, QL:LATENT]
    raw_grads(xq, xkv, gq, gkv, refs, previous, squares)


def add_kernel(left, right, out):
    out[...] = left[...] + right[...]


def scale_kernel(limit, sq, sk, sv, *refs):
    *parts, oq, ok, ov, bq, bk, bv, sem = refs
    total = parts[0][...]
    for part in parts[1:]:
        total = total + part[...]
    total = jnp.sum(total, keepdims=True)
    factor = jnp.minimum(1.0, limit / jnp.sqrt(total + eps))
    copies = []
    for source, buffer, out in ((sq, bq, oq), (sk, bk, ok), (sv, bv, ov)):
        for start in range(0, source.shape[0], 256):
            rows = slice(start, start + 256)
            buffer[rows, :] = (source[rows, :] * factor).astype(jnp.bfloat16)
            copy = pltpu.make_async_copy(buffer.at[rows], out.at[rows], sem.at[len(copies)])
            copy.start()
            copies.append(copy)
    for copy in copies:
        copy.wait()


def vmem(count):
    return [pl.BlockSpec(memory_space=pltpu.VMEM)] * count


def hbm(count):
    return [pl.BlockSpec(memory_space=pltpu.HBM)] * count


def params():
    return pltpu.CompilerParams(vmem_limit_bytes=VMEM_LIMIT)


def free():
    return pl.CostEstimate(flops=0, bytes_accessed=0, transcendentals=0)


def struct(shape, dtype):
    return jax.ShapeDtypeStruct(shape, dtype)


def exchange(value, axis, size, k):
    return lax.ppermute(value, axis, [(i, i ^ k) for i in range(size)])


def far_away(value):
    return pltpu.with_memory_space_constraint(value, pltpu.HBM)


def turned_round(mask, n_dp):
    bits = n_dp.bit_length() - 1
    return sum(((mask >> i) & 1) << (bits - 1 - i) for i in range(bits))


def across(value, n_dp, n_head, mask):
    masks = (mask, turned_round(mask, n_dp))
    pairs = [
        (d * n_head + h, (d ^ masks[h % 2]) * n_head + h) for d in range(n_dp) for h in range(n_head)
    ]
    return lax.ppermute(value, ("dp", "head"), pairs)


def per_device(n_dp, n_head, query_latent, kv_latent, out_grad, query_up, key_up, value_up):
    length = query_latent.shape[0]
    half = length // 2
    wide_q, wide_k = query_up.shape[1], key_up.shape[1]
    heads = wide_k // DN
    index = lax.axis_index("head")
    place = jnp.stack([index // 2, index % 2]).astype(jnp.int32)
    table = jnp.asarray(rotary_tables(length))
    smem = [pl.BlockSpec(memory_space=pltpu.SMEM)]
    inputs = [far_away(value) for value in (query_latent, kv_latent.T, out_grad)]
    width = QL + KL + TILE

    packed, cotangent = pl.pallas_call(
        load_kernel,
        out_shape=(
            pltpu.VMEM((half, width), jnp.bfloat16),
            pltpu.VMEM((length, wide_k), jnp.bfloat16),
        ),
        in_specs=smem + hbm(3),
        out_specs=vmem(2),
        scratch_shapes=[pltpu.VMEM((KL + DR, half), jnp.bfloat16), pltpu.SemaphoreType.DMA((3,))],
        compiler_params=params(),
        cost_estimate=free(),
        name="load",
    )(place, *inputs)

    packed, place = lax.optimization_barrier((packed, place))
    singles = [1 << i for i in reversed(range(n_dp.bit_length() - 1))]
    cotangents = {k: across(cotangent, n_dp, n_head, k) for k in singles}
    latents = {k: across(packed, n_dp, n_head, k) for k in singles}

    def rows_shape(rows):
        widths = (QL, KL + DR, wide_q, 2 * wide_k)
        return tuple(pltpu.VMEM((rows, width), jnp.bfloat16) for width in widths)

    def scratch(rows):
        widths = (wide_k, wide_q, 2 * TILE * heads, wide_k)
        return [pltpu.VMEM((rows, width), jnp.bfloat16) for width in widths]

    weights_shape = tuple(
        pltpu.VMEM(shape, jnp.bfloat16) for shape in ((QL, wide_q), (KL, wide_k), (KL, wide_k))
    )
    sums_shape = tuple(pltpu.VMEM(w.shape, jnp.float32) for w in weights_shape)
    *outs, keep, send_stay, send_go = pl.pallas_call(
        functools.partial(own_kernel, n_head),
        out_shape=(
            *weights_shape,
            pltpu.VMEM(table.shape, jnp.float32),
            *rows_shape(length),
            struct((half, width), jnp.float32),
            struct((half // 2, width), jnp.bfloat16),
            struct((half // 2, width), jnp.bfloat16),
        ),
        in_specs=smem + hbm(7),
        out_specs=vmem(11),
        scratch_shapes=[pltpu.VMEM((KL + DR, length), jnp.bfloat16)]
        + scratch(length)
        + [pltpu.VMEM((length, width), jnp.float32), pltpu.SemaphoreType.DMA((7,))],
        compiler_params=params(),
        cost_estimate=free(),
        name="own",
    )(place, *inputs, *[far_away(value) for value in (query_up, key_up, value_up, table)])
    weights, found = outs[:4], outs[4:]

    rows = length // n_head

    def add_sums(found, sums, terms):
        extra_out = ()
        if terms:
            extra_out = (
                struct((8, TILE), jnp.float32),
                struct((rows, QL), jnp.float32),
                struct((rows, KL + DR), jnp.float32),
            )
        return list(
            pl.pallas_call(
                functools.partial(sums_kernel, not sums, bool(terms)),
                out_shape=(*sums_shape, *extra_out),
                in_specs=vmem(4 + len(sums) + len(terms)),
                out_specs=vmem(3 + len(extra_out)),
                input_output_aliases={4: 0, 5: 1, 6: 2} if sums else {},
                compiler_params=params(),
                cost_estimate=free(),
                name="sums_last" if terms else "sums",
            )(*found, *sums, *terms)
        )

    sums = add_sums(found, [], [])

    def fold(keep, *received):
        half_shape = (keep.shape[0] // 2, width)
        return pl.pallas_call(
            fold_kernel,
            out_shape=(struct(half_shape, jnp.float32), struct(half_shape, jnp.bfloat16)),
            in_specs=vmem(1 + len(received)),
            out_specs=vmem(2),
            compiler_params=params(),
            cost_estimate=free(),
            name="fold",
        )(keep, *received)

    stay, go = fold(keep, *[exchange(send, "head", n_head, 1) for send in (send_stay, send_go)])
    bits = [2 << i for i in range(n_head.bit_length() - 2)]
    for bit in bits[:-2]:
        stay, go = fold(stay, exchange(go, "head", n_head, bit))
    came = exchange(go, "head", n_head, bits[-2])

    values = [latents[k] for k in singles] + [cotangents[k] for k in singles]
    *values, sums[2] = lax.optimization_barrier((*values, sums[2]))
    latents = dict(zip(singles, values))
    cotangents = dict(zip(singles, values[len(singles) :]))
    for k in range(3, n_dp):
        if k not in latents:
            latents[k] = across(latents[k & (k - 1)], n_dp, n_head, k & -k)
            cotangents[k] = across(cotangents[k & (k - 1)], n_dp, n_head, k & -k)
    def swapped(k):
        return exchange(latents[turned_round(k, n_dp)], "head", n_head, 1)

    groups = [(1, 2)] + [(k,) for k in range(3, n_dp)]
    for group in groups:
        n_seq = len(group)
        blocks = []
        for k in group:
            blocks += [latents[k], swapped(k), cotangents[k]]
        found = list(
            pl.pallas_call(
                functools.partial(far_kernel, n_seq),
                out_shape=rows_shape(n_seq * length),
                in_specs=smem + vmem(len(blocks) + 4),
                out_specs=vmem(4),
                scratch_shapes=scratch(n_seq * length),
                compiler_params=params(),
                cost_estimate=free(),
                name="far",
            )(place, *blocks, *weights)
        )
        last = group is groups[-1]
        if not last:
            k = groups[groups.index(group) + 1][0]
            latents[k], found[3], came = lax.optimization_barrier((latents[k], found[3], came))
            if group is groups[0]:
                stay, go = fold(stay, came)
                terms = [stay, exchange(go, "head", n_head, bits[-1])]
        sums = add_sums(found, sums, terms if last else [])
    *sums, squares, latent_q, latent_kv = sums

    count = (QL * wide_q + 2 * KL * wide_k) * n_head
    limit = max_rms * count**0.5
    squares = pl.pallas_call(
        add_kernel,
        out_shape=struct((8, TILE), jnp.float32),
        in_specs=vmem(2),
        out_specs=pl.BlockSpec(memory_space=pltpu.VMEM),
        compiler_params=params(),
        cost_estimate=free(),
        name="add",
    )(squares, exchange(squares, "head", n_head, 1))
    parts = [squares] + [exchange(squares, "head", n_head, 2 * k) for k in range(1, n_head // 2)]
    scaled = pl.pallas_call(
        functools.partial(scale_kernel, limit),
        out_shape=tuple(struct(w.shape, jnp.bfloat16) for w in weights_shape),
        in_specs=vmem(3 + len(parts)),
        out_specs=hbm(3),
        scratch_shapes=list(weights_shape)
        + [pltpu.SemaphoreType.DMA(((QL + 2 * KL) // 256,))],
        compiler_params=params(),
        cost_estimate=free(),
        name="scale",
    )(*sums, *parts)
    return (latent_q, latent_kv, *scaled)


def solution(mesh):
    placed = (
        P("dp", None),
        P("dp", None),
        P("dp", "head"),
        P(None, "head"),
        P(None, "head"),
        P(None, "head"),
    )
    return jax.shard_map(
        functools.partial(per_device, mesh.shape["dp"], mesh.shape["head"]),
        mesh=mesh,
        in_specs=placed,
        out_specs=(
            P(("dp", "head"), None),
            P(("dp", "head"), None),
            P(None, "head"),
            P(None, "head"),
            P(None, "head"),
        ),
        check_vma=False,
    )
```

```python
import functools

import jax
import jax.numpy as jnp
import numpy as np
from jax import lax
from jax.experimental import pallas as pl
from jax.experimental.pallas import tpu as pltpu
from jax.sharding import PartitionSpec as P

QL = 1536
KL = 512
DN = 128
DR = 64
TILE = 128
WIDTH = DN + DR
PAIR = 2 * WIDTH
LATENT = QL + KL + DR

max_rms = 1.0
eps = 1e-06
VMEM_LIMIT = 32 * 2**20

NT = (((1,), (1,)), ((), ()))
TN = (((0,), (0,)), ((), ()))


def dot(left, right, dims=(((1,), (0,)), ((), ()))):
    return lax.dot_general(left, right, dims, preferred_element_type=jnp.float32)


def rotary_tables(length):
    half = DR // 2
    freqs = np.float32(10000.0) ** (
        np.float32(-2.0) * np.arange(half, dtype=np.float32) / np.float32(DR)
    )
    angle = np.arange(length, dtype=np.float32)[:, None] * freqs.astype(np.float32)[None, :]
    cosine, sine = np.cos(angle), np.sin(angle)
    ones, zeros = np.ones((length, DR), np.float32), np.zeros((length, DR), np.float32)
    return np.concatenate([cosine, cosine, ones, -sine, sine, zeros], axis=1)


def swap_halves(tile):
    lane = lax.broadcasted_iota(jnp.int32, tile.shape, 1)
    first = lane % DR < DR // 2
    return jnp.where(
        first, pltpu.roll(tile, TILE - DR // 2, 1), pltpu.roll(tile, DR // 2, 1)
    )


def rounded(values):
    return values.astype(jnp.bfloat16).astype(jnp.float32)


def softmax_grads(scores, grad_probs):
    length = scores.shape[0]
    block = length // 2
    scale = 1.0 / (DN + DR) ** 0.5
    key = lax.broadcasted_iota(jnp.int32, (block, block), 0)
    query = lax.broadcasted_iota(jnp.int32, (block, block), 1)
    allowed = key <= query
    grad_probs = rounded(grad_probs)
    probs_columns, grads_columns = [], []
    for column in range(2):
        columns = slice(column * block, (column + 1) * block)
        parts = [scores[:block, columns], scores[block:, columns]][: column + 1]
        parts[-1] = jnp.where(allowed, parts[-1], -jnp.inf)
        tops = [jnp.max(part, axis=0, keepdims=True) for part in parts]
        top = tops[0] if column == 0 else jnp.maximum(*tops)
        parts = [jnp.exp((part - top) * scale) for part in parts]
        sums = [jnp.sum(part, axis=0, keepdims=True) for part in parts]
        inverse = 1.0 / (sums[0] if column == 0 else sums[0] + sums[1])
        parts = [part * inverse for part in parts]
        grads = [grad_probs[:block, columns], grad_probs[block:, columns]][: column + 1]
        means = [jnp.sum(g * p, axis=0, keepdims=True) for g, p in zip(grads, parts)]
        mean = means[0] if column == 0 else means[0] + means[1]
        grads = [(p * (g - mean) * scale).astype(jnp.bfloat16) for g, p in zip(grads, parts)]
        parts = [p.astype(jnp.bfloat16) for p in parts]
        if column == 0:
            parts.append(jnp.zeros((block, block), jnp.bfloat16))
            grads.append(jnp.zeros((block, block), jnp.bfloat16))
        probs_columns.append(jnp.concatenate(parts, axis=0))
        grads_columns.append(jnp.concatenate(grads, axis=0))
    return jnp.concatenate(probs_columns, axis=1), jnp.concatenate(grads_columns, axis=1)


def backward(length, xq, xkv, grad, weights, table, gq, gkv, qw, kw, vw, rot_out, ready):
    wq, wk, wv = weights
    n_seq = xq.shape[0] // length
    wide = wk.shape[1]
    heads = wide // DN
    low = lax.broadcasted_iota(jnp.int32, (length, TILE), 1) < DR
    spans = [slice(s * length, (s + 1) * length) for s in range(n_seq)]

    ready[0]()
    cos_low, sin_low = table[:, :TILE], table[:, TILE:]
    cos_tiles = (cos_low, pltpu.roll(cos_low, DR, 1))
    sin_tiles = (sin_low, pltpu.roll(sin_low, DR, 1))
    latent = xkv[:, :KL]
    for pair in range(heads // 2):
        columns = slice(2 * DN * pair, 2 * DN * (pair + 1))
        keys = dot(latent, wk[:, columns])
        vw[:, columns] = dot(latent, wv[:, columns]).astype(jnp.bfloat16)
        for span in spans:
            rot = jnp.concatenate(
                [xkv[span, KL : KL + DR].astype(jnp.float32), jnp.zeros((length, DR), jnp.float32)],
                axis=1,
            )
            odd = pltpu.roll(keys[span, DN:], DR, 1)
            tiles = (
                keys[span, :DN],
                rot,
                jnp.where(low, 0.0, odd),
                jnp.where(low, odd, pltpu.roll(rot, DR, 1)),
            )
            for i, tile in enumerate(tiles):
                start = (4 * pair + i) * TILE
                kw[span, start : start + TILE] = tile.astype(jnp.bfloat16)
    ready[1]()
    for pair in range(heads // 2):
        queries = dot(xq[...], wq[:, PAIR * pair : PAIR * (pair + 1)])
        for span in spans:
            for i in range(3):
                part = rounded(queries[span, i * TILE : (i + 1) * TILE])
                if i > 0:
                    part = part * cos_tiles[i - 1] + swap_halves(part) * sin_tiles[i - 1]
                start = PAIR * pair + i * TILE
                qw[span, start : start + TILE] = part.astype(jnp.bfloat16)

    items = [(span, head) for span in spans for head in range(heads)]

    def windows(span, head):
        start = PAIR * (head // 2) + TILE * (head % 2)
        return (
            qw[span, start : start + 2 * TILE],
            kw[span, 2 * TILE * head : 2 * TILE * (head + 1)],
            slice(head * DN, (head + 1) * DN),
        )

    def first_products(span, head):
        query_window, key_window, columns = windows(span, head)
        return (
            dot(key_window, query_window, NT),
            dot(vw[span, columns], grad[span, columns], NT),
        )

    rot_sums = [jnp.zeros((length, TILE), jnp.float32) for _ in spans]
    pending = first_products(*items[0])
    even_part = None
    for index, (span, head) in enumerate(items):
        products = pending
        if index + 1 < len(items):
            pending = first_products(*items[index + 1])
        probs, grad_scores = softmax_grads(*products)
        query_window, key_window, columns = windows(span, head)
        gkv[span, wide + head * DN : wide + (head + 1) * DN] = dot(probs, grad[span, columns]).astype(
            jnp.bfloat16
        )
        key_part = dot(grad_scores, query_window)
        query_part = dot(grad_scores, key_window, TN)
        seq = index // heads
        if head % 2 == 0:
            gkv[span, columns] = key_part[:, :TILE].astype(jnp.bfloat16)
            if rot_out is not None:
                rot_sums[seq] = rot_sums[seq] + rounded(key_part[:, TILE:])
            even_part = query_part
            continue
        turned = pltpu.roll(key_part[:, TILE:], DR, 1)
        gkv[span, columns] = jnp.where(low, pltpu.roll(key_part[:, :TILE], DR, 1), turned).astype(
            jnp.bfloat16
        )
        if rot_out is not None:
            rot_sums[seq] = rot_sums[seq] + rounded(turned)
        parts = [
            even_part[:, :TILE],
            even_part[:, TILE:] + query_part[:, :TILE],
            query_part[:, TILE:],
        ]
        for i in range(3):
            part = parts[i]
            if i > 0:
                part = rounded(part)
                part = part * cos_tiles[i - 1] - swap_halves(part) * sin_tiles[i - 1]
            start = PAIR * (head // 2) + i * TILE
            gq[span, start : start + TILE] = part.astype(jnp.bfloat16)
    if rot_out is not None:
        rot_out[...] = rot_sums[0]


def raw_grads(xq, xkv, gq, gkv, sums, previous, squares):
    wide = sums[1].shape[1]
    total = jnp.zeros((8, TILE), jnp.float32)
    step = KL
    for block in range(QL // step + 1):
        if block < QL // step:
            rows = slice(block * step, (block + 1) * step)
            targets = ((0, rows, dot(xq[:, rows], gq[...], TN)),)
        else:
            rows = slice(0, KL)
            product = dot(xkv[:, :KL], gkv[...], TN)
            targets = ((1, rows, product[:, :wide]), (2, rows, product[:, wide:]))
        for which, rows, product in targets:
            if previous is not None:
                product = product + previous[which][rows, :]
            sums[which][rows, :] = product
            if squares is None:
                continue
            folded = jnp.zeros((8, product.shape[1]), jnp.float32)
            for start in range(rows.start, rows.stop, 64):
                part = sums[which][start : start + 64, :]
                folded = folded + jnp.sum((part * part).reshape(8, 8, part.shape[1]), axis=0)
            for column in range(0, product.shape[1], TILE):
                total = total + folded[:, column : column + TILE]
    if squares is not None:
        squares[...] = total


def load_kernel(place, xq, kvt, grad, packed, kv_rows, sem):
    half, wide = packed.shape[0], grad.shape[1]
    width = QL + KL + TILE
    rows = pl.ds(pl.multiple_of(place[1] * half, half), half)
    pieces = (
        (kvt.at[:, rows], kv_rows),
        (xq.at[rows], packed.at[:, :QL]),
        (grad.at[:half], packed.at[:, width : width + wide]),
        (grad.at[half:], packed.at[:, width + wide :]),
    )
    copies = [pltpu.make_async_copy(*piece, sem.at[i]) for i, piece in enumerate(pieces)]
    for copy in copies:
        copy.start()
    copies[0].wait()
    for block in range(0, KL + DR, TILE):
        stop = min(block + TILE, KL + DR)
        packed[:, QL + block : QL + stop] = kv_rows[block:stop, :].T
    packed[:, LATENT:width] = jnp.zeros((half, TILE - DR), jnp.bfloat16)
    for copy in copies[1:]:
        copy.wait()


def own_kernel(n_head, place, xq_in, kvt_in, grad_in, wq_in, wk_in, wv_in, table_in, *refs):
    wq, wk, wv, table, xq, xkv, gq, gkv, keep, send_stay, send_go, *refs = refs
    kvt, grad, qw, kw, vw, term, sem = refs
    pieces = (
        (kvt_in, kvt),
        (table_in, table),
        (wk_in, wk),
        (wv_in, wv),
        (xq_in, xq),
        (wq_in, wq),
        (grad_in, grad),
    )
    copies = [pltpu.make_async_copy(*piece, sem.at[i]) for i, piece in enumerate(pieces)]
    for copy in copies:
        copy.start()

    def latents_ready():
        for copy in copies[:4]:
            copy.wait()
        for block in range(0, KL + DR, TILE):
            stop = min(block + TILE, KL + DR)
            xkv[:, block:stop] = kvt[block:stop, :].T

    def queries_ready():
        for copy in copies[4:]:
            copy.wait()

    length = xq.shape[0]
    rot = term.at[:, QL + KL :]
    ready = (latents_ready, queries_ready)
    backward(length, xq, xkv, grad, (wq, wk, wv), table, gq, gkv, qw, kw, vw, rot, ready)
    wide = wk.shape[1]
    term[:, :QL] = dot(gq[...], wq[...], NT)
    term[:, QL : QL + KL] = dot(gkv[:, :wide], wk[...], NT) + dot(gkv[:, wide:], wv[...], NT)
    rows = length // n_head
    chip, core = place[0], place[1]
    masks = [turned_round(k, n_head // 2) for k in range(n_head // 2)]

    def chosen(which):
        starts = [(2 * jnp.bitwise_xor(chip, mask) + which) * rows for mask in masks]
        return jnp.concatenate([term[pl.ds(pl.multiple_of(i, rows), rows), :] for i in starts])

    keep[...] = chosen(core)
    send = chosen(1 - core).astype(jnp.bfloat16)
    send_stay[...] = send[: send_stay.shape[0], :]
    send_go[...] = send[send_stay.shape[0] :, :]


def fold_kernel(keep, *refs):
    received, (stay, go) = refs[:-2], refs[-2:]
    total = jnp.concatenate([part[...] for part in received]).astype(jnp.float32) + keep[...]
    stay[...] = total[: stay.shape[0], :]
    go[...] = total[stay.shape[0] :, :].astype(jnp.bfloat16)


def far_kernel(n_seq, place, *refs):
    blocks, refs = refs[: 2 * n_seq], refs[2 * n_seq :]
    wq, wk, wv, table, xq, xkv, gq, gkv, grad, qw, kw, vw = refs
    half, wide = blocks[0].shape[0], grad.shape[1]
    length = 2 * half
    width = QL + KL + TILE
    core = place[1]
    for s in range(n_seq):
        mine, other = blocks[2 * s : 2 * s + 2]
        for source, side in ((mine, core), (other, 1 - core)):
            rows = pl.ds(pl.multiple_of(s * length + side * half, half), half)
            xq[rows, :] = source[:, :QL]
            xkv[rows, :] = source[:, QL:LATENT]
        start = s * length
        grad[start : start + half, :] = mine[:, width : width + wide]
        grad[start + half : start + length, :] = mine[:, width + wide :]
    ready = (lambda: None, lambda: None)
    backward(length, xq, xkv, grad, (wq, wk, wv), table, gq, gkv, qw, kw, vw, None, ready)


def sums_kernel(first, last, xq, xkv, gq, gkv, *refs):
    previous, refs = (None, refs) if first else (refs[:3], refs[3:])
    squares = None
    if last:
        local, received, *refs, squares, latent_q, latent_kv = refs
        total = local[...] + received[...].astype(jnp.float32)
        latent_q[...] = total[:, :QL]
        latent_kv[...] = total[:, QL:LATENT]
    raw_grads(xq, xkv, gq, gkv, refs, previous, squares)


def add_kernel(left, right, out):
    out[...] = left[...] + right[...]


def scale_kernel(limit, sq, sk, sv, *refs):
    *parts, oq, ok, ov, bq, bk, bv, sem = refs
    total = parts[0][...]
    for part in parts[1:]:
        total = total + part[...]
    total = jnp.sum(total, keepdims=True)
    factor = jnp.minimum(1.0, limit / jnp.sqrt(total + eps))
    copies = []
    for source, buffer, out in ((sq, bq, oq), (sk, bk, ok), (sv, bv, ov)):
        for start in range(0, source.shape[0], 256):
            rows = slice(start, start + 256)
            buffer[rows, :] = (source[rows, :] * factor).astype(jnp.bfloat16)
            copy = pltpu.make_async_copy(buffer.at[rows], out.at[rows], sem.at[len(copies)])
            copy.start()
            copies.append(copy)
    for copy in copies:
        copy.wait()


def vmem(count):
    return [pl.BlockSpec(memory_space=pltpu.VMEM)] * count


def hbm(count):
    return [pl.BlockSpec(memory_space=pltpu.HBM)] * count


def params():
    return pltpu.CompilerParams(vmem_limit_bytes=VMEM_LIMIT)


def free():
    return pl.CostEstimate(flops=0, bytes_accessed=0, transcendentals=0)


def struct(shape, dtype):
    return jax.ShapeDtypeStruct(shape, dtype)


def exchange(value, axis, size, k):
    return lax.ppermute(value, axis, [(i, i ^ k) for i in range(size)])


def far_away(value):
    return pltpu.with_memory_space_constraint(value, pltpu.HBM)


def turned_round(mask, n_dp):
    bits = n_dp.bit_length() - 1
    return sum(((mask >> i) & 1) << (bits - 1 - i) for i in range(bits))


def across(value, n_dp, n_head, mask):
    masks = (mask, turned_round(mask, n_dp))
    pairs = [
        (d * n_head + h, (d ^ masks[h % 2]) * n_head + h) for d in range(n_dp) for h in range(n_head)
    ]
    return lax.ppermute(value, ("dp", "head"), pairs)


def per_device(n_dp, n_head, query_latent, kv_latent, out_grad, query_up, key_up, value_up):
    length = query_latent.shape[0]
    half = length // 2
    wide_q, wide_k = query_up.shape[1], key_up.shape[1]
    heads = wide_k // DN
    index = lax.axis_index("head")
    place = jnp.stack([index // 2, index % 2]).astype(jnp.int32)
    table = jnp.asarray(rotary_tables(length))
    smem = [pl.BlockSpec(memory_space=pltpu.SMEM)]
    inputs = [far_away(value) for value in (query_latent, kv_latent.T, out_grad)]
    width = QL + KL + TILE

    packed = pl.pallas_call(
        load_kernel,
        out_shape=pltpu.VMEM((half, width + 2 * wide_k), jnp.bfloat16),
        in_specs=smem + hbm(3),
        out_specs=pl.BlockSpec(memory_space=pltpu.VMEM),
        scratch_shapes=[pltpu.VMEM((KL + DR, half), jnp.bfloat16), pltpu.SemaphoreType.DMA((4,))],
        compiler_params=params(),
        cost_estimate=free(),
        name="load",
    )(place, *inputs)
    packed, place = lax.optimization_barrier((packed, place))
    singles = [1 << i for i in reversed(range(n_dp.bit_length() - 1))]
    received = {k: across(packed, n_dp, n_head, k) for k in singles}

    def rows_shape(rows):
        widths = (QL, KL + DR, wide_q, 2 * wide_k)
        return tuple(pltpu.VMEM((rows, width), jnp.bfloat16) for width in widths)

    def scratch(rows):
        widths = (wide_k, wide_q, 2 * TILE * heads, wide_k)
        return [pltpu.VMEM((rows, width), jnp.bfloat16) for width in widths]

    weights_shape = tuple(
        pltpu.VMEM(shape, jnp.bfloat16) for shape in ((QL, wide_q), (KL, wide_k), (KL, wide_k))
    )
    sums_shape = tuple(pltpu.VMEM(w.shape, jnp.float32) for w in weights_shape)
    *outs, keep, send_stay, send_go = pl.pallas_call(
        functools.partial(own_kernel, n_head),
        out_shape=(
            *weights_shape,
            pltpu.VMEM(table.shape, jnp.float32),
            *rows_shape(length),
            struct((half, width), jnp.float32),
            struct((half // 2, width), jnp.bfloat16),
            struct((half // 2, width), jnp.bfloat16),
        ),
        in_specs=smem + hbm(7),
        out_specs=vmem(11),
        scratch_shapes=[pltpu.VMEM((KL + DR, length), jnp.bfloat16)]
        + scratch(length)
        + [pltpu.VMEM((length, width), jnp.float32), pltpu.SemaphoreType.DMA((7,))],
        compiler_params=params(),
        cost_estimate=free(),
        name="own",
    )(place, *inputs, *[far_away(value) for value in (query_up, key_up, value_up, table)])
    weights, found = outs[:4], outs[4:]

    rows = length // n_head

    def add_sums(found, sums, terms):
        extra_out = ()
        if terms:
            extra_out = (
                struct((8, TILE), jnp.float32),
                struct((rows, QL), jnp.float32),
                struct((rows, KL + DR), jnp.float32),
            )
        return list(
            pl.pallas_call(
                functools.partial(sums_kernel, not sums, bool(terms)),
                out_shape=(*sums_shape, *extra_out),
                in_specs=vmem(4 + len(sums) + len(terms)),
                out_specs=vmem(3 + len(extra_out)),
                input_output_aliases={4: 0, 5: 1, 6: 2} if sums else {},
                compiler_params=params(),
                cost_estimate=free(),
                name="sums_last" if terms else "sums",
            )(*found, *sums, *terms)
        )

    sums = add_sums(found, [], [])

    def fold(keep, *received):
        half_shape = (keep.shape[0] // 2, width)
        return pl.pallas_call(
            fold_kernel,
            out_shape=(struct(half_shape, jnp.float32), struct(half_shape, jnp.bfloat16)),
            in_specs=vmem(1 + len(received)),
            out_specs=vmem(2),
            compiler_params=params(),
            cost_estimate=free(),
            name="fold",
        )(keep, *received)

    stay, go = fold(keep, *[exchange(send, "head", n_head, 1) for send in (send_stay, send_go)])
    bits = [2 << i for i in range(n_head.bit_length() - 2)]
    for bit in bits[:-2]:
        stay, go = fold(stay, exchange(go, "head", n_head, bit))
    came = exchange(go, "head", n_head, bits[-2])

    values = [received[k] for k in singles]
    *values, sums[2], came = lax.optimization_barrier((*values, sums[2], came))
    received = dict(zip(singles, values))
    for k in range(3, n_dp):
        if k not in received:
            received[k] = across(received[k & (k - 1)], n_dp, n_head, k & -k)
    stay, go = fold(stay, came)
    terms = [stay, exchange(go, "head", n_head, bits[-1])]

    def swapped(k):
        return exchange(received[turned_round(k, n_dp)], "head", n_head, 1)

    groups = [(1, 2)] + [(k,) for k in range(3, n_dp)]
    for group in groups:
        n_seq = len(group)
        blocks = []
        for k in group:
            blocks += [received[k], swapped(k)]
        found = list(
            pl.pallas_call(
                functools.partial(far_kernel, n_seq),
                out_shape=rows_shape(n_seq * length),
                in_specs=smem + vmem(len(blocks) + 4),
                out_specs=vmem(4),
                scratch_shapes=scratch(n_seq * length),
                compiler_params=params(),
                cost_estimate=free(),
                name="far",
            )(place, *blocks, *weights)
        )
        last = group is groups[-1]
        if group is groups[0]:
            found[3], terms[1] = lax.optimization_barrier((found[3], terms[1]))
        sums = add_sums(found, sums, terms if last else [])
        if not last:
            k = groups[groups.index(group) + 1][0]
            received[k], sums[2] = lax.optimization_barrier((received[k], sums[2]))
    *sums, squares, latent_q, latent_kv = sums

    count = (QL * wide_q + 2 * KL * wide_k) * n_head
    limit = max_rms * count**0.5
    squares = pl.pallas_call(
        add_kernel,
        out_shape=struct((8, TILE), jnp.float32),
        in_specs=vmem(2),
        out_specs=pl.BlockSpec(memory_space=pltpu.VMEM),
        compiler_params=params(),
        cost_estimate=free(),
        name="add",
    )(squares, exchange(squares, "head", n_head, 1))
    parts = [squares] + [exchange(squares, "head", n_head, 2 * k) for k in range(1, n_head // 2)]
    scaled = pl.pallas_call(
        functools.partial(scale_kernel, limit),
        out_shape=tuple(struct(w.shape, jnp.bfloat16) for w in weights_shape),
        in_specs=vmem(3 + len(parts)),
        out_specs=hbm(3),
        scratch_shapes=list(weights_shape)
        + [pltpu.SemaphoreType.DMA(((QL + 2 * KL) // 256,))],
        compiler_params=params(),
        cost_estimate=free(),
        name="scale",
    )(*sums, *parts)
    return (latent_q, latent_kv, *scaled)


def solution(mesh):
    placed = (
        P("dp", None),
        P("dp", None),
        P("dp", "head"),
        P(None, "head"),
        P(None, "head"),
        P(None, "head"),
    )
    return jax.shard_map(
        functools.partial(per_device, mesh.shape["dp"], mesh.shape["head"]),
        mesh=mesh,
        in_specs=placed,
        out_specs=(
            P(("dp", "head"), None),
            P(("dp", "head"), None),
            P(None, "head"),
            P(None, "head"),
            P(None, "head"),
        ),
        check_vma=False,
    )
```

```python
import functools

import jax
import jax.numpy as jnp
import numpy as np
from jax import lax
from jax.experimental import pallas as pl
from jax.experimental.pallas import tpu as pltpu
from jax.sharding import PartitionSpec as P

QL = 1536
KL = 512
DN = 128
DR = 64
TILE = 128
WIDTH = DN + DR
PAIR = 2 * WIDTH
LATENT = QL + KL + DR

max_rms = 1.0
eps = 1e-06
VMEM_LIMIT = 32 * 2**20

NT = (((1,), (1,)), ((), ()))
TN = (((0,), (0,)), ((), ()))


def dot(left, right, dims=(((1,), (0,)), ((), ()))):
    return lax.dot_general(left, right, dims, preferred_element_type=jnp.float32)


def rotary_tables(length):
    half = DR // 2
    freqs = np.float32(10000.0) ** (
        np.float32(-2.0) * np.arange(half, dtype=np.float32) / np.float32(DR)
    )
    angle = np.arange(length, dtype=np.float32)[:, None] * freqs.astype(np.float32)[None, :]
    cosine, sine = np.cos(angle), np.sin(angle)
    ones, zeros = np.ones((length, DR), np.float32), np.zeros((length, DR), np.float32)
    return np.concatenate([cosine, cosine, ones, -sine, sine, zeros], axis=1)


def swap_halves(tile):
    lane = lax.broadcasted_iota(jnp.int32, tile.shape, 1)
    first = lane % DR < DR // 2
    return jnp.where(
        first, pltpu.roll(tile, TILE - DR // 2, 1), pltpu.roll(tile, DR // 2, 1)
    )


def rounded(values):
    return values.astype(jnp.bfloat16).astype(jnp.float32)


def softmax_grads(scores, grad_probs):
    length = scores.shape[0]
    block = length // 2
    scale = 1.0 / (DN + DR) ** 0.5
    key = lax.broadcasted_iota(jnp.int32, (block, block), 0)
    query = lax.broadcasted_iota(jnp.int32, (block, block), 1)
    allowed = key <= query
    grad_probs = rounded(grad_probs)
    probs_columns, grads_columns = [], []
    for column in range(2):
        columns = slice(column * block, (column + 1) * block)
        parts = [scores[:block, columns], scores[block:, columns]][: column + 1]
        parts[-1] = jnp.where(allowed, parts[-1], -jnp.inf)
        tops = [jnp.max(part, axis=0, keepdims=True) for part in parts]
        top = tops[0] if column == 0 else jnp.maximum(*tops)
        parts = [jnp.exp((part - top) * scale) for part in parts]
        sums = [jnp.sum(part, axis=0, keepdims=True) for part in parts]
        inverse = 1.0 / (sums[0] if column == 0 else sums[0] + sums[1])
        parts = [part * inverse for part in parts]
        grads = [grad_probs[:block, columns], grad_probs[block:, columns]][: column + 1]
        means = [jnp.sum(g * p, axis=0, keepdims=True) for g, p in zip(grads, parts)]
        mean = means[0] if column == 0 else means[0] + means[1]
        grads = [(p * (g - mean) * scale).astype(jnp.bfloat16) for g, p in zip(grads, parts)]
        parts = [p.astype(jnp.bfloat16) for p in parts]
        if column == 0:
            parts.append(jnp.zeros((block, block), jnp.bfloat16))
            grads.append(jnp.zeros((block, block), jnp.bfloat16))
        probs_columns.append(jnp.concatenate(parts, axis=0))
        grads_columns.append(jnp.concatenate(grads, axis=0))
    return jnp.concatenate(probs_columns, axis=1), jnp.concatenate(grads_columns, axis=1)


def backward(length, xq, xkv, grad, weights, table, gq, gkv, qw, kw, vw, rot_out, ready):
    wq, wk, wv = weights
    n_seq = xq.shape[0] // length
    wide = wk.shape[1]
    heads = wide // DN
    low = lax.broadcasted_iota(jnp.int32, (length, TILE), 1) < DR
    spans = [slice(s * length, (s + 1) * length) for s in range(n_seq)]

    ready[0]()
    cos_low, sin_low = table[:, :TILE], table[:, TILE:]
    cos_tiles = (cos_low, pltpu.roll(cos_low, DR, 1))
    sin_tiles = (sin_low, pltpu.roll(sin_low, DR, 1))
    latent = xkv[:, :KL]
    for pair in range(heads // 2):
        columns = slice(2 * DN * pair, 2 * DN * (pair + 1))
        keys = dot(latent, wk[:, columns])
        vw[:, columns] = dot(latent, wv[:, columns]).astype(jnp.bfloat16)
        for span in spans:
            rot = jnp.concatenate(
                [xkv[span, KL : KL + DR].astype(jnp.float32), jnp.zeros((length, DR), jnp.float32)],
                axis=1,
            )
            odd = pltpu.roll(keys[span, DN:], DR, 1)
            tiles = (
                keys[span, :DN],
                rot,
                jnp.where(low, 0.0, odd),
                jnp.where(low, odd, pltpu.roll(rot, DR, 1)),
            )
            for i, tile in enumerate(tiles):
                start = (4 * pair + i) * TILE
                kw[span, start : start + TILE] = tile.astype(jnp.bfloat16)
    ready[1]()
    for pair in range(heads // 2):
        queries = dot(xq[...], wq[:, PAIR * pair : PAIR * (pair + 1)])
        for span in spans:
            for i in range(3):
                part = rounded(queries[span, i * TILE : (i + 1) * TILE])
                if i > 0:
                    part = part * cos_tiles[i - 1] + swap_halves(part) * sin_tiles[i - 1]
                start = PAIR * pair + i * TILE
                qw[span, start : start + TILE] = part.astype(jnp.bfloat16)

    items = [(span, head) for span in spans for head in range(heads)]

    def windows(span, head):
        start = PAIR * (head // 2) + TILE * (head % 2)
        return (
            qw[span, start : start + 2 * TILE],
            kw[span, 2 * TILE * head : 2 * TILE * (head + 1)],
            slice(head * DN, (head + 1) * DN),
        )

    def first_products(span, head):
        query_window, key_window, columns = windows(span, head)
        return (
            dot(key_window, query_window, NT),
            dot(vw[span, columns], grad[span, columns], NT),
        )

    rot_sums = [jnp.zeros((length, TILE), jnp.float32) for _ in spans]
    pending = first_products(*items[0])
    even_part = None
    for index, (span, head) in enumerate(items):
        products = pending
        if index + 1 < len(items):
            pending = first_products(*items[index + 1])
        probs, grad_scores = softmax_grads(*products)
        query_window, key_window, columns = windows(span, head)
        gkv[span, wide + head * DN : wide + (head + 1) * DN] = dot(probs, grad[span, columns]).astype(
            jnp.bfloat16
        )
        key_part = dot(grad_scores, query_window)
        query_part = dot(grad_scores, key_window, TN)
        seq = index // heads
        if head % 2 == 0:
            gkv[span, columns] = key_part[:, :TILE].astype(jnp.bfloat16)
            if rot_out is not None:
                rot_sums[seq] = rot_sums[seq] + rounded(key_part[:, TILE:])
            even_part = query_part
            continue
        turned = pltpu.roll(key_part[:, TILE:], DR, 1)
        gkv[span, columns] = jnp.where(low, pltpu.roll(key_part[:, :TILE], DR, 1), turned).astype(
            jnp.bfloat16
        )
        if rot_out is not None:
            rot_sums[seq] = rot_sums[seq] + rounded(turned)
        parts = [
            even_part[:, :TILE],
            even_part[:, TILE:] + query_part[:, :TILE],
            query_part[:, TILE:],
        ]
        for i in range(3):
            part = parts[i]
            if i > 0:
                part = rounded(part)
                part = part * cos_tiles[i - 1] - swap_halves(part) * sin_tiles[i - 1]
            start = PAIR * (head // 2) + i * TILE
            gq[span, start : start + TILE] = part.astype(jnp.bfloat16)
    if rot_out is not None:
        rot_out[...] = rot_sums[0]


def raw_grads(xq, xkv, gq, gkv, previous, emit):
    wide = gkv.shape[1] // 2
    step = KL
    for block in range(QL // step + 1):
        if block < QL // step:
            rows = slice(block * step, (block + 1) * step)
            targets = ((0, rows, dot(xq[:, rows], gq[...], TN)),)
        else:
            rows = slice(0, KL)
            product = dot(xkv[:, :KL], gkv[...], TN)
            targets = ((1, rows, product[:, :wide]), (2, rows, product[:, wide:]))
        for which, rows, product in targets:
            if previous is not None:
                product = product + previous[which][rows, :]
            emit(which, rows, product)


def load_kernel(place, xq, kvt, grad, packed, kv_rows, sem):
    half, wide = packed.shape[0], grad.shape[1]
    width = QL + KL + TILE
    rows = pl.ds(pl.multiple_of(place[1] * half, half), half)
    pieces = (
        (kvt.at[:, rows], kv_rows),
        (xq.at[rows], packed.at[:, :QL]),
        (grad.at[:half], packed.at[:, width : width + wide]),
        (grad.at[half:], packed.at[:, width + wide :]),
    )
    copies = [pltpu.make_async_copy(*piece, sem.at[i]) for i, piece in enumerate(pieces)]
    for copy in copies:
        copy.start()
    copies[0].wait()
    for block in range(0, KL + DR, TILE):
        stop = min(block + TILE, KL + DR)
        packed[:, QL + block : QL + stop] = kv_rows[block:stop, :].T
    packed[:, LATENT:width] = jnp.zeros((half, TILE - DR), jnp.bfloat16)
    for copy in copies[1:]:
        copy.wait()


def own_kernel(n_head, place, xq_in, kvt_in, grad_in, wq_in, wk_in, wv_in, table_in, *refs):
    wq, wk, wv, table, xq, xkv, gq, gkv, keep, send_stay, send_go, *refs = refs
    kvt, grad, qw, kw, vw, term, sem = refs
    pieces = (
        (kvt_in, kvt),
        (table_in, table),
        (wk_in, wk),
        (wv_in, wv),
        (xq_in, xq),
        (wq_in, wq),
        (grad_in, grad),
    )
    copies = [pltpu.make_async_copy(*piece, sem.at[i]) for i, piece in enumerate(pieces)]
    for copy in copies:
        copy.start()

    def latents_ready():
        for copy in copies[:4]:
            copy.wait()
        for block in range(0, KL + DR, TILE):
            stop = min(block + TILE, KL + DR)
            xkv[:, block:stop] = kvt[block:stop, :].T

    def queries_ready():
        for copy in copies[4:]:
            copy.wait()

    length = xq.shape[0]
    rot = term.at[:, QL + KL :]
    ready = (latents_ready, queries_ready)
    backward(length, xq, xkv, grad, (wq, wk, wv), table, gq, gkv, qw, kw, vw, rot, ready)
    wide = wk.shape[1]
    term[:, :QL] = dot(gq[...], wq[...], NT)
    term[:, QL : QL + KL] = dot(gkv[:, :wide], wk[...], NT) + dot(gkv[:, wide:], wv[...], NT)
    rows = length // n_head
    chip, core = place[0], place[1]
    masks = [turned_round(k, n_head // 2) for k in range(n_head // 2)]

    def chosen(which):
        starts = [(2 * jnp.bitwise_xor(chip, mask) + which) * rows for mask in masks]
        return jnp.concatenate([term[pl.ds(pl.multiple_of(i, rows), rows), :] for i in starts])

    keep[...] = chosen(core)
    send = chosen(1 - core).astype(jnp.bfloat16)
    send_stay[...] = send[: send_stay.shape[0], :]
    send_go[...] = send[send_stay.shape[0] :, :]


def fold_kernel(keep, *refs):
    received, (stay, go) = refs[:-2], refs[-2:]
    total = jnp.concatenate([part[...] for part in received]).astype(jnp.float32) + keep[...]
    stay[...] = total[: stay.shape[0], :]
    go[...] = total[stay.shape[0] :, :].astype(jnp.bfloat16)


def far_kernel(n_seq, place, *refs):
    blocks, refs = refs[: 2 * n_seq], refs[2 * n_seq :]
    wq, wk, wv, table, xq, xkv, gq, gkv, grad, qw, kw, vw = refs
    half, wide = blocks[0].shape[0], grad.shape[1]
    length = 2 * half
    width = QL + KL + TILE
    core = place[1]
    for s in range(n_seq):
        mine, other = blocks[2 * s : 2 * s + 2]
        for source, side in ((mine, core), (other, 1 - core)):
            rows = pl.ds(pl.multiple_of(s * length + side * half, half), half)
            xq[rows, :] = source[:, :QL]
            xkv[rows, :] = source[:, QL:LATENT]
        start = s * length
        grad[start : start + half, :] = mine[:, width : width + wide]
        grad[start + half : start + length, :] = mine[:, width + wide :]
    ready = (lambda: None, lambda: None)
    backward(length, xq, xkv, grad, (wq, wk, wv), table, gq, gkv, qw, kw, vw, None, ready)


def sums_kernel(first, with_squares, xq, xkv, gq, gkv, *refs):
    previous, refs = (None, refs) if first else (refs[:3], refs[3:])
    taken = None
    if with_squares and not first:
        taken, *refs = refs
    sums = refs[:3]
    totals = [jnp.zeros((8, TILE), jnp.float32)]

    def emit(which, rows, block):
        sums[which][rows, :] = block
        if not with_squares:
            return
        folded = jnp.zeros((8, block.shape[1]), jnp.float32)
        for start in range(rows.start, rows.stop, 64):
            part = sums[which][start : start + 64, :]
            folded = folded + jnp.sum((part * part).reshape(8, 8, part.shape[1]), axis=0)
        for column in range(0, block.shape[1], TILE):
            totals[0] = totals[0] + folded[:, column : column + TILE]

    raw_grads(xq, xkv, gq, gkv, previous, emit)
    if with_squares:
        refs[3][...] = totals[0] if first else totals[0] - taken[...]


def add_kernel(*refs):
    total = refs[0][...]
    for ref in refs[1:-1]:
        total = total + ref[...]
    refs[-1][...] = total


def final_kernel(limit, n_parts, share, xq, xkv, gq, gkv, *refs):
    previous, (local, received), refs = refs[:3], refs[3:5], refs[5:]
    parts, refs = refs[:n_parts], refs[n_parts:]
    outs, (latent_q, latent_kv), buffers, sem = refs[:3], refs[3:5], refs[5:8], refs[8]
    total = parts[0][...]
    for part in parts[1:]:
        total = total + part[...]
    total = jnp.maximum(jnp.sum(total, keepdims=True) * share, 0.0)
    factor = jnp.minimum(1.0, limit / jnp.sqrt(total + eps))
    copies = []

    def emit(which, rows, block):
        buffers[which][rows, :] = (block * factor).astype(jnp.bfloat16)
        copy = pltpu.make_async_copy(
            buffers[which].at[rows], outs[which].at[rows], sem.at[len(copies)]
        )
        copy.start()
        copies.append(copy)

    raw_grads(xq, xkv, gq, gkv, previous, emit)
    terms = local[...] + received[...].astype(jnp.float32)
    latent_q[...] = terms[:, :QL]
    latent_kv[...] = terms[:, QL:LATENT]
    for copy in copies:
        copy.wait()


def vmem(count):
    return [pl.BlockSpec(memory_space=pltpu.VMEM)] * count


def hbm(count):
    return [pl.BlockSpec(memory_space=pltpu.HBM)] * count


def params():
    return pltpu.CompilerParams(vmem_limit_bytes=VMEM_LIMIT)


def free():
    return pl.CostEstimate(flops=0, bytes_accessed=0, transcendentals=0)


def struct(shape, dtype):
    return jax.ShapeDtypeStruct(shape, dtype)


def exchange(value, axis, size, k):
    return lax.ppermute(value, axis, [(i, i ^ k) for i in range(size)])


def far_away(value):
    return pltpu.with_memory_space_constraint(value, pltpu.HBM)


def turned_round(mask, n_dp):
    bits = n_dp.bit_length() - 1
    return sum(((mask >> i) & 1) << (bits - 1 - i) for i in range(bits))


def across(value, n_dp, n_head, mask):
    masks = (mask, turned_round(mask, n_dp))
    pairs = [
        (d * n_head + h, (d ^ masks[h % 2]) * n_head + h) for d in range(n_dp) for h in range(n_head)
    ]
    return lax.ppermute(value, ("dp", "head"), pairs)


def per_device(n_dp, n_head, query_latent, kv_latent, out_grad, query_up, key_up, value_up):
    length = query_latent.shape[0]
    half = length // 2
    wide_q, wide_k = query_up.shape[1], key_up.shape[1]
    heads = wide_k // DN
    index = lax.axis_index("head")
    place = jnp.stack([index // 2, index % 2]).astype(jnp.int32)
    table = jnp.asarray(rotary_tables(length))
    smem = [pl.BlockSpec(memory_space=pltpu.SMEM)]
    inputs = [far_away(value) for value in (query_latent, kv_latent.T, out_grad)]
    width = QL + KL + TILE

    packed = pl.pallas_call(
        load_kernel,
        out_shape=pltpu.VMEM((half, width + 2 * wide_k), jnp.bfloat16),
        in_specs=smem + hbm(3),
        out_specs=pl.BlockSpec(memory_space=pltpu.VMEM),
        scratch_shapes=[pltpu.VMEM((KL + DR, half), jnp.bfloat16), pltpu.SemaphoreType.DMA((4,))],
        compiler_params=params(),
        cost_estimate=free(),
        name="load",
    )(place, *inputs)
    packed, place = lax.optimization_barrier((packed, place))
    singles = [1 << i for i in reversed(range(n_dp.bit_length() - 1))]
    received = {k: across(packed, n_dp, n_head, k) for k in singles}

    def rows_shape(rows):
        widths = (QL, KL + DR, wide_q, 2 * wide_k)
        return tuple(pltpu.VMEM((rows, width), jnp.bfloat16) for width in widths)

    def scratch(rows):
        widths = (wide_k, wide_q, 2 * TILE * heads, wide_k)
        return [pltpu.VMEM((rows, width), jnp.bfloat16) for width in widths]

    weights_shape = tuple(
        pltpu.VMEM(shape, jnp.bfloat16) for shape in ((QL, wide_q), (KL, wide_k), (KL, wide_k))
    )
    sums_shape = tuple(pltpu.VMEM(w.shape, jnp.float32) for w in weights_shape)
    *outs, keep, send_stay, send_go = pl.pallas_call(
        functools.partial(own_kernel, n_head),
        out_shape=(
            *weights_shape,
            pltpu.VMEM(table.shape, jnp.float32),
            *rows_shape(length),
            struct((half, width), jnp.float32),
            struct((half // 2, width), jnp.bfloat16),
            struct((half // 2, width), jnp.bfloat16),
        ),
        in_specs=smem + hbm(7),
        out_specs=vmem(11),
        scratch_shapes=[pltpu.VMEM((KL + DR, length), jnp.bfloat16)]
        + scratch(length)
        + [pltpu.VMEM((length, width), jnp.float32), pltpu.SemaphoreType.DMA((7,))],
        compiler_params=params(),
        cost_estimate=free(),
        name="own",
    )(place, *inputs, *[far_away(value) for value in (query_up, key_up, value_up, table)])
    weights, found = outs[:4], outs[4:]

    rows, n_chip = length // n_head, n_head // 2
    squares_shape = struct((8, TILE), jnp.float32)

    def add_sums(found, sums, with_squares, taken=()):
        extra_out = (squares_shape,) if with_squares else ()
        return list(
            pl.pallas_call(
                functools.partial(sums_kernel, not sums, with_squares),
                out_shape=(*sums_shape, *extra_out),
                in_specs=vmem(4 + len(sums) + len(taken)),
                out_specs=vmem(3 + len(extra_out)),
                input_output_aliases={4: 0, 5: 1, 6: 2} if sums else {},
                compiler_params=params(),
                cost_estimate=free(),
                name="sums",
            )(*found, *sums, *taken)
        )

    def add(*values):
        return pl.pallas_call(
            add_kernel,
            out_shape=squares_shape,
            in_specs=vmem(len(values)),
            out_specs=pl.BlockSpec(memory_space=pltpu.VMEM),
            compiler_params=params(),
            cost_estimate=free(),
            name="add",
        )(*values)

    *sums, own_squares = add_sums(found, [], True)

    def fold(keep, *received):
        half_shape = (keep.shape[0] // 2, width)
        return pl.pallas_call(
            fold_kernel,
            out_shape=(struct(half_shape, jnp.float32), struct(half_shape, jnp.bfloat16)),
            in_specs=vmem(1 + len(received)),
            out_specs=vmem(2),
            compiler_params=params(),
            cost_estimate=free(),
            name="fold",
        )(keep, *received)

    stay, go = fold(keep, *[exchange(send, "head", n_head, 1) for send in (send_stay, send_go)])
    bits = [2 << i for i in range(n_head.bit_length() - 2)]
    for bit in bits[:-2]:
        stay, go = fold(stay, exchange(go, "head", n_head, bit))
    came = exchange(go, "head", n_head, bits[-2])

    values = [received[k] for k in singles]
    *values, sums[2], came = lax.optimization_barrier((*values, sums[2], came))
    received = dict(zip(singles, values))
    for k in range(3, n_dp):
        if k not in received:
            received[k] = across(received[k & (k - 1)], n_dp, n_head, k & -k)
    stay, go = fold(stay, came)
    terms = [stay, exchange(go, "head", n_head, bits[-1])]

    def swapped(k):
        return exchange(received[turned_round(k, n_dp)], "head", n_head, 1)

    groups = [(1, 2)] + [(k,) for k in range(3, n_dp)]
    for index, group in enumerate(groups):
        n_seq = len(group)
        blocks = []
        for k in group:
            blocks += [received[k], swapped(k)]
        last = index == len(groups) - 1
        if last:
            blocks[1], *parts = lax.optimization_barrier((blocks[1], *parts))
            squares = add(*parts)
            parts = [squares] + [exchange(squares, "dp", n_dp, k) for k in range(1, n_dp)]
        found = list(
            pl.pallas_call(
                functools.partial(far_kernel, n_seq),
                out_shape=rows_shape(n_seq * length),
                in_specs=smem + vmem(len(blocks) + 4),
                out_specs=vmem(4),
                scratch_shapes=scratch(n_seq * length),
                compiler_params=params(),
                cost_estimate=free(),
                name="far",
            )(place, *blocks, *weights)
        )
        if last:
            break
        if index == 0:
            found[3], terms[1] = lax.optimization_barrier((found[3], terms[1]))
        if index < len(groups) - 2:
            sums = add_sums(found, sums, False)
        else:
            *sums, squares = add_sums(found, sums, True, [own_squares])
            squares = add(squares, exchange(squares, "head", n_head, 1))
            parts = [squares] + [exchange(squares, "head", n_head, 2 * k) for k in range(1, n_chip)]
        k = groups[index + 1][0]
        received[k], sums[2] = lax.optimization_barrier((received[k], sums[2]))

    count = (QL * wide_q + 2 * KL * wide_k) * n_head
    limit = max_rms * count**0.5
    *scaled, latent_q, latent_kv = pl.pallas_call(
        functools.partial(final_kernel, limit, len(parts), 1.0 / (n_dp - 2)),
        out_shape=(
            *[struct(w.shape, jnp.bfloat16) for w in weights_shape],
            struct((rows, QL), jnp.float32),
            struct((rows, KL + DR), jnp.float32),
        ),
        in_specs=vmem(4 + 3 + 2 + len(parts)),
        out_specs=hbm(3) + vmem(2),
        scratch_shapes=list(weights_shape) + [pltpu.SemaphoreType.DMA((QL // KL + 2,))],
        compiler_params=params(),
        cost_estimate=free(),
        name="final",
    )(*found, *sums, *terms, *parts)
    return (latent_q, latent_kv, *scaled)


def solution(mesh):
    placed = (
        P("dp", None),
        P("dp", None),
        P("dp", "head"),
        P(None, "head"),
        P(None, "head"),
        P(None, "head"),
    )
    return jax.shard_map(
        functools.partial(per_device, mesh.shape["dp"], mesh.shape["head"]),
        mesh=mesh,
        in_specs=placed,
        out_specs=(
            P(("dp", "head"), None),
            P(("dp", "head"), None),
            P(None, "head"),
            P(None, "head"),
            P(None, "head"),
        ),
        check_vma=False,
    )
```

```python
import functools

import jax
import jax.numpy as jnp
import numpy as np
from jax import lax
from jax.experimental import pallas as pl
from jax.experimental.pallas import tpu as pltpu
from jax.sharding import PartitionSpec as P

QL = 1536
KL = 512
DN = 128
DR = 64
TILE = 128
WIDTH = DN + DR
PAIR = 2 * WIDTH
LATENT = QL + KL + DR

max_rms = 1.0
eps = 1e-06
VMEM_LIMIT = 32 * 2**20

NT = (((1,), (1,)), ((), ()))
TN = (((0,), (0,)), ((), ()))


def dot(left, right, dims=(((1,), (0,)), ((), ()))):
    return lax.dot_general(left, right, dims, preferred_element_type=jnp.float32)


def rotary_tables(length):
    half = DR // 2
    freqs = np.float32(10000.0) ** (
        np.float32(-2.0) * np.arange(half, dtype=np.float32) / np.float32(DR)
    )
    angle = np.arange(length, dtype=np.float32)[:, None] * freqs.astype(np.float32)[None, :]
    cosine, sine = np.cos(angle), np.sin(angle)
    ones, zeros = np.ones((length, DR), np.float32), np.zeros((length, DR), np.float32)
    return np.concatenate([cosine, cosine, ones, -sine, sine, zeros], axis=1)


def swap_halves(tile):
    lane = lax.broadcasted_iota(jnp.int32, tile.shape, 1)
    first = lane % DR < DR // 2
    return jnp.where(
        first, pltpu.roll(tile, TILE - DR // 2, 1), pltpu.roll(tile, DR // 2, 1)
    )


def rounded(values):
    return values.astype(jnp.bfloat16).astype(jnp.float32)


def softmax_grads(scores, grad_probs):
    length = scores.shape[0]
    block = length // 2
    scale = 1.0 / (DN + DR) ** 0.5
    key = lax.broadcasted_iota(jnp.int32, (block, block), 0)
    query = lax.broadcasted_iota(jnp.int32, (block, block), 1)
    allowed = key <= query
    grad_probs = rounded(grad_probs)
    probs_columns, grads_columns = [], []
    for column in range(2):
        columns = slice(column * block, (column + 1) * block)
        parts = [scores[:block, columns], scores[block:, columns]][: column + 1]
        parts[-1] = jnp.where(allowed, parts[-1], -jnp.inf)
        tops = [jnp.max(part, axis=0, keepdims=True) for part in parts]
        top = tops[0] if column == 0 else jnp.maximum(*tops)
        parts = [jnp.exp((part - top) * scale) for part in parts]
        sums = [jnp.sum(part, axis=0, keepdims=True) for part in parts]
        inverse = 1.0 / (sums[0] if column == 0 else sums[0] + sums[1])
        parts = [part * inverse for part in parts]
        grads = [grad_probs[:block, columns], grad_probs[block:, columns]][: column + 1]
        means = [jnp.sum(g * p, axis=0, keepdims=True) for g, p in zip(grads, parts)]
        mean = means[0] if column == 0 else means[0] + means[1]
        grads = [(p * (g - mean) * scale).astype(jnp.bfloat16) for g, p in zip(grads, parts)]
        parts = [p.astype(jnp.bfloat16) for p in parts]
        if column == 0:
            parts.append(jnp.zeros((block, block), jnp.bfloat16))
            grads.append(jnp.zeros((block, block), jnp.bfloat16))
        probs_columns.append(jnp.concatenate(parts, axis=0))
        grads_columns.append(jnp.concatenate(grads, axis=0))
    return jnp.concatenate(probs_columns, axis=1), jnp.concatenate(grads_columns, axis=1)


def backward(length, xq, xkv, grad, weights, table, gq, gkv, qw, kw, vw, rot_out, ready):
    wq, wk, wv = weights
    n_seq = xq.shape[0] // length
    wide = wk.shape[1]
    heads = wide // DN
    low = lax.broadcasted_iota(jnp.int32, (length, TILE), 1) < DR
    spans = [slice(s * length, (s + 1) * length) for s in range(n_seq)]

    ready[0]()
    cos_low, sin_low = table[:, :TILE], table[:, TILE:]
    cos_tiles = (cos_low, pltpu.roll(cos_low, DR, 1))
    sin_tiles = (sin_low, pltpu.roll(sin_low, DR, 1))
    latent = xkv[:, :KL]
    for pair in range(heads // 2):
        columns = slice(2 * DN * pair, 2 * DN * (pair + 1))
        keys = dot(latent, wk[:, columns])
        vw[:, columns] = dot(latent, wv[:, columns]).astype(jnp.bfloat16)
        for span in spans:
            rot = jnp.concatenate(
                [xkv[span, KL : KL + DR].astype(jnp.float32), jnp.zeros((length, DR), jnp.float32)],
                axis=1,
            )
            odd = pltpu.roll(keys[span, DN:], DR, 1)
            tiles = (
                keys[span, :DN],
                rot,
                jnp.where(low, 0.0, odd),
                jnp.where(low, odd, pltpu.roll(rot, DR, 1)),
            )
            for i, tile in enumerate(tiles):
                start = (4 * pair + i) * TILE
                kw[span, start : start + TILE] = tile.astype(jnp.bfloat16)
    ready[1]()
    for pair in range(heads // 2):
        queries = dot(xq[...], wq[:, PAIR * pair : PAIR * (pair + 1)])
        for span in spans:
            for i in range(3):
                part = rounded(queries[span, i * TILE : (i + 1) * TILE])
                if i > 0:
                    part = part * cos_tiles[i - 1] + swap_halves(part) * sin_tiles[i - 1]
                start = PAIR * pair + i * TILE
                qw[span, start : start + TILE] = part.astype(jnp.bfloat16)

    items = [(span, head) for span in spans for head in range(heads)]

    def windows(span, head):
        start = PAIR * (head // 2) + TILE * (head % 2)
        return (
            qw[span, start : start + 2 * TILE],
            kw[span, 2 * TILE * head : 2 * TILE * (head + 1)],
            slice(head * DN, (head + 1) * DN),
        )

    def first_products(span, head):
        query_window, key_window, columns = windows(span, head)
        return (
            dot(key_window, query_window, NT),
            dot(vw[span, columns], grad[span, columns], NT),
        )

    rot_sums = [jnp.zeros((length, TILE), jnp.float32) for _ in spans]
    pending = first_products(*items[0])
    even_part = None
    for index, (span, head) in enumerate(items):
        products = pending
        if index + 1 < len(items):
            pending = first_products(*items[index + 1])
        probs, grad_scores = softmax_grads(*products)
        query_window, key_window, columns = windows(span, head)
        gkv[span, wide + head * DN : wide + (head + 1) * DN] = dot(probs, grad[span, columns]).astype(
            jnp.bfloat16
        )
        key_part = dot(grad_scores, query_window)
        query_part = dot(grad_scores, key_window, TN)
        seq = index // heads
        if head % 2 == 0:
            gkv[span, columns] = key_part[:, :TILE].astype(jnp.bfloat16)
            if rot_out is not None:
                rot_sums[seq] = rot_sums[seq] + rounded(key_part[:, TILE:])
            even_part = query_part
            continue
        turned = pltpu.roll(key_part[:, TILE:], DR, 1)
        gkv[span, columns] = jnp.where(low, pltpu.roll(key_part[:, :TILE], DR, 1), turned).astype(
            jnp.bfloat16
        )
        if rot_out is not None:
            rot_sums[seq] = rot_sums[seq] + rounded(turned)
        parts = [
            even_part[:, :TILE],
            even_part[:, TILE:] + query_part[:, :TILE],
            query_part[:, TILE:],
        ]
        for i in range(3):
            part = parts[i]
            if i > 0:
                part = rounded(part)
                part = part * cos_tiles[i - 1] - swap_halves(part) * sin_tiles[i - 1]
            start = PAIR * (head // 2) + i * TILE
            gq[span, start : start + TILE] = part.astype(jnp.bfloat16)
    if rot_out is not None:
        rot_out[...] = rot_sums[0]


def raw_grads(xq, xkv, gq, gkv, previous, emit):
    wide = gkv.shape[1] // 2
    step = KL
    for block in range(QL // step + 1):
        if block < QL // step:
            rows = slice(block * step, (block + 1) * step)
            targets = ((0, rows, dot(xq[:, rows], gq[...], TN)),)
        else:
            rows = slice(0, KL)
            product = dot(xkv[:, :KL], gkv[...], TN)
            targets = ((1, rows, product[:, :wide]), (2, rows, product[:, wide:]))
        for which, rows, product in targets:
            if previous is not None:
                product = product + previous[which][rows, :]
            emit(which, rows, product)


def load_kernel(place, xq, kvt, grad, packed, kv_rows, sem):
    half, wide = packed.shape[0], grad.shape[1]
    width = QL + KL + TILE
    rows = pl.ds(pl.multiple_of(place[1] * half, half), half)
    pieces = (
        (kvt.at[:, rows], kv_rows),
        (xq.at[rows], packed.at[:, :QL]),
        (grad.at[:half], packed.at[:, width : width + wide]),
        (grad.at[half:], packed.at[:, width + wide :]),
    )
    copies = [pltpu.make_async_copy(*piece, sem.at[i]) for i, piece in enumerate(pieces)]
    for copy in copies:
        copy.start()
    copies[0].wait()
    for block in range(0, KL + DR, TILE):
        stop = min(block + TILE, KL + DR)
        packed[:, QL + block : QL + stop] = kv_rows[block:stop, :].T
    packed[:, LATENT:width] = jnp.zeros((half, TILE - DR), jnp.bfloat16)
    for copy in copies[1:]:
        copy.wait()


def own_kernel(n_head, place, xq_in, kvt_in, grad_in, wq_in, wk_in, wv_in, table_in, *refs):
    wq, wk, wv, table, xq, xkv, gq, gkv, keep, send_stay, send_go, *refs = refs
    kvt, grad, qw, kw, vw, term, sem = refs
    pieces = (
        (kvt_in, kvt),
        (table_in, table),
        (wk_in, wk),
        (wv_in, wv),
        (xq_in, xq),
        (wq_in, wq),
        (grad_in, grad),
    )
    copies = [pltpu.make_async_copy(*piece, sem.at[i]) for i, piece in enumerate(pieces)]
    for copy in copies:
        copy.start()

    def latents_ready():
        for copy in copies[:4]:
            copy.wait()
        for block in range(0, KL + DR, TILE):
            stop = min(block + TILE, KL + DR)
            xkv[:, block:stop] = kvt[block:stop, :].T

    def queries_ready():
        for copy in copies[4:]:
            copy.wait()

    length = xq.shape[0]
    rot = term.at[:, QL + KL :]
    ready = (latents_ready, queries_ready)
    backward(length, xq, xkv, grad, (wq, wk, wv), table, gq, gkv, qw, kw, vw, rot, ready)
    wide = wk.shape[1]
    term[:, :QL] = dot(gq[...], wq[...], NT)
    term[:, QL : QL + KL] = dot(gkv[:, :wide], wk[...], NT) + dot(gkv[:, wide:], wv[...], NT)
    rows = length // n_head
    chip, core = place[0], place[1]
    masks = [turned_round(k, n_head // 2) for k in range(n_head // 2)]

    def chosen(which):
        starts = [(2 * jnp.bitwise_xor(chip, mask) + which) * rows for mask in masks]
        return jnp.concatenate([term[pl.ds(pl.multiple_of(i, rows), rows), :] for i in starts])

    keep[...] = chosen(core)
    send = chosen(1 - core).astype(jnp.bfloat16)
    send_stay[...] = send[: send_stay.shape[0], :]
    send_go[...] = send[send_stay.shape[0] :, :]


def fold_kernel(keep, *refs):
    received, (stay, go) = refs[:-2], refs[-2:]
    total = jnp.concatenate([part[...] for part in received]).astype(jnp.float32) + keep[...]
    stay[...] = total[: stay.shape[0], :]
    go[...] = total[stay.shape[0] :, :].astype(jnp.bfloat16)


def far_kernel(n_seq, place, *refs):
    blocks, refs = refs[: 2 * n_seq], refs[2 * n_seq :]
    wq, wk, wv, table, xq, xkv, gq, gkv, grad, qw, kw, vw = refs
    half, wide = blocks[0].shape[0], grad.shape[1]
    length = 2 * half
    width = QL + KL + TILE
    core = place[1]
    for s in range(n_seq):
        mine, other = blocks[2 * s : 2 * s + 2]
        for source, side in ((mine, core), (other, 1 - core)):
            rows = pl.ds(pl.multiple_of(s * length + side * half, half), half)
            xq[rows, :] = source[:, :QL]
            xkv[rows, :] = source[:, QL:LATENT]
        start = s * length
        grad[start : start + half, :] = mine[:, width : width + wide]
        grad[start + half : start + length, :] = mine[:, width + wide :]
    ready = (lambda: None, lambda: None)
    backward(length, xq, xkv, grad, (wq, wk, wv), table, gq, gkv, qw, kw, vw, None, ready)


def sums_kernel(first, with_squares, xq, xkv, gq, gkv, *refs):
    previous, refs = (None, refs) if first else (refs[:3], refs[3:])
    taken = None
    if with_squares and not first:
        taken, *refs = refs
    sums = refs[:3]
    totals = [jnp.zeros((8, TILE), jnp.float32)]

    def emit(which, rows, block):
        sums[which][rows, :] = block
        if not with_squares:
            return
        folded = jnp.zeros((8, block.shape[1]), jnp.float32)
        for start in range(rows.start, rows.stop, 64):
            part = sums[which][start : start + 64, :]
            folded = folded + jnp.sum((part * part).reshape(8, 8, part.shape[1]), axis=0)
        for column in range(0, block.shape[1], TILE):
            totals[0] = totals[0] + folded[:, column : column + TILE]

    raw_grads(xq, xkv, gq, gkv, previous, emit)
    if with_squares:
        refs[3][...] = totals[0] if first else totals[0] - taken[...]


def add_kernel(*refs):
    total = refs[0][...]
    for ref in refs[1:-1]:
        total = total + ref[...]
    refs[-1][...] = total


def last_kernel(xq, xkv, gq, gkv, pq, pk, pv, sq, sk, sv):
    sums = (sq, sk, sv)

    def emit(which, rows, block):
        sums[which][rows, :] = block

    raw_grads(xq, xkv, gq, gkv, (pq, pk, pv), emit)


def scale_kernel(limit, share, left, right, sq, sk, sv, local, received, *refs):
    oq, ok, ov, latent_q, latent_kv, bq, bk, bv, sem = refs
    total = jnp.sum(left[...] + right[...], keepdims=True)
    total = jnp.maximum(total * share, 0.0)
    factor = jnp.minimum(1.0, limit / jnp.sqrt(total + eps))
    copies = []
    for source, buffer, out in ((sq, bq, oq), (sk, bk, ok), (sv, bv, ov)):
        for start in range(0, source.shape[0], 256):
            rows = slice(start, start + 256)
            buffer[rows, :] = (source[rows, :] * factor).astype(jnp.bfloat16)
            copy = pltpu.make_async_copy(buffer.at[rows], out.at[rows], sem.at[len(copies)])
            copy.start()
            copies.append(copy)
    terms = local[...] + received[...].astype(jnp.float32)
    latent_q[...] = terms[:, :QL]
    latent_kv[...] = terms[:, QL:LATENT]
    for copy in copies:
        copy.wait()


def vmem(count):
    return [pl.BlockSpec(memory_space=pltpu.VMEM)] * count


def hbm(count):
    return [pl.BlockSpec(memory_space=pltpu.HBM)] * count


def params():
    return pltpu.CompilerParams(vmem_limit_bytes=VMEM_LIMIT)


def free():
    return pl.CostEstimate(flops=0, bytes_accessed=0, transcendentals=0)


def struct(shape, dtype):
    return jax.ShapeDtypeStruct(shape, dtype)


def exchange(value, axis, size, k):
    return lax.ppermute(value, axis, [(i, i ^ k) for i in range(size)])


def far_away(value):
    return pltpu.with_memory_space_constraint(value, pltpu.HBM)


def turned_round(mask, n_dp):
    bits = n_dp.bit_length() - 1
    return sum(((mask >> i) & 1) << (bits - 1 - i) for i in range(bits))


def across(value, n_dp, n_head, mask):
    masks = (mask, turned_round(mask, n_dp))
    pairs = [
        (d * n_head + h, (d ^ masks[h % 2]) * n_head + h) for d in range(n_dp) for h in range(n_head)
    ]
    return lax.ppermute(value, ("dp", "head"), pairs)


def per_device(n_dp, n_head, query_latent, kv_latent, out_grad, query_up, key_up, value_up):
    length = query_latent.shape[0]
    half = length // 2
    wide_q, wide_k = query_up.shape[1], key_up.shape[1]
    heads = wide_k // DN
    index = lax.axis_index("head")
    place = jnp.stack([index // 2, index % 2]).astype(jnp.int32)
    table = jnp.asarray(rotary_tables(length))
    smem = [pl.BlockSpec(memory_space=pltpu.SMEM)]
    inputs = [far_away(value) for value in (query_latent, kv_latent.T, out_grad)]
    width = QL + KL + TILE

    packed = pl.pallas_call(
        load_kernel,
        out_shape=pltpu.VMEM((half, width + 2 * wide_k), jnp.bfloat16),
        in_specs=smem + hbm(3),
        out_specs=pl.BlockSpec(memory_space=pltpu.VMEM),
        scratch_shapes=[pltpu.VMEM((KL + DR, half), jnp.bfloat16), pltpu.SemaphoreType.DMA((4,))],
        compiler_params=params(),
        cost_estimate=free(),
        name="load",
    )(place, *inputs)
    packed, place = lax.optimization_barrier((packed, place))
    singles = [1 << i for i in reversed(range(n_dp.bit_length() - 1))]
    received = {k: across(packed, n_dp, n_head, k) for k in singles}

    def rows_shape(rows):
        widths = (QL, KL + DR, wide_q, 2 * wide_k)
        return tuple(pltpu.VMEM((rows, width), jnp.bfloat16) for width in widths)

    def scratch(rows):
        widths = (wide_k, wide_q, 2 * TILE * heads, wide_k)
        return [pltpu.VMEM((rows, width), jnp.bfloat16) for width in widths]

    weights_shape = tuple(
        pltpu.VMEM(shape, jnp.bfloat16) for shape in ((QL, wide_q), (KL, wide_k), (KL, wide_k))
    )
    sums_shape = tuple(pltpu.VMEM(w.shape, jnp.float32) for w in weights_shape)
    *outs, keep, send_stay, send_go = pl.pallas_call(
        functools.partial(own_kernel, n_head),
        out_shape=(
            *weights_shape,
            pltpu.VMEM(table.shape, jnp.float32),
            *rows_shape(length),
            struct((half, width), jnp.float32),
            struct((half // 2, width), jnp.bfloat16),
            struct((half // 2, width), jnp.bfloat16),
        ),
        in_specs=smem + hbm(7),
        out_specs=vmem(11),
        scratch_shapes=[pltpu.VMEM((KL + DR, length), jnp.bfloat16)]
        + scratch(length)
        + [pltpu.VMEM((length, width), jnp.float32), pltpu.SemaphoreType.DMA((7,))],
        compiler_params=params(),
        cost_estimate=free(),
        name="own",
    )(place, *inputs, *[far_away(value) for value in (query_up, key_up, value_up, table)])
    weights, found = outs[:4], outs[4:]

    rows, n_chip = length // n_head, n_head // 2
    squares_shape = struct((8, TILE), jnp.float32)

    def add_sums(found, sums, with_squares, taken=()):
        extra_out = (squares_shape,) if with_squares else ()
        return list(
            pl.pallas_call(
                functools.partial(sums_kernel, not sums, with_squares),
                out_shape=(*sums_shape, *extra_out),
                in_specs=vmem(4 + len(sums) + len(taken)),
                out_specs=vmem(3 + len(extra_out)),
                input_output_aliases={4: 0, 5: 1, 6: 2} if sums else {},
                compiler_params=params(),
                cost_estimate=free(),
                name="sums",
            )(*found, *sums, *taken)
        )

    def add(*values):
        return pl.pallas_call(
            add_kernel,
            out_shape=squares_shape,
            in_specs=vmem(len(values)),
            out_specs=pl.BlockSpec(memory_space=pltpu.VMEM),
            compiler_params=params(),
            cost_estimate=free(),
            name="add",
        )(*values)

    *sums, own_squares = add_sums(found, [], True)

    def fold(keep, *received):
        half_shape = (keep.shape[0] // 2, width)
        return pl.pallas_call(
            fold_kernel,
            out_shape=(struct(half_shape, jnp.float32), struct(half_shape, jnp.bfloat16)),
            in_specs=vmem(1 + len(received)),
            out_specs=vmem(2),
            compiler_params=params(),
            cost_estimate=free(),
            name="fold",
        )(keep, *received)

    stay, go = fold(keep, *[exchange(send, "head", n_head, 1) for send in (send_stay, send_go)])
    bits = [2 << i for i in range(n_head.bit_length() - 2)]
    for bit in bits[:-2]:
        stay, go = fold(stay, exchange(go, "head", n_head, bit))
    came = exchange(go, "head", n_head, bits[-2])

    values = [received[k] for k in singles]
    *values, sums[2], came = lax.optimization_barrier((*values, sums[2], came))
    received = dict(zip(singles, values))
    for k in range(3, n_dp):
        if k not in received:
            received[k] = across(received[k & (k - 1)], n_dp, n_head, k & -k)
    def swapped(k):
        return exchange(received[turned_round(k, n_dp)], "head", n_head, 1)

    def hop(squares, axis, size, mask):
        return add(squares, exchange(squares, axis, size, mask))

    groups = [(1, 2)] + [(k,) for k in range(3, n_dp)]
    for index, group in enumerate(groups):
        n_seq = len(group)
        blocks = []
        for k in group:
            blocks += [received[k], swapped(k)]
        last = index == len(groups) - 1
        if last:
            blocks[1], squares = lax.optimization_barrier((blocks[1], squares))
            came = exchange(squares, "head", n_head, bits[-1])
        found = list(
            pl.pallas_call(
                functools.partial(far_kernel, n_seq),
                out_shape=rows_shape(n_seq * length),
                in_specs=smem + vmem(len(blocks) + 4),
                out_specs=vmem(4),
                scratch_shapes=scratch(n_seq * length),
                compiler_params=params(),
                cost_estimate=free(),
                name="far",
            )(place, *blocks, *weights)
        )
        if last:
            break
        if index == 0:
            came, found[3] = lax.optimization_barrier((came, found[3]))
            stay, go = fold(stay, came)
            terms = [stay, exchange(go, "head", n_head, bits[-1])]
        if index < len(groups) - 2:
            sums = add_sums(found, sums, False)
        else:
            *sums, squares = add_sums(found, sums, True, [own_squares])
            squares = hop(squares, "head", n_head, 1)
        k = groups[index + 1][0]
        received[k], sums[2] = lax.optimization_barrier((received[k], sums[2]))

    came, found[3] = lax.optimization_barrier((came, found[3]))
    squares = add(squares, came)
    for bit in bits[1:-1]:
        squares = hop(squares, "head", n_head, bit)
    came = exchange(squares, "head", n_head, bits[0])
    sums = pl.pallas_call(
        last_kernel,
        out_shape=sums_shape,
        in_specs=vmem(4 + 3),
        out_specs=vmem(3),
        input_output_aliases={4: 0, 5: 1, 6: 2},
        compiler_params=params(),
        cost_estimate=free(),
        name="last",
    )(*found, *sums)
    came, terms[1], *sums = lax.optimization_barrier((came, terms[1], *sums))
    squares = add(squares, came)
    for k in singles[:-1]:
        squares = hop(squares, "dp", n_dp, k)

    count = (QL * wide_q + 2 * KL * wide_k) * n_head
    limit = max_rms * count**0.5
    *scaled, latent_q, latent_kv = pl.pallas_call(
        functools.partial(scale_kernel, limit, 1.0 / (n_dp - 2)),
        out_shape=(
            *[struct(w.shape, jnp.bfloat16) for w in weights_shape],
            struct((rows, QL), jnp.float32),
            struct((rows, KL + DR), jnp.float32),
        ),
        in_specs=vmem(7),
        out_specs=hbm(3) + vmem(2),
        scratch_shapes=list(weights_shape) + [pltpu.SemaphoreType.DMA(((QL + 2 * KL) // 256,))],
        compiler_params=params(),
        cost_estimate=free(),
        name="scale",
    )(squares, exchange(squares, "dp", n_dp, singles[-1]), *sums, *terms)
    return (latent_q, latent_kv, *scaled)


def solution(mesh):
    placed = (
        P("dp", None),
        P("dp", None),
        P("dp", "head"),
        P(None, "head"),
        P(None, "head"),
        P(None, "head"),
    )
    return jax.shard_map(
        functools.partial(per_device, mesh.shape["dp"], mesh.shape["head"]),
        mesh=mesh,
        in_specs=placed,
        out_specs=(
            P(("dp", "head"), None),
            P(("dp", "head"), None),
            P(None, "head"),
            P(None, "head"),
            P(None, "head"),
        ),
        check_vma=False,
    )
```

```python
import functools

import jax
import jax.numpy as jnp
import numpy as np
from jax import lax
from jax.experimental import pallas as pl
from jax.experimental.pallas import tpu as pltpu
from jax.sharding import PartitionSpec as P

QL = 1536
KL = 512
DN = 128
DR = 64
TILE = 128
WIDTH = DN + DR
PAIR = 2 * WIDTH
LATENT = QL + KL + DR

max_rms = 1.0
eps = 1e-06
VMEM_LIMIT = 32 * 2**20

NT = (((1,), (1,)), ((), ()))
TN = (((0,), (0,)), ((), ()))


def dot(left, right, dims=(((1,), (0,)), ((), ()))):
    return lax.dot_general(left, right, dims, preferred_element_type=jnp.float32)


def rotary_tables(length):
    half = DR // 2
    freqs = np.float32(10000.0) ** (
        np.float32(-2.0) * np.arange(half, dtype=np.float32) / np.float32(DR)
    )
    angle = np.arange(length, dtype=np.float32)[:, None] * freqs.astype(np.float32)[None, :]
    cosine, sine = np.cos(angle), np.sin(angle)
    ones, zeros = np.ones((length, DR), np.float32), np.zeros((length, DR), np.float32)
    return np.concatenate([cosine, cosine, ones, -sine, sine, zeros], axis=1)


def swap_halves(tile):
    lane = lax.broadcasted_iota(jnp.int32, tile.shape, 1)
    first = lane % DR < DR // 2
    return jnp.where(
        first, pltpu.roll(tile, TILE - DR // 2, 1), pltpu.roll(tile, DR // 2, 1)
    )


def rounded(values):
    return values.astype(jnp.bfloat16).astype(jnp.float32)


def softmax_grads(scores, grad_probs):
    length = scores.shape[0]
    block = length // 2
    scale = 1.0 / (DN + DR) ** 0.5
    key = lax.broadcasted_iota(jnp.int32, (block, block), 0)
    query = lax.broadcasted_iota(jnp.int32, (block, block), 1)
    allowed = key <= query
    grad_probs = rounded(grad_probs)
    probs_columns, grads_columns = [], []
    for column in range(2):
        columns = slice(column * block, (column + 1) * block)
        parts = [scores[:block, columns], scores[block:, columns]][: column + 1]
        parts[-1] = jnp.where(allowed, parts[-1], -jnp.inf)
        tops = [jnp.max(part, axis=0, keepdims=True) for part in parts]
        top = tops[0] if column == 0 else jnp.maximum(*tops)
        parts = [jnp.exp((part - top) * scale) for part in parts]
        sums = [jnp.sum(part, axis=0, keepdims=True) for part in parts]
        inverse = 1.0 / (sums[0] if column == 0 else sums[0] + sums[1])
        parts = [part * inverse for part in parts]
        grads = [grad_probs[:block, columns], grad_probs[block:, columns]][: column + 1]
        means = [jnp.sum(g * p, axis=0, keepdims=True) for g, p in zip(grads, parts)]
        mean = means[0] if column == 0 else means[0] + means[1]
        grads = [(p * (g - mean) * scale).astype(jnp.bfloat16) for g, p in zip(grads, parts)]
        parts = [p.astype(jnp.bfloat16) for p in parts]
        if column == 0:
            parts.append(jnp.zeros((block, block), jnp.bfloat16))
            grads.append(jnp.zeros((block, block), jnp.bfloat16))
        probs_columns.append(jnp.concatenate(parts, axis=0))
        grads_columns.append(jnp.concatenate(grads, axis=0))
    return jnp.concatenate(probs_columns, axis=1), jnp.concatenate(grads_columns, axis=1)


def backward(length, xq, xkv, grad, weights, table, gq, gkv, qw, kw, vw, rot_out, ready):
    wq, wk, wv = weights
    n_seq = xq.shape[0] // length
    wide = wk.shape[1]
    heads = wide // DN
    low = lax.broadcasted_iota(jnp.int32, (length, TILE), 1) < DR
    spans = [slice(s * length, (s + 1) * length) for s in range(n_seq)]

    ready[0]()
    cos_low, sin_low = table[:, :TILE], table[:, TILE:]
    cos_tiles = (cos_low, pltpu.roll(cos_low, DR, 1))
    sin_tiles = (sin_low, pltpu.roll(sin_low, DR, 1))
    latent = xkv[:, :KL]
    for pair in range(heads // 2):
        columns = slice(2 * DN * pair, 2 * DN * (pair + 1))
        keys = dot(latent, wk[:, columns])
        vw[:, columns] = dot(latent, wv[:, columns]).astype(jnp.bfloat16)
        for span in spans:
            rot = jnp.concatenate(
                [xkv[span, KL : KL + DR].astype(jnp.float32), jnp.zeros((length, DR), jnp.float32)],
                axis=1,
            )
            odd = pltpu.roll(keys[span, DN:], DR, 1)
            tiles = (
                keys[span, :DN],
                rot,
                jnp.where(low, 0.0, odd),
                jnp.where(low, odd, pltpu.roll(rot, DR, 1)),
            )
            for i, tile in enumerate(tiles):
                start = (4 * pair + i) * TILE
                kw[span, start : start + TILE] = tile.astype(jnp.bfloat16)
    ready[1]()
    for pair in range(heads // 2):
        queries = dot(xq[...], wq[:, PAIR * pair : PAIR * (pair + 1)])
        for span in spans:
            for i in range(3):
                part = rounded(queries[span, i * TILE : (i + 1) * TILE])
                if i > 0:
                    part = part * cos_tiles[i - 1] + swap_halves(part) * sin_tiles[i - 1]
                start = PAIR * pair + i * TILE
                qw[span, start : start + TILE] = part.astype(jnp.bfloat16)

    items = [(span, head) for span in spans for head in range(heads)]

    def windows(span, head):
        start = PAIR * (head // 2) + TILE * (head % 2)
        return (
            qw[span, start : start + 2 * TILE],
            kw[span, 2 * TILE * head : 2 * TILE * (head + 1)],
            slice(head * DN, (head + 1) * DN),
        )

    def first_products(span, head):
        query_window, key_window, columns = windows(span, head)
        return (
            dot(key_window, query_window, NT),
            dot(vw[span, columns], grad[span, columns], NT),
        )

    rot_sums = [jnp.zeros((length, TILE), jnp.float32) for _ in spans]
    pending = first_products(*items[0])
    even_part = None
    for index, (span, head) in enumerate(items):
        products = pending
        if index + 1 < len(items):
            pending = first_products(*items[index + 1])
        probs, grad_scores = softmax_grads(*products)
        query_window, key_window, columns = windows(span, head)
        gkv[span, wide + head * DN : wide + (head + 1) * DN] = dot(probs, grad[span, columns]).astype(
            jnp.bfloat16
        )
        key_part = dot(grad_scores, query_window)
        query_part = dot(grad_scores, key_window, TN)
        seq = index // heads
        if head % 2 == 0:
            gkv[span, columns] = key_part[:, :TILE].astype(jnp.bfloat16)
            if rot_out is not None:
                rot_sums[seq] = rot_sums[seq] + rounded(key_part[:, TILE:])
            even_part = query_part
            continue
        turned = pltpu.roll(key_part[:, TILE:], DR, 1)
        gkv[span, columns] = jnp.where(low, pltpu.roll(key_part[:, :TILE], DR, 1), turned).astype(
            jnp.bfloat16
        )
        if rot_out is not None:
            rot_sums[seq] = rot_sums[seq] + rounded(turned)
        parts = [
            even_part[:, :TILE],
            even_part[:, TILE:] + query_part[:, :TILE],
            query_part[:, TILE:],
        ]
        for i in range(3):
            part = parts[i]
            if i > 0:
                part = rounded(part)
                part = part * cos_tiles[i - 1] - swap_halves(part) * sin_tiles[i - 1]
            start = PAIR * (head // 2) + i * TILE
            gq[span, start : start + TILE] = part.astype(jnp.bfloat16)
    if rot_out is not None:
        rot_out[...] = rot_sums[0]


def raw_grads(parts, left, right, sums, previous):
    wide = right.shape[1] // parts
    total = jnp.zeros((8, TILE), jnp.float32)
    for start in range(0, sums[0].shape[0], KL):
        rows = slice(start, start + KL)
        product = dot(left[:, rows], right[...], TN)
        for part in range(parts):
            block = product[:, part * wide : (part + 1) * wide]
            if previous is not None:
                block = block + previous[part][rows, :]
            sums[part][rows, :] = block
            folded = jnp.sum((block * block).reshape(KL // 8, 8, wide), axis=0)
            for column in range(0, wide, TILE):
                total = total + folded[:, column : column + TILE]
    return total


def load_kernel(place, xq, kvt, grad, packed, kv_rows, sem):
    half, wide = packed.shape[0], grad.shape[1]
    width = QL + KL + TILE
    rows = pl.ds(pl.multiple_of(place[1] * half, half), half)
    pieces = (
        (kvt.at[:, rows], kv_rows),
        (xq.at[rows], packed.at[:, :QL]),
        (grad.at[:half], packed.at[:, width : width + wide]),
        (grad.at[half:], packed.at[:, width + wide :]),
    )
    copies = [pltpu.make_async_copy(*piece, sem.at[i]) for i, piece in enumerate(pieces)]
    for copy in copies:
        copy.start()
    copies[0].wait()
    for block in range(0, KL + DR, TILE):
        stop = min(block + TILE, KL + DR)
        packed[:, QL + block : QL + stop] = kv_rows[block:stop, :].T
    packed[:, LATENT:width] = jnp.zeros((half, TILE - DR), jnp.bfloat16)
    for copy in copies[1:]:
        copy.wait()


def own_kernel(n_head, place, xq_in, kvt_in, grad_in, wq_in, wk_in, wv_in, table_in, *refs):
    wq, wk, wv, table, xq, xkv, gq, gkv, keep, send_stay, send_go, *refs = refs
    kvt, grad, qw, kw, vw, term, sem = refs
    pieces = (
        (kvt_in, kvt),
        (table_in, table),
        (wk_in, wk),
        (wv_in, wv),
        (xq_in, xq),
        (wq_in, wq),
        (grad_in, grad),
    )
    copies = [pltpu.make_async_copy(*piece, sem.at[i]) for i, piece in enumerate(pieces)]
    for copy in copies:
        copy.start()

    def latents_ready():
        for copy in copies[:4]:
            copy.wait()
        for block in range(0, KL + DR, TILE):
            stop = min(block + TILE, KL + DR)
            xkv[:, block:stop] = kvt[block:stop, :].T

    def queries_ready():
        for copy in copies[4:]:
            copy.wait()

    length = xq.shape[0]
    rot = term.at[:, QL + KL :]
    ready = (latents_ready, queries_ready)
    backward(length, xq, xkv, grad, (wq, wk, wv), table, gq, gkv, qw, kw, vw, rot, ready)
    wide = wk.shape[1]
    term[:, :QL] = dot(gq[...], wq[...], NT)
    term[:, QL : QL + KL] = dot(gkv[:, :wide], wk[...], NT) + dot(gkv[:, wide:], wv[...], NT)
    rows = length // n_head
    chip, core = place[0], place[1]
    masks = [turned_round(k, n_head // 2) for k in range(n_head // 2)]

    def chosen(which):
        starts = [(2 * jnp.bitwise_xor(chip, mask) + which) * rows for mask in masks]
        return jnp.concatenate([term[pl.ds(pl.multiple_of(i, rows), rows), :] for i in starts])

    keep[...] = chosen(core)
    send = chosen(1 - core).astype(jnp.bfloat16)
    send_stay[...] = send[: send_stay.shape[0], :]
    send_go[...] = send[send_stay.shape[0] :, :]


def fold_kernel(keep, *refs):
    received, (stay, go) = refs[:-2], refs[-2:]
    total = jnp.concatenate([part[...] for part in received]).astype(jnp.float32) + keep[...]
    stay[...] = total[: stay.shape[0], :]
    go[...] = total[stay.shape[0] :, :].astype(jnp.bfloat16)


def far_kernel(n_seq, place, *refs):
    blocks, refs = refs[: 2 * n_seq], refs[2 * n_seq :]
    wq, wk, wv, table, xq, xkv, gq, gkv, grad, qw, kw, vw = refs
    half, wide = blocks[0].shape[0], grad.shape[1]
    length = 2 * half
    width = QL + KL + TILE
    core = place[1]
    for s in range(n_seq):
        mine, other = blocks[2 * s : 2 * s + 2]
        for source, side in ((mine, core), (other, 1 - core)):
            rows = pl.ds(pl.multiple_of(s * length + side * half, half), half)
            xq[rows, :] = source[:, :QL]
            xkv[rows, :] = source[:, QL:LATENT]
        start = s * length
        grad[start : start + half, :] = mine[:, width : width + wide]
        grad[start + half : start + length, :] = mine[:, width + wide :]
    ready = (lambda: None, lambda: None)
    backward(length, xq, xkv, grad, (wq, wk, wv), table, gq, gkv, qw, kw, vw, None, ready)


def sums_kernel(parts, first, left, right, *refs):
    previous, sums = (None, refs) if first else (refs[:parts], refs[parts:])
    raw_grads(parts, left, right, sums, previous)


def last_kernel(xq, xkv, gq, gkv, pq, pk, pv, local, received, sq, sk, sv, squares, latent_q, latent_kv):
    terms = local[...] + received[...].astype(jnp.float32)
    latent_q[...] = terms[:, :QL]
    latent_kv[...] = terms[:, QL:LATENT]
    squares[...] = raw_grads(1, xq, gq, (sq,), (pq,)) + raw_grads(2, xkv, gkv, (sk, sv), (pk, pv))


def add_kernel(left, right, out):
    out[...] = left[...] + right[...]


def add_once_kernel(place, own, *refs):
    total = jnp.where(place[1] == 0, own[...], 0.0)
    for ref in refs[:-1]:
        total = total + ref[...]
    refs[-1][...] = total


def scale_kernel(limit, sq, sk, sv, *refs):
    *parts, oq, ok, ov, bq, bk, bv, sem = refs
    total = parts[0][...]
    for part in parts[1:]:
        total = total + part[...]
    total = jnp.sum(total, keepdims=True)
    factor = jnp.minimum(1.0, limit / jnp.sqrt(total + eps))
    copies = []
    for source, buffer, out in ((sq, bq, oq), (sk, bk, ok), (sv, bv, ov)):
        for start in range(0, source.shape[0], 256):
            rows = slice(start, start + 256)
            buffer[rows, :] = (source[rows, :] * factor).astype(jnp.bfloat16)
            copy = pltpu.make_async_copy(buffer.at[rows], out.at[rows], sem.at[len(copies)])
            copy.start()
            copies.append(copy)
    for copy in copies:
        copy.wait()


def vmem(count):
    return [pl.BlockSpec(memory_space=pltpu.VMEM)] * count


def hbm(count):
    return [pl.BlockSpec(memory_space=pltpu.HBM)] * count


def params():
    return pltpu.CompilerParams(vmem_limit_bytes=VMEM_LIMIT)


def free():
    return pl.CostEstimate(flops=0, bytes_accessed=0, transcendentals=0)


def struct(shape, dtype):
    return jax.ShapeDtypeStruct(shape, dtype)


def exchange(value, axis, size, k):
    return lax.ppermute(value, axis, [(i, i ^ k) for i in range(size)])


def far_away(value):
    return pltpu.with_memory_space_constraint(value, pltpu.HBM)


def turned_round(mask, n_dp):
    bits = n_dp.bit_length() - 1
    return sum(((mask >> i) & 1) << (bits - 1 - i) for i in range(bits))


def across(value, n_dp, n_head, mask):
    masks = (mask, turned_round(mask, n_dp))
    pairs = [
        (d * n_head + h, (d ^ masks[h % 2]) * n_head + h) for d in range(n_dp) for h in range(n_head)
    ]
    return lax.ppermute(value, ("dp", "head"), pairs)


def per_device(n_dp, n_head, query_latent, kv_latent, out_grad, query_up, key_up, value_up):
    length = query_latent.shape[0]
    half = length // 2
    wide_q, wide_k = query_up.shape[1], key_up.shape[1]
    heads = wide_k // DN
    index = lax.axis_index("head")
    place = jnp.stack([index // 2, index % 2]).astype(jnp.int32)
    table = jnp.asarray(rotary_tables(length))
    smem = [pl.BlockSpec(memory_space=pltpu.SMEM)]
    inputs = [far_away(value) for value in (query_latent, kv_latent.T, out_grad)]
    width = QL + KL + TILE

    packed = pl.pallas_call(
        load_kernel,
        out_shape=pltpu.VMEM((half, width + 2 * wide_k), jnp.bfloat16),
        in_specs=smem + hbm(3),
        out_specs=pl.BlockSpec(memory_space=pltpu.VMEM),
        scratch_shapes=[pltpu.VMEM((KL + DR, half), jnp.bfloat16), pltpu.SemaphoreType.DMA((4,))],
        compiler_params=params(),
        cost_estimate=free(),
        name="load",
    )(place, *inputs)
    packed, place = lax.optimization_barrier((packed, place))
    singles = [1 << i for i in reversed(range(n_dp.bit_length() - 1))]
    received = {k: across(packed, n_dp, n_head, k) for k in singles}

    def rows_shape(rows):
        widths = (QL, KL + DR, wide_q, 2 * wide_k)
        return tuple(pltpu.VMEM((rows, width), jnp.bfloat16) for width in widths)

    def scratch(rows):
        widths = (wide_k, wide_q, 2 * TILE * heads, wide_k)
        return [pltpu.VMEM((rows, width), jnp.bfloat16) for width in widths]

    weights_shape = tuple(
        pltpu.VMEM(shape, jnp.bfloat16) for shape in ((QL, wide_q), (KL, wide_k), (KL, wide_k))
    )
    sums_shape = tuple(pltpu.VMEM(w.shape, jnp.float32) for w in weights_shape)
    *outs, keep, send_stay, send_go = pl.pallas_call(
        functools.partial(own_kernel, n_head),
        out_shape=(
            *weights_shape,
            pltpu.VMEM(table.shape, jnp.float32),
            *rows_shape(length),
            struct((half, width), jnp.float32),
            struct((half // 2, width), jnp.bfloat16),
            struct((half // 2, width), jnp.bfloat16),
        ),
        in_specs=smem + hbm(7),
        out_specs=vmem(11),
        scratch_shapes=[pltpu.VMEM((KL + DR, length), jnp.bfloat16)]
        + scratch(length)
        + [pltpu.VMEM((length, width), jnp.float32), pltpu.SemaphoreType.DMA((7,))],
        compiler_params=params(),
        cost_estimate=free(),
        name="own",
    )(place, *inputs, *[far_away(value) for value in (query_up, key_up, value_up, table)])
    weights, found = outs[:4], outs[4:]

    rows = length // n_head
    squares_shape = struct((8, TILE), jnp.float32)

    def add_sums(left, right, shapes, sums):
        return list(
            pl.pallas_call(
                functools.partial(sums_kernel, len(shapes), not sums),
                out_shape=shapes,
                in_specs=vmem(2 + len(sums)),
                out_specs=vmem(len(shapes)),
                input_output_aliases={2 + i: i for i in range(len(sums))},
                compiler_params=params(),
                cost_estimate=free(),
                name="sums",
            )(left, right, *sums)
        )

    def add(kernel, *values):
        scalars = smem if kernel is add_once_kernel else []
        return pl.pallas_call(
            kernel,
            out_shape=squares_shape,
            in_specs=scalars + vmem(len(values) - len(scalars)),
            out_specs=pl.BlockSpec(memory_space=pltpu.VMEM),
            compiler_params=params(),
            cost_estimate=free(),
            name="add",
        )(*values)

    sums = add_sums(found[0], found[2], sums_shape[:1], [])
    sums += add_sums(found[1], found[3], sums_shape[1:], [])

    def fold(keep, *received):
        half_shape = (keep.shape[0] // 2, width)
        return pl.pallas_call(
            fold_kernel,
            out_shape=(struct(half_shape, jnp.float32), struct(half_shape, jnp.bfloat16)),
            in_specs=vmem(1 + len(received)),
            out_specs=vmem(2),
            compiler_params=params(),
            cost_estimate=free(),
            name="fold",
        )(keep, *received)

    stay, go = fold(keep, *[exchange(send, "head", n_head, 1) for send in (send_stay, send_go)])
    bits = [2 << i for i in range(n_head.bit_length() - 2)]
    for bit in bits[:-2]:
        stay, go = fold(stay, exchange(go, "head", n_head, bit))
    came = exchange(go, "head", n_head, bits[-2])

    values = [received[k] for k in singles]
    *values, sums[2], came = lax.optimization_barrier((*values, sums[2], came))
    received = dict(zip(singles, values))
    for k in range(3, n_dp):
        if k not in received:
            received[k] = across(received[k & (k - 1)], n_dp, n_head, k & -k)
    stay, go = fold(stay, came)
    terms = [stay, exchange(go, "head", n_head, bits[-1])]

    def swapped(k):
        return exchange(received[turned_round(k, n_dp)], "head", n_head, 1)

    groups = [(1, 2)] + [(k,) for k in range(3, n_dp)]
    for group in groups:
        n_seq = len(group)
        blocks = []
        for k in group:
            blocks += [received[k], swapped(k)]
        if group is not groups[0]:
            blocks[1], sums[1] = lax.optimization_barrier((blocks[1], sums[1]))
        found = list(
            pl.pallas_call(
                functools.partial(far_kernel, n_seq),
                out_shape=rows_shape(n_seq * length),
                in_specs=smem + vmem(len(blocks) + 4),
                out_specs=vmem(4),
                scratch_shapes=scratch(n_seq * length),
                compiler_params=params(),
                cost_estimate=free(),
                name="far",
            )(place, *blocks, *weights)
        )
        if group is groups[-1]:
            break
        if group is groups[0]:
            found[2], terms[1] = lax.optimization_barrier((found[2], terms[1]))
        sums[:1] = add_sums(found[0], found[2], sums_shape[:1], sums[:1])
        k = groups[groups.index(group) + 1][0]
        received[k], sums[0] = lax.optimization_barrier((received[k], sums[0]))
        sums[1:] = add_sums(found[1], found[3], sums_shape[1:], sums[1:])

    *sums, squares, latent_q, latent_kv = pl.pallas_call(
        last_kernel,
        out_shape=(
            *sums_shape,
            squares_shape,
            struct((rows, QL), jnp.float32),
            struct((rows, KL + DR), jnp.float32),
        ),
        in_specs=vmem(4 + 3 + 2),
        out_specs=vmem(6),
        input_output_aliases={4: 0, 5: 1, 6: 2},
        compiler_params=params(),
        cost_estimate=free(),
        name="last",
    )(*found, *sums, *terms)

    count = (QL * wide_q + 2 * KL * wide_k) * n_head
    limit = max_rms * count**0.5
    squares = add(add_kernel, squares, exchange(squares, "head", n_head, 1))
    came = []
    for mask in range(1, n_head // 2, 2):
        masks = (2 * mask, 2 * mask + 2)
        pairs = [(i, i ^ masks[i % 2]) for i in range(n_head) if masks[i % 2] < n_head]
        came.append(lax.ppermute(squares, "head", pairs))
    squares = add(add_once_kernel, place, squares, *came)
    parts = [squares, exchange(squares, "head", n_head, 1)]
    scaled = pl.pallas_call(
        functools.partial(scale_kernel, limit),
        out_shape=tuple(struct(w.shape, jnp.bfloat16) for w in weights_shape),
        in_specs=vmem(3 + len(parts)),
        out_specs=hbm(3),
        scratch_shapes=list(weights_shape)
        + [pltpu.SemaphoreType.DMA(((QL + 2 * KL) // 256,))],
        compiler_params=params(),
        cost_estimate=free(),
        name="scale",
    )(*sums, *parts)
    return (latent_q, latent_kv, *scaled)


def solution(mesh):
    placed = (
        P("dp", None),
        P("dp", None),
        P("dp", "head"),
        P(None, "head"),
        P(None, "head"),
        P(None, "head"),
    )
    return jax.shard_map(
        functools.partial(per_device, mesh.shape["dp"], mesh.shape["head"]),
        mesh=mesh,
        in_specs=placed,
        out_specs=(
            P(("dp", "head"), None),
            P(("dp", "head"), None),
            P(None, "head"),
            P(None, "head"),
            P(None, "head"),
        ),
        check_vma=False,
    )
```

```python
import functools

import jax
import jax.numpy as jnp
import numpy as np
from jax import lax
from jax.experimental import pallas as pl
from jax.experimental.pallas import tpu as pltpu
from jax.sharding import PartitionSpec as P

QL = 1536
KL = 512
DN = 128
DR = 64
TILE = 128
WIDTH = DN + DR
PAIR = 2 * WIDTH
LATENT = QL + KL + DR

max_rms = 1.0
eps = 1e-06
VMEM_LIMIT = 32 * 2**20

NT = (((1,), (1,)), ((), ()))
TN = (((0,), (0,)), ((), ()))


def dot(left, right, dims=(((1,), (0,)), ((), ()))):
    return lax.dot_general(left, right, dims, preferred_element_type=jnp.float32)


def rotary_tables(length):
    half = DR // 2
    freqs = np.float32(10000.0) ** (
        np.float32(-2.0) * np.arange(half, dtype=np.float32) / np.float32(DR)
    )
    angle = np.arange(length, dtype=np.float32)[:, None] * freqs.astype(np.float32)[None, :]
    cosine, sine = np.cos(angle), np.sin(angle)
    ones, zeros = np.ones((length, DR), np.float32), np.zeros((length, DR), np.float32)
    return np.concatenate([cosine, cosine, ones, -sine, sine, zeros], axis=1)


def swap_halves(tile):
    lane = lax.broadcasted_iota(jnp.int32, tile.shape, 1)
    first = lane % DR < DR // 2
    return jnp.where(
        first, pltpu.roll(tile, TILE - DR // 2, 1), pltpu.roll(tile, DR // 2, 1)
    )


def rounded(values):
    return values.astype(jnp.bfloat16).astype(jnp.float32)


def softmax_grads(scores, grad_probs):
    length = scores.shape[0]
    block = length // 2
    scale = 1.0 / (DN + DR) ** 0.5
    key = lax.broadcasted_iota(jnp.int32, (block, block), 0)
    query = lax.broadcasted_iota(jnp.int32, (block, block), 1)
    allowed = key <= query
    grad_probs = rounded(grad_probs)
    probs_columns, grads_columns = [], []
    for column in range(2):
        columns = slice(column * block, (column + 1) * block)
        parts = [scores[:block, columns], scores[block:, columns]][: column + 1]
        parts[-1] = jnp.where(allowed, parts[-1], -jnp.inf)
        tops = [jnp.max(part, axis=0, keepdims=True) for part in parts]
        top = tops[0] if column == 0 else jnp.maximum(*tops)
        parts = [jnp.exp((part - top) * scale) for part in parts]
        sums = [jnp.sum(part, axis=0, keepdims=True) for part in parts]
        inverse = 1.0 / (sums[0] if column == 0 else sums[0] + sums[1])
        parts = [part * inverse for part in parts]
        grads = [grad_probs[:block, columns], grad_probs[block:, columns]][: column + 1]
        means = [jnp.sum(g * p, axis=0, keepdims=True) for g, p in zip(grads, parts)]
        mean = means[0] if column == 0 else means[0] + means[1]
        grads = [(p * (g - mean) * scale).astype(jnp.bfloat16) for g, p in zip(grads, parts)]
        parts = [p.astype(jnp.bfloat16) for p in parts]
        if column == 0:
            parts.append(jnp.zeros((block, block), jnp.bfloat16))
            grads.append(jnp.zeros((block, block), jnp.bfloat16))
        probs_columns.append(jnp.concatenate(parts, axis=0))
        grads_columns.append(jnp.concatenate(grads, axis=0))
    return jnp.concatenate(probs_columns, axis=1), jnp.concatenate(grads_columns, axis=1)


def backward(length, xq, xkv, grad, weights, table, gq, gkv, qw, kw, vw, rot_out, ready):
    wq, wk, wv = weights
    n_seq = xq.shape[0] // length
    wide = wk.shape[1]
    heads = wide // DN
    low = lax.broadcasted_iota(jnp.int32, (length, TILE), 1) < DR
    spans = [slice(s * length, (s + 1) * length) for s in range(n_seq)]

    ready[0]()
    cos_low, sin_low = table[:, :TILE], table[:, TILE:]
    cos_tiles = (cos_low, pltpu.roll(cos_low, DR, 1))
    sin_tiles = (sin_low, pltpu.roll(sin_low, DR, 1))
    latent = xkv[:, :KL]
    for pair in range(heads // 2):
        columns = slice(2 * DN * pair, 2 * DN * (pair + 1))
        keys = dot(latent, wk[:, columns])
        vw[:, columns] = dot(latent, wv[:, columns]).astype(jnp.bfloat16)
        for span in spans:
            rot = jnp.concatenate(
                [xkv[span, KL : KL + DR].astype(jnp.float32), jnp.zeros((length, DR), jnp.float32)],
                axis=1,
            )
            odd = pltpu.roll(keys[span, DN:], DR, 1)
            tiles = (
                keys[span, :DN],
                rot,
                jnp.where(low, 0.0, odd),
                jnp.where(low, odd, pltpu.roll(rot, DR, 1)),
            )
            for i, tile in enumerate(tiles):
                start = (4 * pair + i) * TILE
                kw[span, start : start + TILE] = tile.astype(jnp.bfloat16)
    ready[1]()
    for pair in range(heads // 2):
        queries = dot(xq[...], wq[:, PAIR * pair : PAIR * (pair + 1)])
        for span in spans:
            for i in range(3):
                part = rounded(queries[span, i * TILE : (i + 1) * TILE])
                if i > 0:
                    part = part * cos_tiles[i - 1] + swap_halves(part) * sin_tiles[i - 1]
                start = PAIR * pair + i * TILE
                qw[span, start : start + TILE] = part.astype(jnp.bfloat16)

    items = [(span, head) for span in spans for head in range(heads)]

    def windows(span, head):
        start = PAIR * (head // 2) + TILE * (head % 2)
        return (
            qw[span, start : start + 2 * TILE],
            kw[span, 2 * TILE * head : 2 * TILE * (head + 1)],
            slice(head * DN, (head + 1) * DN),
        )

    def first_products(span, head):
        query_window, key_window, columns = windows(span, head)
        return (
            dot(key_window, query_window, NT),
            dot(vw[span, columns], grad[span, columns], NT),
        )

    rot_sums = [jnp.zeros((length, TILE), jnp.float32) for _ in spans]
    pending = first_products(*items[0])
    even_part = None
    for index, (span, head) in enumerate(items):
        products = pending
        if index + 1 < len(items):
            pending = first_products(*items[index + 1])
        probs, grad_scores = softmax_grads(*products)
        query_window, key_window, columns = windows(span, head)
        gkv[span, wide + head * DN : wide + (head + 1) * DN] = dot(probs, grad[span, columns]).astype(
            jnp.bfloat16
        )
        key_part = dot(grad_scores, query_window)
        query_part = dot(grad_scores, key_window, TN)
        seq = index // heads
        if head % 2 == 0:
            gkv[span, columns] = key_part[:, :TILE].astype(jnp.bfloat16)
            if rot_out is not None:
                rot_sums[seq] = rot_sums[seq] + rounded(key_part[:, TILE:])
            even_part = query_part
            continue
        turned = pltpu.roll(key_part[:, TILE:], DR, 1)
        gkv[span, columns] = jnp.where(low, pltpu.roll(key_part[:, :TILE], DR, 1), turned).astype(
            jnp.bfloat16
        )
        if rot_out is not None:
            rot_sums[seq] = rot_sums[seq] + rounded(turned)
        parts = [
            even_part[:, :TILE],
            even_part[:, TILE:] + query_part[:, :TILE],
            query_part[:, TILE:],
        ]
        for i in range(3):
            part = parts[i]
            if i > 0:
                part = rounded(part)
                part = part * cos_tiles[i - 1] - swap_halves(part) * sin_tiles[i - 1]
            start = PAIR * (head // 2) + i * TILE
            gq[span, start : start + TILE] = part.astype(jnp.bfloat16)
    if rot_out is not None:
        rot_out[...] = rot_sums[0]


def raw_grads(parts, left, right, sums, previous):
    wide = right.shape[1] // parts
    total = jnp.zeros((8, TILE), jnp.float32)
    for start in range(0, sums[0].shape[0], KL):
        rows = slice(start, start + KL)
        product = dot(left[:, rows], right[...], TN)
        for part in range(parts):
            block = product[:, part * wide : (part + 1) * wide]
            if previous is not None:
                block = block + previous[part][rows, :]
            sums[part][rows, :] = block
            folded = jnp.sum((block * block).reshape(KL // 8, 8, wide), axis=0)
            for column in range(0, wide, TILE):
                total = total + folded[:, column : column + TILE]
    return total


def load_kernel(place, xq, kvt, grad, packed, kv_rows, sem):
    half, wide = packed.shape[0], grad.shape[1]
    width = QL + KL + TILE
    rows = pl.ds(pl.multiple_of(place[1] * half, half), half)
    pieces = (
        (kvt.at[:, rows], kv_rows),
        (xq.at[rows], packed.at[:, :QL]),
        (grad.at[:half], packed.at[:, width : width + wide]),
        (grad.at[half:], packed.at[:, width + wide :]),
    )
    copies = [pltpu.make_async_copy(*piece, sem.at[i]) for i, piece in enumerate(pieces)]
    for copy in copies:
        copy.start()
    copies[0].wait()
    for block in range(0, KL + DR, TILE):
        stop = min(block + TILE, KL + DR)
        packed[:, QL + block : QL + stop] = kv_rows[block:stop, :].T
    packed[:, LATENT:width] = jnp.zeros((half, TILE - DR), jnp.bfloat16)
    for copy in copies[1:]:
        copy.wait()


def own_kernel(n_head, place, xq_in, kvt_in, grad_in, wq_in, wk_in, wv_in, table_in, *refs):
    wq, wk, wv, table, xq, xkv, gq, gkv, keep, send_stay, send_go, *refs = refs
    kvt, grad, qw, kw, vw, term, sem = refs
    pieces = (
        (kvt_in, kvt),
        (table_in, table),
        (wk_in, wk),
        (wv_in, wv),
        (xq_in, xq),
        (wq_in, wq),
        (grad_in, grad),
    )
    copies = [pltpu.make_async_copy(*piece, sem.at[i]) for i, piece in enumerate(pieces)]
    for copy in copies:
        copy.start()

    def latents_ready():
        for copy in copies[:4]:
            copy.wait()
        for block in range(0, KL + DR, TILE):
            stop = min(block + TILE, KL + DR)
            xkv[:, block:stop] = kvt[block:stop, :].T

    def queries_ready():
        for copy in copies[4:]:
            copy.wait()

    length = xq.shape[0]
    rot = term.at[:, QL + KL :]
    ready = (latents_ready, queries_ready)
    backward(length, xq, xkv, grad, (wq, wk, wv), table, gq, gkv, qw, kw, vw, rot, ready)
    wide = wk.shape[1]
    term[:, :QL] = dot(gq[...], wq[...], NT)
    term[:, QL : QL + KL] = dot(gkv[:, :wide], wk[...], NT) + dot(gkv[:, wide:], wv[...], NT)
    rows = length // n_head
    chip, core = place[0], place[1]
    masks = [turned_round(k, n_head // 2) for k in range(n_head // 2)]

    def chosen(which):
        starts = [(2 * jnp.bitwise_xor(chip, mask) + which) * rows for mask in masks]
        return jnp.concatenate([term[pl.ds(pl.multiple_of(i, rows), rows), :] for i in starts])

    keep[...] = chosen(core)
    send = chosen(1 - core).astype(jnp.bfloat16)
    send_stay[...] = send[: send_stay.shape[0], :]
    send_go[...] = send[send_stay.shape[0] :, :]


def fold_kernel(keep, *refs):
    received, (stay, go) = refs[:-2], refs[-2:]
    total = jnp.concatenate([part[...] for part in received]).astype(jnp.float32) + keep[...]
    stay[...] = total[: stay.shape[0], :]
    go[...] = total[stay.shape[0] :, :].astype(jnp.bfloat16)


def far_kernel(n_seq, place, *refs):
    blocks, refs = refs[: 2 * n_seq], refs[2 * n_seq :]
    wq, wk, wv, table, xq, xkv, gq, gkv, grad, qw, kw, vw = refs
    half, wide = blocks[0].shape[0], grad.shape[1]
    length = 2 * half
    width = QL + KL + TILE
    core = place[1]
    for s in range(n_seq):
        mine, other = blocks[2 * s : 2 * s + 2]
        for source, side in ((mine, core), (other, 1 - core)):
            rows = pl.ds(pl.multiple_of(s * length + side * half, half), half)
            xq[rows, :] = source[:, :QL]
            xkv[rows, :] = source[:, QL:LATENT]
        start = s * length
        grad[start : start + half, :] = mine[:, width : width + wide]
        grad[start + half : start + length, :] = mine[:, width + wide :]
    ready = (lambda: None, lambda: None)
    backward(length, xq, xkv, grad, (wq, wk, wv), table, gq, gkv, qw, kw, vw, None, ready)


def sums_kernel(parts, first, left, right, *refs):
    previous, sums = (None, refs) if first else (refs[:parts], refs[parts:])
    raw_grads(parts, left, right, sums, previous)


def last_kernel(xq, xkv, gq, gkv, pq, pk, pv, sq, sk, sv, squares):
    squares[...] = raw_grads(1, xq, gq, (sq,), (pq,)) + raw_grads(2, xkv, gkv, (sk, sv), (pk, pv))


def add_kernel(left, right, out):
    out[...] = left[...] + right[...]


def scale_kernel(limit, local, received, sq, sk, sv, *refs):
    *parts, oq, ok, ov, latent_q, latent_kv, bq, bk, bv, sem = refs
    total = parts[0][...]
    for part in parts[1:]:
        total = total + part[...]
    total = jnp.sum(total, keepdims=True)
    factor = jnp.minimum(1.0, limit / jnp.sqrt(total + eps))
    copies = []
    for source, buffer, out in ((sq, bq, oq), (sk, bk, ok), (sv, bv, ov)):
        for start in range(0, source.shape[0], 256):
            rows = slice(start, start + 256)
            buffer[rows, :] = (source[rows, :] * factor).astype(jnp.bfloat16)
            copy = pltpu.make_async_copy(buffer.at[rows], out.at[rows], sem.at[len(copies)])
            copy.start()
            copies.append(copy)
    terms = local[...] + received[...].astype(jnp.float32)
    latent_q[...] = terms[:, :QL]
    latent_kv[...] = terms[:, QL:LATENT]
    for copy in copies:
        copy.wait()


def vmem(count):
    return [pl.BlockSpec(memory_space=pltpu.VMEM)] * count


def hbm(count):
    return [pl.BlockSpec(memory_space=pltpu.HBM)] * count


def params():
    return pltpu.CompilerParams(vmem_limit_bytes=VMEM_LIMIT)


def free():
    return pl.CostEstimate(flops=0, bytes_accessed=0, transcendentals=0)


def struct(shape, dtype):
    return jax.ShapeDtypeStruct(shape, dtype)


def exchange(value, axis, size, k):
    return lax.ppermute(value, axis, [(i, i ^ k) for i in range(size)])


def far_away(value):
    return pltpu.with_memory_space_constraint(value, pltpu.HBM)


def turned_round(mask, n_dp):
    bits = n_dp.bit_length() - 1
    return sum(((mask >> i) & 1) << (bits - 1 - i) for i in range(bits))


def across(value, n_dp, n_head, mask):
    masks = (mask, turned_round(mask, n_dp))
    pairs = [
        (d * n_head + h, (d ^ masks[h % 2]) * n_head + h) for d in range(n_dp) for h in range(n_head)
    ]
    return lax.ppermute(value, ("dp", "head"), pairs)


def per_device(n_dp, n_head, query_latent, kv_latent, out_grad, query_up, key_up, value_up):
    length = query_latent.shape[0]
    half = length // 2
    wide_q, wide_k = query_up.shape[1], key_up.shape[1]
    heads = wide_k // DN
    index = lax.axis_index("head")
    place = jnp.stack([index // 2, index % 2]).astype(jnp.int32)
    table = jnp.asarray(rotary_tables(length))
    smem = [pl.BlockSpec(memory_space=pltpu.SMEM)]
    inputs = [far_away(value) for value in (query_latent, kv_latent.T, out_grad)]
    width = QL + KL + TILE

    packed = pl.pallas_call(
        load_kernel,
        out_shape=pltpu.VMEM((half, width + 2 * wide_k), jnp.bfloat16),
        in_specs=smem + hbm(3),
        out_specs=pl.BlockSpec(memory_space=pltpu.VMEM),
        scratch_shapes=[pltpu.VMEM((KL + DR, half), jnp.bfloat16), pltpu.SemaphoreType.DMA((4,))],
        compiler_params=params(),
        cost_estimate=free(),
        name="load",
    )(place, *inputs)
    packed, place = lax.optimization_barrier((packed, place))
    singles = [1 << i for i in reversed(range(n_dp.bit_length() - 1))]
    received = {k: across(packed, n_dp, n_head, k) for k in singles}

    def rows_shape(rows):
        widths = (QL, KL + DR, wide_q, 2 * wide_k)
        return tuple(pltpu.VMEM((rows, width), jnp.bfloat16) for width in widths)

    def scratch(rows):
        widths = (wide_k, wide_q, 2 * TILE * heads, wide_k)
        return [pltpu.VMEM((rows, width), jnp.bfloat16) for width in widths]

    weights_shape = tuple(
        pltpu.VMEM(shape, jnp.bfloat16) for shape in ((QL, wide_q), (KL, wide_k), (KL, wide_k))
    )
    sums_shape = tuple(pltpu.VMEM(w.shape, jnp.float32) for w in weights_shape)
    *outs, keep, send_stay, send_go = pl.pallas_call(
        functools.partial(own_kernel, n_head),
        out_shape=(
            *weights_shape,
            pltpu.VMEM(table.shape, jnp.float32),
            *rows_shape(length),
            struct((half, width), jnp.float32),
            struct((half // 2, width), jnp.bfloat16),
            struct((half // 2, width), jnp.bfloat16),
        ),
        in_specs=smem + hbm(7),
        out_specs=vmem(11),
        scratch_shapes=[pltpu.VMEM((KL + DR, length), jnp.bfloat16)]
        + scratch(length)
        + [pltpu.VMEM((length, width), jnp.float32), pltpu.SemaphoreType.DMA((7,))],
        compiler_params=params(),
        cost_estimate=free(),
        name="own",
    )(place, *inputs, *[far_away(value) for value in (query_up, key_up, value_up, table)])
    weights, found = outs[:4], outs[4:]

    rows = length // n_head
    squares_shape = struct((8, TILE), jnp.float32)

    def add_sums(left, right, shapes, sums):
        return list(
            pl.pallas_call(
                functools.partial(sums_kernel, len(shapes), not sums),
                out_shape=shapes,
                in_specs=vmem(2 + len(sums)),
                out_specs=vmem(len(shapes)),
                input_output_aliases={2 + i: i for i in range(len(sums))},
                compiler_params=params(),
                cost_estimate=free(),
                name="sums",
            )(left, right, *sums)
        )

    def add(left, right):
        return pl.pallas_call(
            add_kernel,
            out_shape=squares_shape,
            in_specs=vmem(2),
            out_specs=pl.BlockSpec(memory_space=pltpu.VMEM),
            compiler_params=params(),
            cost_estimate=free(),
            name="add",
        )(left, right)

    sums = add_sums(found[0], found[2], sums_shape[:1], [])
    sums += add_sums(found[1], found[3], sums_shape[1:], [])

    def fold(keep, *received):
        half_shape = (keep.shape[0] // 2, width)
        return pl.pallas_call(
            fold_kernel,
            out_shape=(struct(half_shape, jnp.float32), struct(half_shape, jnp.bfloat16)),
            in_specs=vmem(1 + len(received)),
            out_specs=vmem(2),
            compiler_params=params(),
            cost_estimate=free(),
            name="fold",
        )(keep, *received)

    stay, go = fold(keep, *[exchange(send, "head", n_head, 1) for send in (send_stay, send_go)])
    bits = [2 << i for i in range(n_head.bit_length() - 2)]
    for bit in bits[:-2]:
        stay, go = fold(stay, exchange(go, "head", n_head, bit))
    came = exchange(go, "head", n_head, bits[-2])

    values = [received[k] for k in singles]
    *values, sums[0], sums[2], came = lax.optimization_barrier((*values, sums[0], sums[2], came))
    received = dict(zip(singles, values))
    for k in range(3, n_dp):
        if k not in received:
            received[k] = across(received[k & (k - 1)], n_dp, n_head, k & -k)
    def swapped(k):
        return exchange(received[turned_round(k, n_dp)], "head", n_head, 1)

    groups = [(1, 2)] + [(k,) for k in range(3, n_dp)]
    for group in groups:
        n_seq = len(group)
        blocks = []
        for k in group:
            blocks += [received[k], swapped(k)]
        if group is not groups[0]:
            blocks[1], sums[1] = lax.optimization_barrier((blocks[1], sums[1]))
        found = list(
            pl.pallas_call(
                functools.partial(far_kernel, n_seq),
                out_shape=rows_shape(n_seq * length),
                in_specs=smem + vmem(len(blocks) + 4),
                out_specs=vmem(4),
                scratch_shapes=scratch(n_seq * length),
                compiler_params=params(),
                cost_estimate=free(),
                name="far",
            )(place, *blocks, *weights)
        )
        if group is groups[-1]:
            break
        if group is groups[0]:
            came, found[3] = lax.optimization_barrier((came, found[3]))
            stay, go = fold(stay, came)
            go, found[2] = lax.optimization_barrier((go, found[2]))
            terms = [stay, exchange(go, "head", n_head, bits[-1])]
        sums[:1] = add_sums(found[0], found[2], sums_shape[:1], sums[:1])
        k = groups[groups.index(group) + 1][0]
        received[k], sums[0] = lax.optimization_barrier((received[k], sums[0]))
        sums[1:] = add_sums(found[1], found[3], sums_shape[1:], sums[1:])

    *sums, squares = pl.pallas_call(
        last_kernel,
        out_shape=(*sums_shape, squares_shape),
        in_specs=vmem(4 + 3),
        out_specs=vmem(4),
        input_output_aliases={4: 0, 5: 1, 6: 2},
        compiler_params=params(),
        cost_estimate=free(),
        name="last",
    )(*found, *sums)

    count = (QL * wide_q + 2 * KL * wide_k) * n_head
    limit = max_rms * count**0.5
    squares = add(squares, exchange(squares, "head", n_head, 1))
    squares, terms[1] = lax.optimization_barrier((squares, terms[1]))
    parts = [squares] + [exchange(squares, "head", n_head, 2 * k) for k in range(1, n_head // 2)]
    *scaled, latent_q, latent_kv = pl.pallas_call(
        functools.partial(scale_kernel, limit),
        out_shape=(
            *[struct(w.shape, jnp.bfloat16) for w in weights_shape],
            struct((rows, QL), jnp.float32),
            struct((rows, KL + DR), jnp.float32),
        ),
        in_specs=vmem(2 + 3 + len(parts)),
        out_specs=hbm(3) + vmem(2),
        scratch_shapes=list(weights_shape)
        + [pltpu.SemaphoreType.DMA(((QL + 2 * KL) // 256,))],
        compiler_params=params(),
        cost_estimate=free(),
        name="scale",
    )(*terms, *sums, *parts)
    return (latent_q, latent_kv, *scaled)


def solution(mesh):
    placed = (
        P("dp", None),
        P("dp", None),
        P("dp", "head"),
        P(None, "head"),
        P(None, "head"),
        P(None, "head"),
    )
    return jax.shard_map(
        functools.partial(per_device, mesh.shape["dp"], mesh.shape["head"]),
        mesh=mesh,
        in_specs=placed,
        out_specs=(
            P(("dp", "head"), None),
            P(("dp", "head"), None),
            P(None, "head"),
            P(None, "head"),
            P(None, "head"),
        ),
        check_vma=False,
    )
```

```python
import functools

import jax
import jax.numpy as jnp
import numpy as np
from jax import lax
from jax.experimental import pallas as pl
from jax.experimental.pallas import tpu as pltpu
from jax.sharding import PartitionSpec as P

QL = 1536
KL = 512
DN = 128
DR = 64
TILE = 128
WIDTH = DN + DR
PAIR = 2 * WIDTH
LATENT = QL + KL + DR

max_rms = 1.0
eps = 1e-06
VMEM_LIMIT = 32 * 2**20

NT = (((1,), (1,)), ((), ()))
TN = (((0,), (0,)), ((), ()))


def dot(left, right, dims=(((1,), (0,)), ((), ()))):
    return lax.dot_general(left, right, dims, preferred_element_type=jnp.float32)


def rotary_tables(length):
    half = DR // 2
    freqs = np.float32(10000.0) ** (
        np.float32(-2.0) * np.arange(half, dtype=np.float32) / np.float32(DR)
    )
    angle = np.arange(length, dtype=np.float32)[:, None] * freqs.astype(np.float32)[None, :]
    cosine, sine = np.cos(angle), np.sin(angle)
    ones, zeros = np.ones((length, DR), np.float32), np.zeros((length, DR), np.float32)
    return np.concatenate([cosine, cosine, ones, -sine, sine, zeros], axis=1)


def swap_halves(tile):
    lane = lax.broadcasted_iota(jnp.int32, tile.shape, 1)
    first = lane % DR < DR // 2
    return jnp.where(
        first, pltpu.roll(tile, TILE - DR // 2, 1), pltpu.roll(tile, DR // 2, 1)
    )


def rounded(values):
    return values.astype(jnp.bfloat16).astype(jnp.float32)


def softmax_grads(scores, grad_probs):
    length = scores.shape[0]
    block = length // 2
    scale = 1.0 / (DN + DR) ** 0.5
    key = lax.broadcasted_iota(jnp.int32, (block, block), 0)
    query = lax.broadcasted_iota(jnp.int32, (block, block), 1)
    allowed = key <= query
    grad_probs = rounded(grad_probs)
    probs_columns, grads_columns = [], []
    for column in range(2):
        columns = slice(column * block, (column + 1) * block)
        parts = [scores[:block, columns], scores[block:, columns]][: column + 1]
        parts[-1] = jnp.where(allowed, parts[-1], -jnp.inf)
        tops = [jnp.max(part, axis=0, keepdims=True) for part in parts]
        top = tops[0] if column == 0 else jnp.maximum(*tops)
        parts = [jnp.exp((part - top) * scale) for part in parts]
        sums = [jnp.sum(part, axis=0, keepdims=True) for part in parts]
        inverse = 1.0 / (sums[0] if column == 0 else sums[0] + sums[1])
        parts = [part * inverse for part in parts]
        grads = [grad_probs[:block, columns], grad_probs[block:, columns]][: column + 1]
        means = [jnp.sum(g * p, axis=0, keepdims=True) for g, p in zip(grads, parts)]
        mean = means[0] if column == 0 else means[0] + means[1]
        grads = [(p * (g - mean) * scale).astype(jnp.bfloat16) for g, p in zip(grads, parts)]
        parts = [p.astype(jnp.bfloat16) for p in parts]
        if column == 0:
            parts.append(jnp.zeros((block, block), jnp.bfloat16))
            grads.append(jnp.zeros((block, block), jnp.bfloat16))
        probs_columns.append(jnp.concatenate(parts, axis=0))
        grads_columns.append(jnp.concatenate(grads, axis=0))
    return jnp.concatenate(probs_columns, axis=1), jnp.concatenate(grads_columns, axis=1)


def backward(length, xq, xkv, grad, weights, table, gq, gkv, qw, kw, vw, rot_out, ready):
    wq, wk, wv = weights
    n_seq = xq.shape[0] // length
    wide = wk.shape[1]
    heads = wide // DN
    low = lax.broadcasted_iota(jnp.int32, (length, TILE), 1) < DR
    spans = [slice(s * length, (s + 1) * length) for s in range(n_seq)]

    ready[0]()
    cos_low, sin_low = table[:, :TILE], table[:, TILE:]
    cos_tiles = (cos_low, pltpu.roll(cos_low, DR, 1))
    sin_tiles = (sin_low, pltpu.roll(sin_low, DR, 1))
    latent = xkv[:, :KL]
    for pair in range(heads // 2):
        columns = slice(2 * DN * pair, 2 * DN * (pair + 1))
        keys = dot(latent, wk[:, columns])
        vw[:, columns] = dot(latent, wv[:, columns]).astype(jnp.bfloat16)
        for span in spans:
            rot = jnp.concatenate(
                [xkv[span, KL : KL + DR].astype(jnp.float32), jnp.zeros((length, DR), jnp.float32)],
                axis=1,
            )
            odd = pltpu.roll(keys[span, DN:], DR, 1)
            tiles = (
                keys[span, :DN],
                rot,
                jnp.where(low, 0.0, odd),
                jnp.where(low, odd, pltpu.roll(rot, DR, 1)),
            )
            for i, tile in enumerate(tiles):
                start = (4 * pair + i) * TILE
                kw[span, start : start + TILE] = tile.astype(jnp.bfloat16)
    ready[1]()
    for pair in range(heads // 2):
        queries = dot(xq[...], wq[:, PAIR * pair : PAIR * (pair + 1)])
        for span in spans:
            for i in range(3):
                part = rounded(queries[span, i * TILE : (i + 1) * TILE])
                if i > 0:
                    part = part * cos_tiles[i - 1] + swap_halves(part) * sin_tiles[i - 1]
                start = PAIR * pair + i * TILE
                qw[span, start : start + TILE] = part.astype(jnp.bfloat16)

    items = [(span, head) for span in spans for head in range(heads)]

    def windows(span, head):
        start = PAIR * (head // 2) + TILE * (head % 2)
        return (
            qw[span, start : start + 2 * TILE],
            kw[span, 2 * TILE * head : 2 * TILE * (head + 1)],
            slice(head * DN, (head + 1) * DN),
        )

    def first_products(span, head):
        query_window, key_window, columns = windows(span, head)
        return (
            dot(key_window, query_window, NT),
            dot(vw[span, columns], grad[span, columns], NT),
        )

    rot_sums = [jnp.zeros((length, TILE), jnp.float32) for _ in spans]
    pending = first_products(*items[0])
    even_part = None
    for index, (span, head) in enumerate(items):
        products = pending
        if index + 1 < len(items):
            pending = first_products(*items[index + 1])
        probs, grad_scores = softmax_grads(*products)
        query_window, key_window, columns = windows(span, head)
        gkv[span, wide + head * DN : wide + (head + 1) * DN] = dot(probs, grad[span, columns]).astype(
            jnp.bfloat16
        )
        key_part = dot(grad_scores, query_window)
        query_part = dot(grad_scores, key_window, TN)
        seq = index // heads
        if head % 2 == 0:
            gkv[span, columns] = key_part[:, :TILE].astype(jnp.bfloat16)
            if rot_out is not None:
                rot_sums[seq] = rot_sums[seq] + rounded(key_part[:, TILE:])
            even_part = query_part
            continue
        turned = pltpu.roll(key_part[:, TILE:], DR, 1)
        gkv[span, columns] = jnp.where(low, pltpu.roll(key_part[:, :TILE], DR, 1), turned).astype(
            jnp.bfloat16
        )
        if rot_out is not None:
            rot_sums[seq] = rot_sums[seq] + rounded(turned)
        parts = [
            even_part[:, :TILE],
            even_part[:, TILE:] + query_part[:, :TILE],
            query_part[:, TILE:],
        ]
        for i in range(3):
            part = parts[i]
            if i > 0:
                part = rounded(part)
                part = part * cos_tiles[i - 1] - swap_halves(part) * sin_tiles[i - 1]
            start = PAIR * (head // 2) + i * TILE
            gq[span, start : start + TILE] = part.astype(jnp.bfloat16)
    if rot_out is not None:
        rot_out[...] = rot_sums[0]


def raw_grads(parts, left, right, sums, previous):
    wide = right.shape[1] // parts
    total = jnp.zeros((8, TILE), jnp.float32)
    for start in range(0, sums[0].shape[0], KL):
        rows = slice(start, start + KL)
        product = dot(left[:, rows], right[...], TN)
        for part in range(parts):
            block = product[:, part * wide : (part + 1) * wide]
            if previous is not None:
                block = block + previous[part][rows, :]
            sums[part][rows, :] = block
            folded = jnp.sum((block * block).reshape(KL // 8, 8, wide), axis=0)
            for column in range(0, wide, TILE):
                total = total + folded[:, column : column + TILE]
    return total


def load_kernel(place, xq, kvt, grad, packed, cotangent, kv_rows, sem):
    half = packed.shape[0]
    rows = pl.ds(pl.multiple_of(place[1] * half, half), half)
    pieces = ((kvt.at[:, rows], kv_rows), (xq.at[rows], packed.at[:, :QL]), (grad, cotangent))
    copies = [pltpu.make_async_copy(*piece, sem.at[i]) for i, piece in enumerate(pieces)]
    for copy in copies:
        copy.start()
    copies[0].wait()
    for block in range(0, KL + DR, TILE):
        stop = min(block + TILE, KL + DR)
        packed[:, QL + block : QL + stop] = kv_rows[block:stop, :].T
    packed[:, LATENT:] = jnp.zeros((half, TILE - DR), jnp.bfloat16)
    for copy in copies[1:]:
        copy.wait()


def own_kernel(n_head, place, xq_in, kvt_in, grad_in, wq_in, wk_in, wv_in, table_in, *refs):
    wq, wk, wv, table, xq, xkv, gq, gkv, keep, send, *refs = refs
    kvt, grad, qw, kw, vw, term, sem = refs
    pieces = (
        (kvt_in, kvt),
        (table_in, table),
        (wk_in, wk),
        (wv_in, wv),
        (xq_in, xq),
        (wq_in, wq),
        (grad_in, grad),
    )
    copies = [pltpu.make_async_copy(*piece, sem.at[i]) for i, piece in enumerate(pieces)]
    for copy in copies:
        copy.start()

    def latents_ready():
        for copy in copies[:4]:
            copy.wait()
        for block in range(0, KL + DR, TILE):
            stop = min(block + TILE, KL + DR)
            xkv[:, block:stop] = kvt[block:stop, :].T

    def queries_ready():
        for copy in copies[4:]:
            copy.wait()

    length = xq.shape[0]
    rot = term.at[:, QL + KL :]
    ready = (latents_ready, queries_ready)
    backward(length, xq, xkv, grad, (wq, wk, wv), table, gq, gkv, qw, kw, vw, rot, ready)
    wide = wk.shape[1]
    term[:, :QL] = dot(gq[...], wq[...], NT)
    term[:, QL : QL + KL] = dot(gkv[:, :wide], wk[...], NT) + dot(gkv[:, wide:], wv[...], NT)
    rows = length // n_head
    chip, core = place[0], place[1]
    masks = [turned_round(k, n_head // 2) for k in range(n_head // 2)]

    def chosen(which):
        starts = [(2 * jnp.bitwise_xor(chip, mask) + which) * rows for mask in masks]
        return jnp.concatenate([term[pl.ds(pl.multiple_of(i, rows), rows), :] for i in starts])

    keep[...] = chosen(core)
    send[...] = chosen(1 - core).astype(jnp.bfloat16)


def fold_kernel(keep, received, stay, go):
    total = keep[...] + received[...].astype(jnp.float32)
    stay[...] = total[: stay.shape[0], :]
    go[...] = total[stay.shape[0] :, :].astype(jnp.bfloat16)


def far_kernel(n_seq, place, *refs):
    blocks, refs = refs[: 3 * n_seq], refs[3 * n_seq :]
    wq, wk, wv, table, xq, xkv, gq, gkv, grad, qw, kw, vw = refs
    half = blocks[0].shape[0]
    length = 2 * half
    core = place[1]
    for s in range(n_seq):
        mine, other, cotangent = blocks[3 * s : 3 * s + 3]
        for source, side in ((mine, core), (other, 1 - core)):
            rows = pl.ds(pl.multiple_of(s * length + side * half, half), half)
            xq[rows, :] = source[:, :QL]
            xkv[rows, :] = source[:, QL:LATENT]
        grad[s * length : (s + 1) * length, :] = cotangent[...]
    ready = (lambda: None, lambda: None)
    backward(length, xq, xkv, grad, (wq, wk, wv), table, gq, gkv, qw, kw, vw, None, ready)


def sums_kernel(parts, first, left, right, *refs):
    previous, sums = (None, refs) if first else (refs[:parts], refs[parts:])
    raw_grads(parts, left, right, sums, previous)


def last_kernel(xq, xkv, gq, gkv, pq, pk, pv, sq, sk, sv, squares):
    squares[...] = raw_grads(1, xq, gq, (sq,), (pq,)) + raw_grads(2, xkv, gkv, (sk, sv), (pk, pv))


def add_kernel(left, right, out):
    out[...] = left[...] + right[...]


def scale_kernel(limit, local, received, sq, sk, sv, *refs):
    *parts, oq, ok, ov, latent_q, latent_kv, bq, bk, bv, sem = refs
    total = parts[0][...]
    for part in parts[1:]:
        total = total + part[...]
    total = jnp.sum(total, keepdims=True)
    factor = jnp.minimum(1.0, limit / jnp.sqrt(total + eps))
    copies = []
    for source, buffer, out in ((sq, bq, oq), (sk, bk, ok), (sv, bv, ov)):
        for start in range(0, source.shape[0], 256):
            rows = slice(start, start + 256)
            buffer[rows, :] = (source[rows, :] * factor).astype(jnp.bfloat16)
            copy = pltpu.make_async_copy(buffer.at[rows], out.at[rows], sem.at[len(copies)])
            copy.start()
            copies.append(copy)
    terms = local[...] + received[...].astype(jnp.float32)
    latent_q[...] = terms[:, :QL]
    latent_kv[...] = terms[:, QL:LATENT]
    for copy in copies:
        copy.wait()


def vmem(count):
    return [pl.BlockSpec(memory_space=pltpu.VMEM)] * count


def hbm(count):
    return [pl.BlockSpec(memory_space=pltpu.HBM)] * count


def params():
    return pltpu.CompilerParams(vmem_limit_bytes=VMEM_LIMIT)


def free():
    return pl.CostEstimate(flops=0, bytes_accessed=0, transcendentals=0)


def struct(shape, dtype):
    return jax.ShapeDtypeStruct(shape, dtype)


def exchange(value, axis, size, k):
    return lax.ppermute(value, axis, [(i, i ^ k) for i in range(size)])


def far_away(value):
    return pltpu.with_memory_space_constraint(value, pltpu.HBM)


def turned_round(mask, n_dp):
    bits = n_dp.bit_length() - 1
    return sum(((mask >> i) & 1) << (bits - 1 - i) for i in range(bits))


def across(value, n_dp, n_head, mask):
    masks = (mask, turned_round(mask, n_dp))
    pairs = [
        (d * n_head + h, (d ^ masks[h % 2]) * n_head + h) for d in range(n_dp) for h in range(n_head)
    ]
    return lax.ppermute(value, ("dp", "head"), pairs)


def per_device(n_dp, n_head, query_latent, kv_latent, out_grad, query_up, key_up, value_up):
    length = query_latent.shape[0]
    half = length // 2
    wide_q, wide_k = query_up.shape[1], key_up.shape[1]
    heads = wide_k // DN
    index = lax.axis_index("head")
    place = jnp.stack([index // 2, index % 2]).astype(jnp.int32)
    table = jnp.asarray(rotary_tables(length))
    smem = [pl.BlockSpec(memory_space=pltpu.SMEM)]
    inputs = [far_away(value) for value in (query_latent, kv_latent.T, out_grad)]
    width = QL + KL + TILE

    packed, cotangent = pl.pallas_call(
        load_kernel,
        out_shape=(
            pltpu.VMEM((half, width), jnp.bfloat16),
            pltpu.VMEM((length, wide_k), jnp.bfloat16),
        ),
        in_specs=smem + hbm(3),
        out_specs=vmem(2),
        scratch_shapes=[pltpu.VMEM((KL + DR, half), jnp.bfloat16), pltpu.SemaphoreType.DMA((3,))],
        compiler_params=params(),
        cost_estimate=free(),
        name="load",
    )(place, *inputs)
    packed, place = lax.optimization_barrier((packed, place))
    singles = [1 << i for i in reversed(range(n_dp.bit_length() - 1))]
    cotangents = {k: across(cotangent, n_dp, n_head, k) for k in singles}
    received = {k: across(packed, n_dp, n_head, k) for k in singles}

    def rows_shape(rows):
        widths = (QL, KL + DR, wide_q, 2 * wide_k)
        return tuple(pltpu.VMEM((rows, width), jnp.bfloat16) for width in widths)

    def scratch(rows):
        widths = (wide_k, wide_q, 2 * TILE * heads, wide_k)
        return [pltpu.VMEM((rows, width), jnp.bfloat16) for width in widths]

    weights_shape = tuple(
        pltpu.VMEM(shape, jnp.bfloat16) for shape in ((QL, wide_q), (KL, wide_k), (KL, wide_k))
    )
    sums_shape = tuple(pltpu.VMEM(w.shape, jnp.float32) for w in weights_shape)
    *outs, keep, send = pl.pallas_call(
        functools.partial(own_kernel, n_head),
        out_shape=(
            *weights_shape,
            pltpu.VMEM(table.shape, jnp.float32),
            *rows_shape(length),
            struct((half, width), jnp.float32),
            struct((half, width), jnp.bfloat16),
        ),
        in_specs=smem + hbm(7),
        out_specs=vmem(10),
        scratch_shapes=[pltpu.VMEM((KL + DR, length), jnp.bfloat16)]
        + scratch(length)
        + [pltpu.VMEM((length, width), jnp.float32), pltpu.SemaphoreType.DMA((7,))],
        compiler_params=params(),
        cost_estimate=free(),
        name="own",
    )(place, *inputs, *[far_away(value) for value in (query_up, key_up, value_up, table)])
    weights, found = outs[:4], outs[4:]

    rows = length // n_head
    squares_shape = struct((8, TILE), jnp.float32)

    def add_sums(left, right, shapes, sums):
        return list(
            pl.pallas_call(
                functools.partial(sums_kernel, len(shapes), not sums),
                out_shape=shapes,
                in_specs=vmem(2 + len(sums)),
                out_specs=vmem(len(shapes)),
                input_output_aliases={2 + i: i for i in range(len(sums))},
                compiler_params=params(),
                cost_estimate=free(),
                name="sums",
            )(left, right, *sums)
        )

    def add(left, right):
        return pl.pallas_call(
            add_kernel,
            out_shape=squares_shape,
            in_specs=vmem(2),
            out_specs=pl.BlockSpec(memory_space=pltpu.VMEM),
            compiler_params=params(),
            cost_estimate=free(),
            name="add",
        )(left, right)

    sums = add_sums(found[0], found[2], sums_shape[:1], [])
    sums += add_sums(found[1], found[3], sums_shape[1:], [])

    def fold(keep, received):
        half_shape = (keep.shape[0] // 2, width)
        return pl.pallas_call(
            fold_kernel,
            out_shape=(struct(half_shape, jnp.float32), struct(half_shape, jnp.bfloat16)),
            in_specs=vmem(2),
            out_specs=vmem(2),
            compiler_params=params(),
            cost_estimate=free(),
            name="fold",
        )(keep, received)

    stay, go = fold(keep, exchange(send, "head", n_head, 1))
    bits = [2 << i for i in range(n_head.bit_length() - 2)]
    for bit in bits[:-2]:
        stay, go = fold(stay, exchange(go, "head", n_head, bit))
    came = exchange(go, "head", n_head, bits[-2])

    values = [received[k] for k in singles]
    *values, sums[0], sums[2] = lax.optimization_barrier((*values, sums[0], sums[2]))
    received = dict(zip(singles, values))
    values = [cotangents[k] for k in singles]
    relayed, *values = lax.optimization_barrier((received, *values))
    cotangents = dict(zip(singles, values))
    for k in range(3, n_dp):
        if k not in received:
            relayed[k] = across(relayed[k & (k - 1)], n_dp, n_head, k & -k)
            received[k] = relayed[k]
            cotangents[k] = across(cotangents[k & (k - 1)], n_dp, n_head, k & -k)

    def swapped(k):
        return exchange(received[turned_round(k, n_dp)], "head", n_head, 1)

    groups = [(1, 2)] + [(k,) for k in range(3, n_dp)]
    for group in groups:
        n_seq = len(group)
        blocks = []
        for k in group:
            blocks += [received[k], swapped(k), cotangents[k]]
        if group is not groups[0]:
            blocks[1], sums[1] = lax.optimization_barrier((blocks[1], sums[1]))
        found = list(
            pl.pallas_call(
                functools.partial(far_kernel, n_seq),
                out_shape=rows_shape(n_seq * length),
                in_specs=smem + vmem(len(blocks) + 4),
                out_specs=vmem(4),
                scratch_shapes=scratch(n_seq * length),
                compiler_params=params(),
                cost_estimate=free(),
                name="far",
            )(place, *blocks, *weights)
        )
        if group is groups[-1]:
            break
        k = groups[groups.index(group) + 1][0]
        if group is groups[0]:
            came, found[3] = lax.optimization_barrier((came, found[3]))
            stay, go = fold(stay, came)
            received[k], go, found[2], found[3] = lax.optimization_barrier(
                (received[k], go, found[2], found[3])
            )
            terms = [stay, exchange(go, "head", n_head, bits[-1])]
        else:
            received[k], found[2], found[3] = lax.optimization_barrier(
                (received[k], found[2], found[3])
            )
        sums[:1] = add_sums(found[0], found[2], sums_shape[:1], sums[:1])
        sums[1:] = add_sums(found[1], found[3], sums_shape[1:], sums[1:])

    *sums, squares = pl.pallas_call(
        last_kernel,
        out_shape=(*sums_shape, squares_shape),
        in_specs=vmem(4 + 3),
        out_specs=vmem(4),
        input_output_aliases={4: 0, 5: 1, 6: 2},
        compiler_params=params(),
        cost_estimate=free(),
        name="last",
    )(*found, *sums)

    count = (QL * wide_q + 2 * KL * wide_k) * n_head
    limit = max_rms * count**0.5
    squares = add(squares, exchange(squares, "head", n_head, 1))
    squares, terms[1] = lax.optimization_barrier((squares, terms[1]))
    parts = [squares] + [exchange(squares, "head", n_head, 2 * k) for k in range(1, n_head // 2)]
    *scaled, latent_q, latent_kv = pl.pallas_call(
        functools.partial(scale_kernel, limit),
        out_shape=(
            *[struct(w.shape, jnp.bfloat16) for w in weights_shape],
            struct((rows, QL), jnp.float32),
            struct((rows, KL + DR), jnp.float32),
        ),
        in_specs=vmem(2 + 3 + len(parts)),
        out_specs=hbm(3) + vmem(2),
        scratch_shapes=list(weights_shape)
        + [pltpu.SemaphoreType.DMA(((QL + 2 * KL) // 256,))],
        compiler_params=params(),
        cost_estimate=free(),
        name="scale",
    )(*terms, *sums, *parts)
    return (latent_q, latent_kv, *scaled)


def solution(mesh):
    placed = (
        P("dp", None),
        P("dp", None),
        P("dp", "head"),
        P(None, "head"),
        P(None, "head"),
        P(None, "head"),
    )
    return jax.shard_map(
        functools.partial(per_device, mesh.shape["dp"], mesh.shape["head"]),
        mesh=mesh,
        in_specs=placed,
        out_specs=(
            P(("dp", "head"), None),
            P(("dp", "head"), None),
            P(None, "head"),
            P(None, "head"),
            P(None, "head"),
        ),
        check_vma=False,
    )
```

```python
import functools

import jax
import jax.numpy as jnp
import numpy as np
from jax import lax
from jax.experimental import pallas as pl
from jax.experimental.pallas import tpu as pltpu
from jax.sharding import PartitionSpec as P

QL = 1536
KL = 512
DN = 128
DR = 64
TILE = 128
WIDTH = DN + DR
PAIR = 2 * WIDTH
LATENT = QL + KL + DR

max_rms = 1.0
eps = 1e-06
VMEM_LIMIT = 32 * 2**20

NT = (((1,), (1,)), ((), ()))
TN = (((0,), (0,)), ((), ()))


def dot(left, right, dims=(((1,), (0,)), ((), ()))):
    return lax.dot_general(left, right, dims, preferred_element_type=jnp.float32)


def rotary_tables(length):
    half = DR // 2
    freqs = np.float32(10000.0) ** (
        np.float32(-2.0) * np.arange(half, dtype=np.float32) / np.float32(DR)
    )
    angle = np.arange(length, dtype=np.float32)[:, None] * freqs.astype(np.float32)[None, :]
    cosine, sine = np.cos(angle), np.sin(angle)
    ones, zeros = np.ones((length, DR), np.float32), np.zeros((length, DR), np.float32)
    return np.concatenate([cosine, cosine, ones, -sine, sine, zeros], axis=1)


def swap_halves(tile):
    lane = lax.broadcasted_iota(jnp.int32, tile.shape, 1)
    first = lane % DR < DR // 2
    return jnp.where(
        first, pltpu.roll(tile, TILE - DR // 2, 1), pltpu.roll(tile, DR // 2, 1)
    )


def rounded(values):
    return values.astype(jnp.bfloat16).astype(jnp.float32)


def softmax_grads(scores, grad_probs):
    length = scores.shape[0]
    block = length // 2
    scale = 1.0 / (DN + DR) ** 0.5
    key = lax.broadcasted_iota(jnp.int32, (block, block), 0)
    query = lax.broadcasted_iota(jnp.int32, (block, block), 1)
    allowed = key <= query
    grad_probs = rounded(grad_probs)
    probs_columns, grads_columns = [], []
    for column in range(2):
        columns = slice(column * block, (column + 1) * block)
        parts = [scores[:block, columns], scores[block:, columns]][: column + 1]
        parts[-1] = jnp.where(allowed, parts[-1], -jnp.inf)
        tops = [jnp.max(part, axis=0, keepdims=True) for part in parts]
        top = tops[0] if column == 0 else jnp.maximum(*tops)
        parts = [jnp.exp((part - top) * scale) for part in parts]
        sums = [jnp.sum(part, axis=0, keepdims=True) for part in parts]
        inverse = 1.0 / (sums[0] if column == 0 else sums[0] + sums[1])
        parts = [part * inverse for part in parts]
        grads = [grad_probs[:block, columns], grad_probs[block:, columns]][: column + 1]
        means = [jnp.sum(g * p, axis=0, keepdims=True) for g, p in zip(grads, parts)]
        mean = means[0] if column == 0 else means[0] + means[1]
        grads = [(p * (g - mean) * scale).astype(jnp.bfloat16) for g, p in zip(grads, parts)]
        parts = [p.astype(jnp.bfloat16) for p in parts]
        if column == 0:
            parts.append(jnp.zeros((block, block), jnp.bfloat16))
            grads.append(jnp.zeros((block, block), jnp.bfloat16))
        probs_columns.append(jnp.concatenate(parts, axis=0))
        grads_columns.append(jnp.concatenate(grads, axis=0))
    return jnp.concatenate(probs_columns, axis=1), jnp.concatenate(grads_columns, axis=1)


def backward(length, xq, xkv, grad, weights, table, gq, gkv, qw, kw, vw, rot_out, ready):
    wq, wk, wv = weights
    n_seq = xq.shape[0] // length
    wide = wk.shape[1]
    heads = wide // DN
    low = lax.broadcasted_iota(jnp.int32, (length, TILE), 1) < DR
    spans = [slice(s * length, (s + 1) * length) for s in range(n_seq)]

    ready[0]()
    cos_low, sin_low = table[:, :TILE], table[:, TILE:]
    cos_tiles = (cos_low, pltpu.roll(cos_low, DR, 1))
    sin_tiles = (sin_low, pltpu.roll(sin_low, DR, 1))
    latent = xkv[:, :KL]
    for pair in range(heads // 2):
        columns = slice(2 * DN * pair, 2 * DN * (pair + 1))
        keys = dot(latent, wk[:, columns])
        vw[:, columns] = dot(latent, wv[:, columns]).astype(jnp.bfloat16)
        for span in spans:
            rot = jnp.concatenate(
                [xkv[span, KL : KL + DR].astype(jnp.float32), jnp.zeros((length, DR), jnp.float32)],
                axis=1,
            )
            odd = pltpu.roll(keys[span, DN:], DR, 1)
            tiles = (
                keys[span, :DN],
                rot,
                jnp.where(low, 0.0, odd),
                jnp.where(low, odd, pltpu.roll(rot, DR, 1)),
            )
            for i, tile in enumerate(tiles):
                start = (4 * pair + i) * TILE
                kw[span, start : start + TILE] = tile.astype(jnp.bfloat16)
    ready[1]()
    for pair in range(heads // 2):
        queries = dot(xq[...], wq[:, PAIR * pair : PAIR * (pair + 1)])
        for span in spans:
            for i in range(3):
                part = rounded(queries[span, i * TILE : (i + 1) * TILE])
                if i > 0:
                    part = part * cos_tiles[i - 1] + swap_halves(part) * sin_tiles[i - 1]
                start = PAIR * pair + i * TILE
                qw[span, start : start + TILE] = part.astype(jnp.bfloat16)

    items = [(span, head) for span in spans for head in range(heads)]

    def windows(span, head):
        start = PAIR * (head // 2) + TILE * (head % 2)
        return (
            qw[span, start : start + 2 * TILE],
            kw[span, 2 * TILE * head : 2 * TILE * (head + 1)],
            slice(head * DN, (head + 1) * DN),
        )

    def first_products(span, head):
        query_window, key_window, columns = windows(span, head)
        return (
            dot(key_window, query_window, NT),
            dot(vw[span, columns], grad[span, columns], NT),
        )

    rot_sums = [jnp.zeros((length, TILE), jnp.float32) for _ in spans]
    pending = first_products(*items[0])
    even_part = None
    for index, (span, head) in enumerate(items):
        products = pending
        if index + 1 < len(items):
            pending = first_products(*items[index + 1])
        probs, grad_scores = softmax_grads(*products)
        query_window, key_window, columns = windows(span, head)
        gkv[span, wide + head * DN : wide + (head + 1) * DN] = dot(probs, grad[span, columns]).astype(
            jnp.bfloat16
        )
        key_part = dot(grad_scores, query_window)
        query_part = dot(grad_scores, key_window, TN)
        seq = index // heads
        if head % 2 == 0:
            gkv[span, columns] = key_part[:, :TILE].astype(jnp.bfloat16)
            if rot_out is not None:
                rot_sums[seq] = rot_sums[seq] + rounded(key_part[:, TILE:])
            even_part = query_part
            continue
        turned = pltpu.roll(key_part[:, TILE:], DR, 1)
        gkv[span, columns] = jnp.where(low, pltpu.roll(key_part[:, :TILE], DR, 1), turned).astype(
            jnp.bfloat16
        )
        if rot_out is not None:
            rot_sums[seq] = rot_sums[seq] + rounded(turned)
        parts = [
            even_part[:, :TILE],
            even_part[:, TILE:] + query_part[:, :TILE],
            query_part[:, TILE:],
        ]
        for i in range(3):
            part = parts[i]
            if i > 0:
                part = rounded(part)
                part = part * cos_tiles[i - 1] - swap_halves(part) * sin_tiles[i - 1]
            start = PAIR * (head // 2) + i * TILE
            gq[span, start : start + TILE] = part.astype(jnp.bfloat16)
    if rot_out is not None:
        rot_out[...] = rot_sums[0]


def raw_grads(parts, left, right, sums, previous):
    wide = right.shape[1] // parts
    total = jnp.zeros((8, TILE), jnp.float32)
    for start in range(0, sums[0].shape[0], KL):
        rows = slice(start, start + KL)
        product = dot(left[:, rows], right[...], TN)
        for part in range(parts):
            block = product[:, part * wide : (part + 1) * wide]
            if previous is not None:
                block = block + previous[part][rows, :]
            sums[part][rows, :] = block
            folded = jnp.sum((block * block).reshape(KL // 8, 8, wide), axis=0)
            for column in range(0, wide, TILE):
                total = total + folded[:, column : column + TILE]
    return total


def load_kernel(place, xq, kvt, grad, packed, cotangent, kv_rows, sem):
    half = packed.shape[0]
    rows = pl.ds(pl.multiple_of(place[1] * half, half), half)
    pieces = ((kvt.at[:, rows], kv_rows), (xq.at[rows], packed.at[:, :QL]), (grad, cotangent))
    copies = [pltpu.make_async_copy(*piece, sem.at[i]) for i, piece in enumerate(pieces)]
    for copy in copies:
        copy.start()
    copies[0].wait()
    for block in range(0, KL + DR, TILE):
        stop = min(block + TILE, KL + DR)
        packed[:, QL + block : QL + stop] = kv_rows[block:stop, :].T
    packed[:, LATENT:] = jnp.zeros((half, TILE - DR), jnp.bfloat16)
    for copy in copies[1:]:
        copy.wait()


def own_kernel(n_head, place, xq_in, kvt_in, grad_in, wq_in, wk_in, wv_in, table_in, *refs):
    wq, wk, wv, table, xq, xkv, gq, gkv, keep, send, *refs = refs
    kvt, grad, qw, kw, vw, term, sem = refs
    pieces = (
        (kvt_in, kvt),
        (table_in, table),
        (wk_in, wk),
        (wv_in, wv),
        (xq_in, xq),
        (wq_in, wq),
        (grad_in, grad),
    )
    copies = [pltpu.make_async_copy(*piece, sem.at[i]) for i, piece in enumerate(pieces)]
    for copy in copies:
        copy.start()

    def latents_ready():
        for copy in copies[:4]:
            copy.wait()
        for block in range(0, KL + DR, TILE):
            stop = min(block + TILE, KL + DR)
            xkv[:, block:stop] = kvt[block:stop, :].T

    def queries_ready():
        for copy in copies[4:]:
            copy.wait()

    length = xq.shape[0]
    rot = term.at[:, QL + KL :]
    ready = (latents_ready, queries_ready)
    backward(length, xq, xkv, grad, (wq, wk, wv), table, gq, gkv, qw, kw, vw, rot, ready)
    wide = wk.shape[1]
    term[:, :QL] = dot(gq[...], wq[...], NT)
    term[:, QL : QL + KL] = dot(gkv[:, :wide], wk[...], NT) + dot(gkv[:, wide:], wv[...], NT)
    rows = length // n_head
    chip, core = place[0], place[1]
    masks = [turned_round(k, n_head // 2) for k in range(n_head // 2)]

    def chosen(which):
        starts = [(2 * jnp.bitwise_xor(chip, mask) + which) * rows for mask in masks]
        return jnp.concatenate([term[pl.ds(pl.multiple_of(i, rows), rows), :] for i in starts])

    keep[...] = chosen(core)
    send[...] = chosen(1 - core).astype(jnp.bfloat16)


def fold_kernel(keep, received, stay, go):
    total = keep[...] + received[...].astype(jnp.float32)
    stay[...] = total[: stay.shape[0], :]
    go[...] = total[stay.shape[0] :, :].astype(jnp.bfloat16)


def far_kernel(n_seq, place, *refs):
    blocks, refs = refs[: 3 * n_seq], refs[3 * n_seq :]
    wq, wk, wv, table, xq, xkv, gq, gkv, grad, qw, kw, vw = refs
    half = blocks[0].shape[0]
    length = 2 * half
    core = place[1]
    for s in range(n_seq):
        mine, other, cotangent = blocks[3 * s : 3 * s + 3]
        for source, side in ((mine, core), (other, 1 - core)):
            rows = pl.ds(pl.multiple_of(s * length + side * half, half), half)
            xq[rows, :] = source[:, :QL]
            xkv[rows, :] = source[:, QL:LATENT]
        grad[s * length : (s + 1) * length, :] = cotangent[...]
    ready = (lambda: None, lambda: None)
    backward(length, xq, xkv, grad, (wq, wk, wv), table, gq, gkv, qw, kw, vw, None, ready)


def sums_kernel(parts, first, left, right, *refs):
    previous, sums = (None, refs) if first else (refs[:parts], refs[parts:])
    raw_grads(parts, left, right, sums, previous)


def last_kernel(xq, xkv, gq, gkv, pq, pk, pv, sq, sk, sv, squares):
    squares[...] = raw_grads(1, xq, gq, (sq,), (pq,)) + raw_grads(2, xkv, gkv, (sk, sv), (pk, pv))


def add_kernel(left, right, out):
    out[...] = left[...] + right[...]


def scale_kernel(limit, local, received, sq, sk, sv, *refs):
    *parts, oq, ok, ov, latent_q, latent_kv, bq, bk, bv, bl, br, sem = refs
    terms = local[...] + received[...].astype(jnp.float32)
    bl[...] = terms[:, :QL]
    br[...] = terms[:, QL:LATENT]
    copies = []
    for buffer, out in ((bl, latent_q), (br, latent_kv)):
        copies.append(pltpu.make_async_copy(buffer, out, sem.at[len(copies)]))
        copies[-1].start()
    total = parts[0][...]
    for part in parts[1:]:
        total = total + part[...]
    total = jnp.sum(total, keepdims=True)
    factor = jnp.minimum(1.0, limit / jnp.sqrt(total + eps))
    for source, buffer, out in ((sq, bq, oq), (sk, bk, ok), (sv, bv, ov)):
        for start in range(0, source.shape[0], 128):
            rows = slice(start, start + 128)
            buffer[rows, :] = (source[rows, :] * factor).astype(jnp.bfloat16)
            copy = pltpu.make_async_copy(buffer.at[rows], out.at[rows], sem.at[len(copies)])
            copy.start()
            copies.append(copy)
    for copy in copies:
        copy.wait()


def vmem(count):
    return [pl.BlockSpec(memory_space=pltpu.VMEM)] * count


def hbm(count):
    return [pl.BlockSpec(memory_space=pltpu.HBM)] * count


def params():
    return pltpu.CompilerParams(vmem_limit_bytes=VMEM_LIMIT)


def free():
    return pl.CostEstimate(flops=0, bytes_accessed=0, transcendentals=0)


def struct(shape, dtype):
    return jax.ShapeDtypeStruct(shape, dtype)


def exchange(value, axis, size, k):
    return lax.ppermute(value, axis, [(i, i ^ k) for i in range(size)])


def far_away(value):
    return pltpu.with_memory_space_constraint(value, pltpu.HBM)


def turned_round(mask, n_dp):
    bits = n_dp.bit_length() - 1
    return sum(((mask >> i) & 1) << (bits - 1 - i) for i in range(bits))


def across(value, n_dp, n_head, mask):
    masks = (mask, turned_round(mask, n_dp))
    pairs = [
        (d * n_head + h, (d ^ masks[h % 2]) * n_head + h) for d in range(n_dp) for h in range(n_head)
    ]
    return lax.ppermute(value, ("dp", "head"), pairs)


def per_device(n_dp, n_head, query_latent, kv_latent, out_grad, query_up, key_up, value_up):
    length = query_latent.shape[0]
    half = length // 2
    wide_q, wide_k = query_up.shape[1], key_up.shape[1]
    heads = wide_k // DN
    index = lax.axis_index("head")
    place = jnp.stack([index // 2, index % 2]).astype(jnp.int32)
    table = jnp.asarray(rotary_tables(length))
    smem = [pl.BlockSpec(memory_space=pltpu.SMEM)]
    inputs = [far_away(value) for value in (query_latent, kv_latent.T, out_grad)]
    width = QL + KL + TILE

    packed, cotangent = pl.pallas_call(
        load_kernel,
        out_shape=(
            pltpu.VMEM((half, width), jnp.bfloat16),
            pltpu.VMEM((length, wide_k), jnp.bfloat16),
        ),
        in_specs=smem + hbm(3),
        out_specs=vmem(2),
        scratch_shapes=[pltpu.VMEM((KL + DR, half), jnp.bfloat16), pltpu.SemaphoreType.DMA((3,))],
        compiler_params=params(),
        cost_estimate=free(),
        name="load",
    )(place, *inputs)
    packed, place = lax.optimization_barrier((packed, place))
    singles = [1 << i for i in reversed(range(n_dp.bit_length() - 1))]
    cotangents = {k: across(cotangent, n_dp, n_head, k) for k in singles}
    received = {k: across(packed, n_dp, n_head, k) for k in singles}

    def rows_shape(rows):
        widths = (QL, KL + DR, wide_q, 2 * wide_k)
        return tuple(pltpu.VMEM((rows, width), jnp.bfloat16) for width in widths)

    def scratch(rows):
        widths = (wide_k, wide_q, 2 * TILE * heads, wide_k)
        return [pltpu.VMEM((rows, width), jnp.bfloat16) for width in widths]

    weights_shape = tuple(
        pltpu.VMEM(shape, jnp.bfloat16) for shape in ((QL, wide_q), (KL, wide_k), (KL, wide_k))
    )
    sums_shape = tuple(pltpu.VMEM(w.shape, jnp.float32) for w in weights_shape)
    *outs, keep, send = pl.pallas_call(
        functools.partial(own_kernel, n_head),
        out_shape=(
            *weights_shape,
            pltpu.VMEM(table.shape, jnp.float32),
            *rows_shape(length),
            struct((half, width), jnp.float32),
            struct((half, width), jnp.bfloat16),
        ),
        in_specs=smem + hbm(7),
        out_specs=vmem(10),
        scratch_shapes=[pltpu.VMEM((KL + DR, length), jnp.bfloat16)]
        + scratch(length)
        + [pltpu.VMEM((length, width), jnp.float32), pltpu.SemaphoreType.DMA((7,))],
        compiler_params=params(),
        cost_estimate=free(),
        name="own",
    )(place, *inputs, *[far_away(value) for value in (query_up, key_up, value_up, table)])
    weights, found = outs[:4], outs[4:]

    rows = length // n_head
    squares_shape = struct((8, TILE), jnp.float32)

    def add_sums(left, right, shapes, sums):
        return list(
            pl.pallas_call(
                functools.partial(sums_kernel, len(shapes), not sums),
                out_shape=shapes,
                in_specs=vmem(2 + len(sums)),
                out_specs=vmem(len(shapes)),
                input_output_aliases={2 + i: i for i in range(len(sums))},
                compiler_params=params(),
                cost_estimate=free(),
                name="sums",
            )(left, right, *sums)
        )

    def add(left, right):
        return pl.pallas_call(
            add_kernel,
            out_shape=squares_shape,
            in_specs=vmem(2),
            out_specs=pl.BlockSpec(memory_space=pltpu.VMEM),
            compiler_params=params(),
            cost_estimate=free(),
            name="add",
        )(left, right)

    sums = add_sums(found[0], found[2], sums_shape[:1], [])
    sums += add_sums(found[1], found[3], sums_shape[1:], [])

    def fold(keep, received):
        half_shape = (keep.shape[0] // 2, width)
        return pl.pallas_call(
            fold_kernel,
            out_shape=(struct(half_shape, jnp.float32), struct(half_shape, jnp.bfloat16)),
            in_specs=vmem(2),
            out_specs=vmem(2),
            compiler_params=params(),
            cost_estimate=free(),
            name="fold",
        )(keep, received)

    stay, go = fold(keep, exchange(send, "head", n_head, 1))
    bits = [2 << i for i in range(n_head.bit_length() - 2)]
    for bit in bits[:-2]:
        stay, go = fold(stay, exchange(go, "head", n_head, bit))
    came = exchange(go, "head", n_head, bits[-2])

    values = [received[k] for k in singles]
    *values, sums[0], sums[2] = lax.optimization_barrier((*values, sums[0], sums[2]))
    received = dict(zip(singles, values))
    values = [cotangents[k] for k in singles]
    relayed, *values = lax.optimization_barrier((received, *values))
    cotangents = dict(zip(singles, values))
    for k in range(3, n_dp):
        if k not in received:
            relayed[k] = across(relayed[k & (k - 1)], n_dp, n_head, k & -k)
            received[k] = relayed[k]
            cotangents[k] = across(cotangents[k & (k - 1)], n_dp, n_head, k & -k)

    def swapped(k):
        return exchange(received[turned_round(k, n_dp)], "head", n_head, 1)

    groups = [(1, 2)] + [(k,) for k in range(3, n_dp)]
    for group in groups:
        n_seq = len(group)
        blocks = []
        for k in group:
            blocks += [received[k], swapped(k), cotangents[k]]
        if group is not groups[0]:
            blocks[1], sums[1] = lax.optimization_barrier((blocks[1], sums[1]))
        found = list(
            pl.pallas_call(
                functools.partial(far_kernel, n_seq),
                out_shape=rows_shape(n_seq * length),
                in_specs=smem + vmem(len(blocks) + 4),
                out_specs=vmem(4),
                scratch_shapes=scratch(n_seq * length),
                compiler_params=params(),
                cost_estimate=free(),
                name="far",
            )(place, *blocks, *weights)
        )
        if group is groups[-1]:
            break
        k = groups[groups.index(group) + 1][0]
        if group is groups[0]:
            came, found[3] = lax.optimization_barrier((came, found[3]))
            stay, go = fold(stay, came)
            go, found[2] = lax.optimization_barrier((go, found[2]))
            terms = [stay, exchange(go, "head", n_head, bits[-1])]
        sums[:1] = add_sums(found[0], found[2], sums_shape[:1], sums[:1])
        received[k], cotangents[k], sums[0] = lax.optimization_barrier(
            (received[k], cotangents[k], sums[0])
        )
        sums[1:] = add_sums(found[1], found[3], sums_shape[1:], sums[1:])

    *sums, squares = pl.pallas_call(
        last_kernel,
        out_shape=(*sums_shape, squares_shape),
        in_specs=vmem(4 + 3),
        out_specs=vmem(4),
        input_output_aliases={4: 0, 5: 1, 6: 2},
        compiler_params=params(),
        cost_estimate=free(),
        name="last",
    )(*found, *sums)

    count = (QL * wide_q + 2 * KL * wide_k) * n_head
    limit = max_rms * count**0.5
    squares = add(squares, exchange(squares, "head", n_head, 1))
    squares, terms[1] = lax.optimization_barrier((squares, terms[1]))
    parts = [squares] + [exchange(squares, "head", n_head, 2 * k) for k in range(1, n_head // 2)]
    *scaled, latent_q, latent_kv = pl.pallas_call(
        functools.partial(scale_kernel, limit),
        out_shape=(
            *[struct(w.shape, jnp.bfloat16) for w in weights_shape],
            struct((rows, QL), jnp.float32),
            struct((rows, KL + DR), jnp.float32),
        ),
        in_specs=vmem(2 + 3 + len(parts)),
        out_specs=hbm(5),
        scratch_shapes=list(weights_shape)
        + [
            pltpu.VMEM((rows, QL), jnp.float32),
            pltpu.VMEM((rows, KL + DR), jnp.float32),
            pltpu.SemaphoreType.DMA((2 + (QL + 2 * KL) // 128,)),
        ],
        compiler_params=params(),
        cost_estimate=free(),
        name="scale",
    )(*terms, *sums, *parts)
    return (latent_q, latent_kv, *scaled)


def solution(mesh):
    placed = (
        P("dp", None),
        P("dp", None),
        P("dp", "head"),
        P(None, "head"),
        P(None, "head"),
        P(None, "head"),
    )
    return jax.shard_map(
        functools.partial(per_device, mesh.shape["dp"], mesh.shape["head"]),
        mesh=mesh,
        in_specs=placed,
        out_specs=(
            P(("dp", "head"), None),
            P(("dp", "head"), None),
            P(None, "head"),
            P(None, "head"),
            P(None, "head"),
        ),
        check_vma=False,
    )
```

```python
import functools

import jax
import jax.numpy as jnp
import numpy as np
from jax import lax
from jax.experimental import pallas as pl
from jax.experimental.pallas import tpu as pltpu
from jax.sharding import PartitionSpec as P

QL = 1536
KL = 512
DN = 128
DR = 64
TILE = 128
WIDTH = DN + DR
PAIR = 2 * WIDTH
LATENT = QL + KL + DR

max_rms = 1.0
eps = 1e-06
VMEM_LIMIT = 32 * 2**20

NT = (((1,), (1,)), ((), ()))
TN = (((0,), (0,)), ((), ()))


def dot(left, right, dims=(((1,), (0,)), ((), ()))):
    return lax.dot_general(left, right, dims, preferred_element_type=jnp.float32)


def rotary_tables(length):
    half = DR // 2
    freqs = np.float32(10000.0) ** (
        np.float32(-2.0) * np.arange(half, dtype=np.float32) / np.float32(DR)
    )
    angle = np.arange(length, dtype=np.float32)[:, None] * freqs.astype(np.float32)[None, :]
    cosine, sine = np.cos(angle), np.sin(angle)
    ones, zeros = np.ones((length, DR), np.float32), np.zeros((length, DR), np.float32)
    return np.concatenate([cosine, cosine, ones, -sine, sine, zeros], axis=1)


def swap_halves(tile):
    lane = lax.broadcasted_iota(jnp.int32, tile.shape, 1)
    first = lane % DR < DR // 2
    return jnp.where(
        first, pltpu.roll(tile, TILE - DR // 2, 1), pltpu.roll(tile, DR // 2, 1)
    )


def rounded(values):
    return values.astype(jnp.bfloat16).astype(jnp.float32)


def softmax_grads(scores, grad_probs):
    length = scores.shape[0]
    block = length // 2
    scale = 1.0 / (DN + DR) ** 0.5
    key = lax.broadcasted_iota(jnp.int32, (block, block), 0)
    query = lax.broadcasted_iota(jnp.int32, (block, block), 1)
    allowed = key <= query
    grad_probs = rounded(grad_probs)
    probs_columns, grads_columns = [], []
    for column in range(2):
        columns = slice(column * block, (column + 1) * block)
        parts = [scores[:block, columns], scores[block:, columns]][: column + 1]
        parts[-1] = jnp.where(allowed, parts[-1], -jnp.inf)
        tops = [jnp.max(part, axis=0, keepdims=True) for part in parts]
        top = tops[0] if column == 0 else jnp.maximum(*tops)
        parts = [jnp.exp((part - top) * scale) for part in parts]
        sums = [jnp.sum(part, axis=0, keepdims=True) for part in parts]
        inverse = 1.0 / (sums[0] if column == 0 else sums[0] + sums[1])
        parts = [part * inverse for part in parts]
        grads = [grad_probs[:block, columns], grad_probs[block:, columns]][: column + 1]
        means = [jnp.sum(g * p, axis=0, keepdims=True) for g, p in zip(grads, parts)]
        mean = means[0] if column == 0 else means[0] + means[1]
        grads = [(p * (g - mean) * scale).astype(jnp.bfloat16) for g, p in zip(grads, parts)]
        parts = [p.astype(jnp.bfloat16) for p in parts]
        if column == 0:
            parts.append(jnp.zeros((block, block), jnp.bfloat16))
            grads.append(jnp.zeros((block, block), jnp.bfloat16))
        probs_columns.append(jnp.concatenate(parts, axis=0))
        grads_columns.append(jnp.concatenate(grads, axis=0))
    return jnp.concatenate(probs_columns, axis=1), jnp.concatenate(grads_columns, axis=1)


def backward(length, xq, xkv, grad, weights, table, gq, gkv, qw, kw, vw, rot_out, ready):
    wq, wk, wv = weights
    n_seq = xq.shape[0] // length
    wide = wk.shape[1]
    heads = wide // DN
    low = lax.broadcasted_iota(jnp.int32, (length, TILE), 1) < DR
    spans = [slice(s * length, (s + 1) * length) for s in range(n_seq)]

    ready[0]()
    cos_low, sin_low = table[:, :TILE], table[:, TILE:]
    cos_tiles = (cos_low, pltpu.roll(cos_low, DR, 1))
    sin_tiles = (sin_low, pltpu.roll(sin_low, DR, 1))
    latent = xkv[:, :KL]
    for pair in range(heads // 2):
        columns = slice(2 * DN * pair, 2 * DN * (pair + 1))
        keys = dot(latent, wk[:, columns])
        vw[:, columns] = dot(latent, wv[:, columns]).astype(jnp.bfloat16)
        for span in spans:
            rot = jnp.concatenate(
                [xkv[span, KL : KL + DR].astype(jnp.float32), jnp.zeros((length, DR), jnp.float32)],
                axis=1,
            )
            odd = pltpu.roll(keys[span, DN:], DR, 1)
            tiles = (
                keys[span, :DN],
                rot,
                jnp.where(low, 0.0, odd),
                jnp.where(low, odd, pltpu.roll(rot, DR, 1)),
            )
            for i, tile in enumerate(tiles):
                start = (4 * pair + i) * TILE
                kw[span, start : start + TILE] = tile.astype(jnp.bfloat16)
    ready[1]()
    for pair in range(heads // 2):
        queries = dot(xq[...], wq[:, PAIR * pair : PAIR * (pair + 1)])
        for span in spans:
            for i in range(3):
                part = rounded(queries[span, i * TILE : (i + 1) * TILE])
                if i > 0:
                    part = part * cos_tiles[i - 1] + swap_halves(part) * sin_tiles[i - 1]
                start = PAIR * pair + i * TILE
                qw[span, start : start + TILE] = part.astype(jnp.bfloat16)

    items = [(span, head) for span in spans for head in range(heads)]

    def windows(span, head):
        start = PAIR * (head // 2) + TILE * (head % 2)
        return (
            qw[span, start : start + 2 * TILE],
            kw[span, 2 * TILE * head : 2 * TILE * (head + 1)],
            slice(head * DN, (head + 1) * DN),
        )

    def first_products(span, head):
        query_window, key_window, columns = windows(span, head)
        return (
            dot(key_window, query_window, NT),
            dot(vw[span, columns], grad[span, columns], NT),
        )

    rot_sums = [jnp.zeros((length, TILE), jnp.float32) for _ in spans]
    even_parts = {}

    def last_products(index, probs, grad_scores):
        span, head = items[index]
        query_window, key_window, columns = windows(span, head)
        gkv[span, wide + head * DN : wide + (head + 1) * DN] = dot(probs, grad[span, columns]).astype(
            jnp.bfloat16
        )
        key_part = dot(grad_scores, query_window)
        query_part = dot(grad_scores, key_window, TN)
        seq = index // heads
        if head % 2 == 0:
            gkv[span, columns] = key_part[:, :TILE].astype(jnp.bfloat16)
            if rot_out is not None:
                rot_sums[seq] = rot_sums[seq] + rounded(key_part[:, TILE:])
            even_parts[index + 1] = query_part
            return
        turned = pltpu.roll(key_part[:, TILE:], DR, 1)
        gkv[span, columns] = jnp.where(low, pltpu.roll(key_part[:, :TILE], DR, 1), turned).astype(
            jnp.bfloat16
        )
        if rot_out is not None:
            rot_sums[seq] = rot_sums[seq] + rounded(turned)
        even_part = even_parts.pop(index)
        parts = [
            even_part[:, :TILE],
            even_part[:, TILE:] + query_part[:, :TILE],
            query_part[:, TILE:],
        ]
        for i in range(3):
            part = parts[i]
            if i > 0:
                part = rounded(part)
                part = part * cos_tiles[i - 1] - swap_halves(part) * sin_tiles[i - 1]
            start = PAIR * (head // 2) + i * TILE
            gq[span, start : start + TILE] = part.astype(jnp.bfloat16)

    ahead = [first_products(*item) for item in items[:2]]
    waiting = None
    for index in range(len(items)):
        found = softmax_grads(*ahead.pop(0))
        if index + 2 < len(items):
            ahead.append(first_products(*items[index + 2]))
        if waiting is not None:
            last_products(index - 1, *waiting)
        waiting = found
    last_products(len(items) - 1, *waiting)
    if rot_out is not None:
        rot_out[...] = rot_sums[0]


def raw_grads(parts, left, right, sums, previous):
    wide = right.shape[1] // parts
    total = jnp.zeros((8, TILE), jnp.float32)
    for start in range(0, sums[0].shape[0], KL):
        rows = slice(start, start + KL)
        product = dot(left[:, rows], right[...], TN)
        for part in range(parts):
            block = product[:, part * wide : (part + 1) * wide]
            if previous is not None:
                block = block + previous[part][rows, :]
            sums[part][rows, :] = block
            folded = jnp.sum((block * block).reshape(KL // 8, 8, wide), axis=0)
            for column in range(0, wide, TILE):
                total = total + folded[:, column : column + TILE]
    return total


def load_kernel(place, xq, kvt, grad, packed, cotangent, kv_rows, sem):
    half = packed.shape[0]
    rows = pl.ds(pl.multiple_of(place[1] * half, half), half)
    pieces = ((kvt.at[:, rows], kv_rows), (xq.at[rows], packed.at[:, :QL]), (grad, cotangent))
    copies = [pltpu.make_async_copy(*piece, sem.at[i]) for i, piece in enumerate(pieces)]
    for copy in copies:
        copy.start()
    copies[0].wait()
    for block in range(0, KL + DR, TILE):
        stop = min(block + TILE, KL + DR)
        packed[:, QL + block : QL + stop] = kv_rows[block:stop, :].T
    packed[:, LATENT:] = jnp.zeros((half, TILE - DR), jnp.bfloat16)
    for copy in copies[1:]:
        copy.wait()


def own_kernel(n_head, place, xq_in, kvt_in, grad_in, wq_in, wk_in, wv_in, table_in, *refs):
    wq, wk, wv, table, xq, xkv, gq, gkv, keep, send, *refs = refs
    kvt, grad, qw, kw, vw, term, sem = refs
    pieces = (
        (kvt_in, kvt),
        (table_in, table),
        (wk_in, wk),
        (wv_in, wv),
        (xq_in, xq),
        (wq_in, wq),
        (grad_in, grad),
    )
    copies = [pltpu.make_async_copy(*piece, sem.at[i]) for i, piece in enumerate(pieces)]
    for copy in copies:
        copy.start()

    def latents_ready():
        for copy in copies[:4]:
            copy.wait()
        for block in range(0, KL + DR, TILE):
            stop = min(block + TILE, KL + DR)
            xkv[:, block:stop] = kvt[block:stop, :].T

    def queries_ready():
        for copy in copies[4:]:
            copy.wait()

    length = xq.shape[0]
    rot = term.at[:, QL + KL :]
    ready = (latents_ready, queries_ready)
    backward(length, xq, xkv, grad, (wq, wk, wv), table, gq, gkv, qw, kw, vw, rot, ready)
    wide = wk.shape[1]
    term[:, :QL] = dot(gq[...], wq[...], NT)
    term[:, QL : QL + KL] = dot(gkv[:, :wide], wk[...], NT) + dot(gkv[:, wide:], wv[...], NT)
    rows = length // n_head
    chip, core = place[0], place[1]
    masks = [turned_round(k, n_head // 2) for k in range(n_head // 2)]

    def chosen(which):
        starts = [(2 * jnp.bitwise_xor(chip, mask) + which) * rows for mask in masks]
        return jnp.concatenate([term[pl.ds(pl.multiple_of(i, rows), rows), :] for i in starts])

    keep[...] = chosen(core)
    send[...] = chosen(1 - core).astype(jnp.bfloat16)


def fold_kernel(keep, received, stay, go):
    total = keep[...] + received[...].astype(jnp.float32)
    stay[...] = total[: stay.shape[0], :]
    go[...] = total[stay.shape[0] :, :].astype(jnp.bfloat16)


def far_kernel(n_seq, place, *refs):
    blocks, refs = refs[: 3 * n_seq], refs[3 * n_seq :]
    wq, wk, wv, table, xq, xkv, gq, gkv, grad, qw, kw, vw = refs
    half = blocks[0].shape[0]
    length = 2 * half
    core = place[1]
    for s in range(n_seq):
        mine, other, cotangent = blocks[3 * s : 3 * s + 3]
        for source, side in ((mine, core), (other, 1 - core)):
            rows = pl.ds(pl.multiple_of(s * length + side * half, half), half)
            xq[rows, :] = source[:, :QL]
            xkv[rows, :] = source[:, QL:LATENT]
        grad[s * length : (s + 1) * length, :] = cotangent[...]
    ready = (lambda: None, lambda: None)
    backward(length, xq, xkv, grad, (wq, wk, wv), table, gq, gkv, qw, kw, vw, None, ready)


def sums_kernel(parts, first, left, right, *refs):
    previous, sums = (None, refs) if first else (refs[:parts], refs[parts:])
    raw_grads(parts, left, right, sums, previous)


def last_kernel(xq, xkv, gq, gkv, pq, pk, pv, sq, sk, sv, squares):
    squares[...] = raw_grads(1, xq, gq, (sq,), (pq,)) + raw_grads(2, xkv, gkv, (sk, sv), (pk, pv))


def add_kernel(left, right, out):
    out[...] = left[...] + right[...]


def scale_kernel(limit, local, received, sq, sk, sv, *refs):
    *parts, oq, ok, ov, latent_q, latent_kv, bq, bk, bv, bl, br, sem = refs
    terms = local[...] + received[...].astype(jnp.float32)
    bl[...] = terms[:, :QL]
    br[...] = terms[:, QL:LATENT]
    copies = []
    for buffer, out in ((bl, latent_q), (br, latent_kv)):
        copies.append(pltpu.make_async_copy(buffer, out, sem.at[len(copies)]))
        copies[-1].start()
    total = parts[0][...]
    for part in parts[1:]:
        total = total + part[...]
    total = jnp.sum(total, keepdims=True)
    factor = jnp.minimum(1.0, limit / jnp.sqrt(total + eps))
    for source, buffer, out in ((sq, bq, oq), (sk, bk, ok), (sv, bv, ov)):
        for start in range(0, source.shape[0], 128):
            rows = slice(start, start + 128)
            buffer[rows, :] = (source[rows, :] * factor).astype(jnp.bfloat16)
            copy = pltpu.make_async_copy(buffer.at[rows], out.at[rows], sem.at[len(copies)])
            copy.start()
            copies.append(copy)
    for copy in copies:
        copy.wait()


def vmem(count):
    return [pl.BlockSpec(memory_space=pltpu.VMEM)] * count


def hbm(count):
    return [pl.BlockSpec(memory_space=pltpu.HBM)] * count


def params():
    return pltpu.CompilerParams(vmem_limit_bytes=VMEM_LIMIT)


def free():
    return pl.CostEstimate(flops=0, bytes_accessed=0, transcendentals=0)


def struct(shape, dtype):
    return jax.ShapeDtypeStruct(shape, dtype)


def exchange(value, axis, size, k):
    return lax.ppermute(value, axis, [(i, i ^ k) for i in range(size)])


def far_away(value):
    return pltpu.with_memory_space_constraint(value, pltpu.HBM)


def turned_round(mask, n_dp):
    bits = n_dp.bit_length() - 1
    return sum(((mask >> i) & 1) << (bits - 1 - i) for i in range(bits))


def across(value, n_dp, n_head, mask):
    masks = (mask, turned_round(mask, n_dp))
    pairs = [
        (d * n_head + h, (d ^ masks[h % 2]) * n_head + h) for d in range(n_dp) for h in range(n_head)
    ]
    return lax.ppermute(value, ("dp", "head"), pairs)


def per_device(n_dp, n_head, query_latent, kv_latent, out_grad, query_up, key_up, value_up):
    length = query_latent.shape[0]
    half = length // 2
    wide_q, wide_k = query_up.shape[1], key_up.shape[1]
    heads = wide_k // DN
    index = lax.axis_index("head")
    place = jnp.stack([index // 2, index % 2]).astype(jnp.int32)
    table = jnp.asarray(rotary_tables(length))
    smem = [pl.BlockSpec(memory_space=pltpu.SMEM)]
    inputs = [far_away(value) for value in (query_latent, kv_latent.T, out_grad)]
    width = QL + KL + TILE

    packed, cotangent = pl.pallas_call(
        load_kernel,
        out_shape=(
            pltpu.VMEM((half, width), jnp.bfloat16),
            pltpu.VMEM((length, wide_k), jnp.bfloat16),
        ),
        in_specs=smem + hbm(3),
        out_specs=vmem(2),
        scratch_shapes=[pltpu.VMEM((KL + DR, half), jnp.bfloat16), pltpu.SemaphoreType.DMA((3,))],
        compiler_params=params(),
        cost_estimate=free(),
        name="load",
    )(place, *inputs)
    packed, place = lax.optimization_barrier((packed, place))
    singles = [1 << i for i in reversed(range(n_dp.bit_length() - 1))]
    cotangents = {k: across(cotangent, n_dp, n_head, k) for k in singles}
    received = {k: across(packed, n_dp, n_head, k) for k in singles}

    def rows_shape(rows):
        widths = (QL, KL + DR, wide_q, 2 * wide_k)
        return tuple(pltpu.VMEM((rows, width), jnp.bfloat16) for width in widths)

    def scratch(rows):
        widths = (wide_k, wide_q, 2 * TILE * heads, wide_k)
        return [pltpu.VMEM((rows, width), jnp.bfloat16) for width in widths]

    weights_shape = tuple(
        pltpu.VMEM(shape, jnp.bfloat16) for shape in ((QL, wide_q), (KL, wide_k), (KL, wide_k))
    )
    sums_shape = tuple(pltpu.VMEM(w.shape, jnp.float32) for w in weights_shape)
    *outs, keep, send = pl.pallas_call(
        functools.partial(own_kernel, n_head),
        out_shape=(
            *weights_shape,
            pltpu.VMEM(table.shape, jnp.float32),
            *rows_shape(length),
            struct((half, width), jnp.float32),
            struct((half, width), jnp.bfloat16),
        ),
        in_specs=smem + hbm(7),
        out_specs=vmem(10),
        scratch_shapes=[pltpu.VMEM((KL + DR, length), jnp.bfloat16)]
        + scratch(length)
        + [pltpu.VMEM((length, width), jnp.float32), pltpu.SemaphoreType.DMA((7,))],
        compiler_params=params(),
        cost_estimate=free(),
        name="own",
    )(place, *inputs, *[far_away(value) for value in (query_up, key_up, value_up, table)])
    weights, found = outs[:4], outs[4:]

    rows = length // n_head
    squares_shape = struct((8, TILE), jnp.float32)

    def add_sums(left, right, shapes, sums):
        return list(
            pl.pallas_call(
                functools.partial(sums_kernel, len(shapes), not sums),
                out_shape=shapes,
                in_specs=vmem(2 + len(sums)),
                out_specs=vmem(len(shapes)),
                input_output_aliases={2 + i: i for i in range(len(sums))},
                compiler_params=params(),
                cost_estimate=free(),
                name="sums",
            )(left, right, *sums)
        )

    def add(left, right):
        return pl.pallas_call(
            add_kernel,
            out_shape=squares_shape,
            in_specs=vmem(2),
            out_specs=pl.BlockSpec(memory_space=pltpu.VMEM),
            compiler_params=params(),
            cost_estimate=free(),
            name="add",
        )(left, right)

    sums = add_sums(found[0], found[2], sums_shape[:1], [])
    sums += add_sums(found[1], found[3], sums_shape[1:], [])

    def fold(keep, received):
        half_shape = (keep.shape[0] // 2, width)
        return pl.pallas_call(
            fold_kernel,
            out_shape=(struct(half_shape, jnp.float32), struct(half_shape, jnp.bfloat16)),
            in_specs=vmem(2),
            out_specs=vmem(2),
            compiler_params=params(),
            cost_estimate=free(),
            name="fold",
        )(keep, received)

    stay, go = fold(keep, exchange(send, "head", n_head, 1))
    bits = [2 << i for i in range(n_head.bit_length() - 2)]
    for bit in bits[:-2]:
        stay, go = fold(stay, exchange(go, "head", n_head, bit))
    came = exchange(go, "head", n_head, bits[-2])

    values = [received[k] for k in singles]
    *values, sums[0], sums[2] = lax.optimization_barrier((*values, sums[0], sums[2]))
    received = dict(zip(singles, values))
    values = [cotangents[k] for k in singles]
    relayed, *values = lax.optimization_barrier((received, *values))
    cotangents = dict(zip(singles, values))
    for k in range(3, n_dp):
        if k not in received:
            relayed[k] = across(relayed[k & (k - 1)], n_dp, n_head, k & -k)
            received[k] = relayed[k]
            cotangents[k] = across(cotangents[k & (k - 1)], n_dp, n_head, k & -k)

    def swapped(k):
        return exchange(received[turned_round(k, n_dp)], "head", n_head, 1)

    groups = [(1, 2)] + [(k,) for k in range(3, n_dp)]
    for group in groups:
        n_seq = len(group)
        blocks = []
        for k in group:
            blocks += [received[k], swapped(k), cotangents[k]]
        if group is not groups[0]:
            blocks[1], sums[1] = lax.optimization_barrier((blocks[1], sums[1]))
        found = list(
            pl.pallas_call(
                functools.partial(far_kernel, n_seq),
                out_shape=rows_shape(n_seq * length),
                in_specs=smem + vmem(len(blocks) + 4),
                out_specs=vmem(4),
                scratch_shapes=scratch(n_seq * length),
                compiler_params=params(),
                cost_estimate=free(),
                name="far",
            )(place, *blocks, *weights)
        )
        if group is groups[-1]:
            break
        k = groups[groups.index(group) + 1][0]
        if group is groups[0]:
            came, found[3] = lax.optimization_barrier((came, found[3]))
            stay, go = fold(stay, came)
            go, found[2] = lax.optimization_barrier((go, found[2]))
            terms = [stay, exchange(go, "head", n_head, bits[-1])]
        sums[:1] = add_sums(found[0], found[2], sums_shape[:1], sums[:1])
        received[k], cotangents[k], sums[0] = lax.optimization_barrier(
            (received[k], cotangents[k], sums[0])
        )
        sums[1:] = add_sums(found[1], found[3], sums_shape[1:], sums[1:])

    *sums, squares = pl.pallas_call(
        last_kernel,
        out_shape=(*sums_shape, squares_shape),
        in_specs=vmem(4 + 3),
        out_specs=vmem(4),
        input_output_aliases={4: 0, 5: 1, 6: 2},
        compiler_params=params(),
        cost_estimate=free(),
        name="last",
    )(*found, *sums)

    count = (QL * wide_q + 2 * KL * wide_k) * n_head
    limit = max_rms * count**0.5
    squares = add(squares, exchange(squares, "head", n_head, 1))
    squares, terms[1] = lax.optimization_barrier((squares, terms[1]))
    parts = [squares] + [exchange(squares, "head", n_head, 2 * k) for k in range(1, n_head // 2)]
    *scaled, latent_q, latent_kv = pl.pallas_call(
        functools.partial(scale_kernel, limit),
        out_shape=(
            *[struct(w.shape, jnp.bfloat16) for w in weights_shape],
            struct((rows, QL), jnp.float32),
            struct((rows, KL + DR), jnp.float32),
        ),
        in_specs=vmem(2 + 3 + len(parts)),
        out_specs=hbm(5),
        scratch_shapes=list(weights_shape)
        + [
            pltpu.VMEM((rows, QL), jnp.float32),
            pltpu.VMEM((rows, KL + DR), jnp.float32),
            pltpu.SemaphoreType.DMA((2 + (QL + 2 * KL) // 128,)),
        ],
        compiler_params=params(),
        cost_estimate=free(),
        name="scale",
    )(*terms, *sums, *parts)
    return (latent_q, latent_kv, *scaled)


def solution(mesh):
    placed = (
        P("dp", None),
        P("dp", None),
        P("dp", "head"),
        P(None, "head"),
        P(None, "head"),
        P(None, "head"),
    )
    return jax.shard_map(
        functools.partial(per_device, mesh.shape["dp"], mesh.shape["head"]),
        mesh=mesh,
        in_specs=placed,
        out_specs=(
            P(("dp", "head"), None),
            P(("dp", "head"), None),
            P(None, "head"),
            P(None, "head"),
            P(None, "head"),
        ),
        check_vma=False,
    )
```

```python
import functools

import jax
import jax.numpy as jnp
import numpy as np
from jax import lax
from jax.experimental import pallas as pl
from jax.experimental.pallas import tpu as pltpu
from jax.sharding import PartitionSpec as P

QL = 1536
KL = 512
DN = 128
DR = 64
TILE = 128
WIDTH = DN + DR
PAIR = 2 * WIDTH
LATENT = QL + KL + DR

max_rms = 1.0
eps = 1e-06
VMEM_LIMIT = 32 * 2**20

NT = (((1,), (1,)), ((), ()))
TN = (((0,), (0,)), ((), ()))


def dot(left, right, dims=(((1,), (0,)), ((), ()))):
    return lax.dot_general(left, right, dims, preferred_element_type=jnp.float32)


def rotary_tables(length):
    half = DR // 2
    freqs = np.float32(10000.0) ** (
        np.float32(-2.0) * np.arange(half, dtype=np.float32) / np.float32(DR)
    )
    angle = np.arange(length, dtype=np.float32)[:, None] * freqs.astype(np.float32)[None, :]
    cosine, sine = np.cos(angle), np.sin(angle)
    ones, zeros = np.ones((length, DR), np.float32), np.zeros((length, DR), np.float32)
    return np.concatenate([cosine, cosine, ones, -sine, sine, zeros], axis=1)


def swap_halves(tile):
    lane = lax.broadcasted_iota(jnp.int32, tile.shape, 1)
    first = lane % DR < DR // 2
    return jnp.where(
        first, pltpu.roll(tile, TILE - DR // 2, 1), pltpu.roll(tile, DR // 2, 1)
    )


def rounded(values):
    return values.astype(jnp.bfloat16).astype(jnp.float32)


def softmax_grads(scores, grad_probs):
    length = scores.shape[0]
    block = length // 2
    scale = 1.0 / (DN + DR) ** 0.5
    key = lax.broadcasted_iota(jnp.int32, (block, block), 0)
    query = lax.broadcasted_iota(jnp.int32, (block, block), 1)
    allowed = key <= query
    grad_probs = rounded(grad_probs)
    probs_columns, grads_columns = [], []
    for column in range(2):
        columns = slice(column * block, (column + 1) * block)
        parts = [scores[:block, columns], scores[block:, columns]][: column + 1]
        parts[-1] = jnp.where(allowed, parts[-1], -jnp.inf)
        tops = [jnp.max(part, axis=0, keepdims=True) for part in parts]
        top = tops[0] if column == 0 else jnp.maximum(*tops)
        parts = [jnp.exp((part - top) * scale) for part in parts]
        sums = [jnp.sum(part, axis=0, keepdims=True) for part in parts]
        inverse = 1.0 / (sums[0] if column == 0 else sums[0] + sums[1])
        parts = [part * inverse for part in parts]
        grads = [grad_probs[:block, columns], grad_probs[block:, columns]][: column + 1]
        means = [jnp.sum(g * p, axis=0, keepdims=True) for g, p in zip(grads, parts)]
        mean = means[0] if column == 0 else means[0] + means[1]
        grads = [(p * (g - mean) * scale).astype(jnp.bfloat16) for g, p in zip(grads, parts)]
        parts = [p.astype(jnp.bfloat16) for p in parts]
        if column == 0:
            parts.append(jnp.zeros((block, block), jnp.bfloat16))
            grads.append(jnp.zeros((block, block), jnp.bfloat16))
        probs_columns.append(jnp.concatenate(parts, axis=0))
        grads_columns.append(jnp.concatenate(grads, axis=0))
    return jnp.concatenate(probs_columns, axis=1), jnp.concatenate(grads_columns, axis=1)


def backward(length, xq, xkv, grad, weights, table, gq, gkv, qw, kw, vw, rot_out, ready):
    wq, wk, wv = weights
    n_seq = xq.shape[0] // length
    wide = wk.shape[1]
    heads = wide // DN
    low = lax.broadcasted_iota(jnp.int32, (length, TILE), 1) < DR
    spans = [slice(s * length, (s + 1) * length) for s in range(n_seq)]

    ready[0]()
    cos_low, sin_low = table[:, :TILE], table[:, TILE:]
    cos_tiles = (cos_low, pltpu.roll(cos_low, DR, 1))
    sin_tiles = (sin_low, pltpu.roll(sin_low, DR, 1))
    latent = xkv[:, :KL]
    for pair in range(heads // 2):
        columns = slice(2 * DN * pair, 2 * DN * (pair + 1))
        keys = dot(latent, wk[:, columns])
        vw[:, columns] = dot(latent, wv[:, columns]).astype(jnp.bfloat16)
        for span in spans:
            rot = jnp.concatenate(
                [xkv[span, KL : KL + DR].astype(jnp.float32), jnp.zeros((length, DR), jnp.float32)],
                axis=1,
            )
            odd = pltpu.roll(keys[span, DN:], DR, 1)
            tiles = (
                keys[span, :DN],
                rot,
                jnp.where(low, 0.0, odd),
                jnp.where(low, odd, pltpu.roll(rot, DR, 1)),
            )
            for i, tile in enumerate(tiles):
                start = (4 * pair + i) * TILE
                kw[span, start : start + TILE] = tile.astype(jnp.bfloat16)
    ready[1]()
    for pair in range(heads // 2):
        queries = dot(xq[...], wq[:, PAIR * pair : PAIR * (pair + 1)])
        for span in spans:
            for i in range(3):
                part = rounded(queries[span, i * TILE : (i + 1) * TILE])
                if i > 0:
                    part = part * cos_tiles[i - 1] + swap_halves(part) * sin_tiles[i - 1]
                start = PAIR * pair + i * TILE
                qw[span, start : start + TILE] = part.astype(jnp.bfloat16)

    items = [(span, head) for span in spans for head in range(heads)]

    def windows(span, head):
        start = PAIR * (head // 2) + TILE * (head % 2)
        return (
            qw[span, start : start + 2 * TILE],
            kw[span, 2 * TILE * head : 2 * TILE * (head + 1)],
            slice(head * DN, (head + 1) * DN),
        )

    def first_products(span, head):
        query_window, key_window, columns = windows(span, head)
        return (
            dot(key_window, query_window, NT),
            dot(vw[span, columns], grad[span, columns], NT),
        )

    rot_sums = [jnp.zeros((length, TILE), jnp.float32) for _ in spans]
    even_parts = {}

    def last_products(index, probs, grad_scores):
        span, head = items[index]
        query_window, key_window, columns = windows(span, head)
        gkv[span, wide + head * DN : wide + (head + 1) * DN] = dot(probs, grad[span, columns]).astype(
            jnp.bfloat16
        )
        key_part = dot(grad_scores, query_window)
        query_part = dot(grad_scores, key_window, TN)
        seq = index // heads
        if head % 2 == 0:
            gkv[span, columns] = key_part[:, :TILE].astype(jnp.bfloat16)
            if rot_out is not None:
                rot_sums[seq] = rot_sums[seq] + rounded(key_part[:, TILE:])
            even_parts[index + 1] = query_part
            return
        turned = pltpu.roll(key_part[:, TILE:], DR, 1)
        gkv[span, columns] = jnp.where(low, pltpu.roll(key_part[:, :TILE], DR, 1), turned).astype(
            jnp.bfloat16
        )
        if rot_out is not None:
            rot_sums[seq] = rot_sums[seq] + rounded(turned)
        even_part = even_parts.pop(index)
        parts = [
            even_part[:, :TILE],
            even_part[:, TILE:] + query_part[:, :TILE],
            query_part[:, TILE:],
        ]
        for i in range(3):
            part = parts[i]
            if i > 0:
                part = rounded(part)
                part = part * cos_tiles[i - 1] - swap_halves(part) * sin_tiles[i - 1]
            start = PAIR * (head // 2) + i * TILE
            gq[span, start : start + TILE] = part.astype(jnp.bfloat16)

    ahead = [first_products(*item) for item in items[:2]]
    waiting = None
    for index in range(len(items)):
        found = softmax_grads(*ahead.pop(0))
        if index + 2 < len(items):
            ahead.append(first_products(*items[index + 2]))
        if waiting is not None:
            last_products(index - 1, *waiting)
        waiting = found
    last_products(len(items) - 1, *waiting)
    if rot_out is not None:
        rot_out[...] = rot_sums[0]


def raw_grads(parts, left, right, sums, previous):
    wide = right.shape[1] // parts
    total = jnp.zeros((8, TILE), jnp.float32)
    for start in range(0, sums[0].shape[0], KL):
        rows = slice(start, start + KL)
        product = dot(left[:, rows], right[...], TN)
        for part in range(parts):
            block = product[:, part * wide : (part + 1) * wide]
            if previous is not None:
                block = block + previous[part][rows, :]
            sums[part][rows, :] = block
            folded = jnp.sum((block * block).reshape(KL // 8, 8, wide), axis=0)
            for column in range(0, wide, TILE):
                total = total + folded[:, column : column + TILE]
    return total


def load_kernel(place, xq, kvt, grad, packed, cotangent, kv_rows, sem):
    half = packed.shape[0]
    rows = pl.ds(pl.multiple_of(place[1] * half, half), half)
    pieces = ((kvt.at[:, rows], kv_rows), (xq.at[rows], packed.at[:, :QL]), (grad, cotangent))
    copies = [pltpu.make_async_copy(*piece, sem.at[i]) for i, piece in enumerate(pieces)]
    for copy in copies:
        copy.start()
    copies[0].wait()
    for block in range(0, KL + DR, TILE):
        stop = min(block + TILE, KL + DR)
        packed[:, QL + block : QL + stop] = kv_rows[block:stop, :].T
    packed[:, LATENT:] = jnp.zeros((half, TILE - DR), jnp.bfloat16)
    for copy in copies[1:]:
        copy.wait()


def own_kernel(n_head, place, xq_in, kvt_in, grad_in, wq_in, wk_in, wv_in, table_in, *refs):
    wq, wk, wv, table, xq, xkv, gq, gkv, keep, send, *refs = refs
    kvt, grad, qw, kw, vw, term, sem = refs
    pieces = (
        (kvt_in, kvt),
        (table_in, table),
        (wk_in, wk),
        (wv_in, wv),
        (xq_in, xq),
        (wq_in, wq),
        (grad_in, grad),
    )
    copies = [pltpu.make_async_copy(*piece, sem.at[i]) for i, piece in enumerate(pieces)]
    for copy in copies:
        copy.start()

    def latents_ready():
        for copy in copies[:4]:
            copy.wait()
        for block in range(0, KL + DR, TILE):
            stop = min(block + TILE, KL + DR)
            xkv[:, block:stop] = kvt[block:stop, :].T

    def queries_ready():
        for copy in copies[4:]:
            copy.wait()

    length = xq.shape[0]
    rot = term.at[:, QL + KL :]
    ready = (latents_ready, queries_ready)
    backward(length, xq, xkv, grad, (wq, wk, wv), table, gq, gkv, qw, kw, vw, rot, ready)
    wide = wk.shape[1]
    term[:, :QL] = dot(gq[...], wq[...], NT)
    term[:, QL : QL + KL] = dot(gkv[:, :wide], wk[...], NT) + dot(gkv[:, wide:], wv[...], NT)
    rows = length // n_head
    chip, core = place[0], place[1]
    masks = [turned_round(k, n_head // 2) for k in range(n_head // 2)]

    def chosen(which):
        starts = [(2 * jnp.bitwise_xor(chip, mask) + which) * rows for mask in masks]
        return jnp.concatenate([term[pl.ds(pl.multiple_of(i, rows), rows), :] for i in starts])

    keep[...] = chosen(core)
    send[...] = chosen(1 - core).astype(jnp.bfloat16)


def fold_kernel(keep, received, stay, go):
    total = keep[...] + received[...].astype(jnp.float32)
    stay[...] = total[: stay.shape[0], :]
    go[...] = total[stay.shape[0] :, :].astype(jnp.bfloat16)


def pad_kernel(cotangent, padded):
    length = cotangent.shape[0]
    padded[:length, :] = cotangent[...]
    padded[length:, :] = jnp.zeros((padded.shape[0] - length, padded.shape[1]), padded.dtype)


def far_kernel(n_seq, place, *refs):
    blocks, refs = refs[: 3 * n_seq], refs[3 * n_seq :]
    wq, wk, wv, table, xq, xkv, gq, gkv, grad, qw, kw, vw = refs
    half = blocks[0].shape[0]
    length = 2 * half
    core = place[1]
    for s in range(n_seq):
        mine, other, cotangent = blocks[3 * s : 3 * s + 3]
        for source, side in ((mine, core), (other, 1 - core)):
            rows = pl.ds(pl.multiple_of(s * length + side * half, half), half)
            xq[rows, :] = source[:, :QL]
            xkv[rows, :] = source[:, QL:LATENT]
        grad[s * length : (s + 1) * length, :] = cotangent[:length, :]
    ready = (lambda: None, lambda: None)
    backward(length, xq, xkv, grad, (wq, wk, wv), table, gq, gkv, qw, kw, vw, None, ready)


def sums_kernel(parts, first, left, right, *refs):
    previous, sums = (None, refs) if first else (refs[:parts], refs[parts:])
    raw_grads(parts, left, right, sums, previous)


def last_kernel(xq, xkv, gq, gkv, pq, pk, pv, sq, sk, sv, squares):
    squares[...] = raw_grads(1, xq, gq, (sq,), (pq,)) + raw_grads(2, xkv, gkv, (sk, sv), (pk, pv))


def add_kernel(left, right, out):
    out[...] = left[...] + right[...]


def scale_kernel(limit, local, received, sq, sk, sv, *refs):
    *parts, oq, ok, ov, latent_q, latent_kv, bq, bk, bv, bl, br, sem = refs
    terms = local[...] + received[...].astype(jnp.float32)
    bl[...] = terms[:, :QL]
    br[...] = terms[:, QL:LATENT]
    copies = []
    for buffer, out in ((bl, latent_q), (br, latent_kv)):
        copies.append(pltpu.make_async_copy(buffer, out, sem.at[len(copies)]))
        copies[-1].start()
    total = parts[0][...]
    for part in parts[1:]:
        total = total + part[...]
    total = jnp.sum(total, keepdims=True)
    factor = jnp.minimum(1.0, limit / jnp.sqrt(total + eps))
    for source, buffer, out in ((sq, bq, oq), (sk, bk, ok), (sv, bv, ov)):
        for start in range(0, source.shape[0], 128):
            rows = slice(start, start + 128)
            buffer[rows, :] = (source[rows, :] * factor).astype(jnp.bfloat16)
            copy = pltpu.make_async_copy(buffer.at[rows], out.at[rows], sem.at[len(copies)])
            copy.start()
            copies.append(copy)
    for copy in copies:
        copy.wait()


def vmem(count):
    return [pl.BlockSpec(memory_space=pltpu.VMEM)] * count


def hbm(count):
    return [pl.BlockSpec(memory_space=pltpu.HBM)] * count


def params():
    return pltpu.CompilerParams(vmem_limit_bytes=VMEM_LIMIT)


def free():
    return pl.CostEstimate(flops=0, bytes_accessed=0, transcendentals=0)


def struct(shape, dtype):
    return jax.ShapeDtypeStruct(shape, dtype)


def exchange(value, axis, size, k):
    return lax.ppermute(value, axis, [(i, i ^ k) for i in range(size)])


def far_away(value):
    return pltpu.with_memory_space_constraint(value, pltpu.HBM)


def turned_round(mask, n_dp):
    bits = n_dp.bit_length() - 1
    return sum(((mask >> i) & 1) << (bits - 1 - i) for i in range(bits))


def across(value, n_dp, n_head, mask):
    masks = (mask, turned_round(mask, n_dp))
    pairs = [
        (d * n_head + h, (d ^ masks[h % 2]) * n_head + h) for d in range(n_dp) for h in range(n_head)
    ]
    return lax.ppermute(value, ("dp", "head"), pairs)


def per_device(n_dp, n_head, query_latent, kv_latent, out_grad, query_up, key_up, value_up):
    length = query_latent.shape[0]
    half = length // 2
    wide_q, wide_k = query_up.shape[1], key_up.shape[1]
    heads = wide_k // DN
    index = lax.axis_index("head")
    place = jnp.stack([index // 2, index % 2]).astype(jnp.int32)
    table = jnp.asarray(rotary_tables(length))
    smem = [pl.BlockSpec(memory_space=pltpu.SMEM)]
    inputs = [far_away(value) for value in (query_latent, kv_latent.T, out_grad)]
    width = QL + KL + TILE

    packed, cotangent = pl.pallas_call(
        load_kernel,
        out_shape=(
            pltpu.VMEM((half, width), jnp.bfloat16),
            pltpu.VMEM((length, wide_k), jnp.bfloat16),
        ),
        in_specs=smem + hbm(3),
        out_specs=vmem(2),
        scratch_shapes=[pltpu.VMEM((KL + DR, half), jnp.bfloat16), pltpu.SemaphoreType.DMA((3,))],
        compiler_params=params(),
        cost_estimate=free(),
        name="load",
    )(place, *inputs)
    packed, place = lax.optimization_barrier((packed, place))
    singles = [1 << i for i in reversed(range(n_dp.bit_length() - 1))]
    cotangents = {k: across(cotangent, n_dp, n_head, k) for k in singles}
    received = {k: across(packed, n_dp, n_head, k) for k in singles}

    def rows_shape(rows):
        widths = (QL, KL + DR, wide_q, 2 * wide_k)
        return tuple(pltpu.VMEM((rows, width), jnp.bfloat16) for width in widths)

    def scratch(rows):
        widths = (wide_k, wide_q, 2 * TILE * heads, wide_k)
        return [pltpu.VMEM((rows, width), jnp.bfloat16) for width in widths]

    weights_shape = tuple(
        pltpu.VMEM(shape, jnp.bfloat16) for shape in ((QL, wide_q), (KL, wide_k), (KL, wide_k))
    )
    sums_shape = tuple(pltpu.VMEM(w.shape, jnp.float32) for w in weights_shape)
    *outs, keep, send = pl.pallas_call(
        functools.partial(own_kernel, n_head),
        out_shape=(
            *weights_shape,
            pltpu.VMEM(table.shape, jnp.float32),
            *rows_shape(length),
            struct((half, width), jnp.float32),
            struct((half, width), jnp.bfloat16),
        ),
        in_specs=smem + hbm(7),
        out_specs=vmem(10),
        scratch_shapes=[pltpu.VMEM((KL + DR, length), jnp.bfloat16)]
        + scratch(length)
        + [pltpu.VMEM((length, width), jnp.float32), pltpu.SemaphoreType.DMA((7,))],
        compiler_params=params(),
        cost_estimate=free(),
        name="own",
    )(place, *inputs, *[far_away(value) for value in (query_up, key_up, value_up, table)])
    weights, found = outs[:4], outs[4:]

    rows = length // n_head
    squares_shape = struct((8, TILE), jnp.float32)

    def add_sums(left, right, shapes, sums):
        return list(
            pl.pallas_call(
                functools.partial(sums_kernel, len(shapes), not sums),
                out_shape=shapes,
                in_specs=vmem(2 + len(sums)),
                out_specs=vmem(len(shapes)),
                input_output_aliases={2 + i: i for i in range(len(sums))},
                compiler_params=params(),
                cost_estimate=free(),
                name="sums",
            )(left, right, *sums)
        )

    def add(left, right):
        return pl.pallas_call(
            add_kernel,
            out_shape=squares_shape,
            in_specs=vmem(2),
            out_specs=pl.BlockSpec(memory_space=pltpu.VMEM),
            compiler_params=params(),
            cost_estimate=free(),
            name="add",
        )(left, right)

    sums = add_sums(found[0], found[2], sums_shape[:1], [])
    sums += add_sums(found[1], found[3], sums_shape[1:], [])

    def fold(keep, received):
        half_shape = (keep.shape[0] // 2, width)
        return pl.pallas_call(
            fold_kernel,
            out_shape=(struct(half_shape, jnp.float32), struct(half_shape, jnp.bfloat16)),
            in_specs=vmem(2),
            out_specs=vmem(2),
            compiler_params=params(),
            cost_estimate=free(),
            name="fold",
        )(keep, received)

    stay, go = fold(keep, exchange(send, "head", n_head, 1))
    bits = [2 << i for i in range(n_head.bit_length() - 2)]
    for bit in bits[:-2]:
        stay, go = fold(stay, exchange(go, "head", n_head, bit))
    came = exchange(go, "head", n_head, bits[-2])

    values = [received[k] for k in singles]
    *values, sums[0], sums[2] = lax.optimization_barrier((*values, sums[0], sums[2]))
    received = dict(zip(singles, values))
    values = [cotangents[k] for k in singles]
    relayed, *values = lax.optimization_barrier((received, *values))
    cotangents = dict(zip(singles, values))
    for k in range(3, n_dp):
        if k not in received:
            relayed[k] = across(relayed[k & (k - 1)], n_dp, n_head, k & -k)
            received[k] = relayed[k]
            source = cotangents[k & (k - 1)]
            if k & (k - 1) in singles:
                source = pl.pallas_call(
                    pad_kernel,
                    out_shape=pltpu.VMEM((length + 32, wide_k), jnp.bfloat16),
                    in_specs=vmem(1),
                    out_specs=pl.BlockSpec(memory_space=pltpu.VMEM),
                    compiler_params=params(),
                    cost_estimate=free(),
                    name="pad",
                )(source)
            cotangents[k] = across(source, n_dp, n_head, k & -k)

    def swapped(k):
        return exchange(received[turned_round(k, n_dp)], "head", n_head, 1)

    groups = [(1, 2)] + [(k,) for k in range(3, n_dp)]
    for group in groups:
        n_seq = len(group)
        blocks = []
        for k in group:
            blocks += [received[k], swapped(k), cotangents[k]]
        if group is not groups[0]:
            blocks[1], sums[1] = lax.optimization_barrier((blocks[1], sums[1]))
        found = list(
            pl.pallas_call(
                functools.partial(far_kernel, n_seq),
                out_shape=rows_shape(n_seq * length),
                in_specs=smem + vmem(len(blocks) + 4),
                out_specs=vmem(4),
                scratch_shapes=scratch(n_seq * length),
                compiler_params=params(),
                cost_estimate=free(),
                name="far",
            )(place, *blocks, *weights)
        )
        if group is groups[-1]:
            break
        k = groups[groups.index(group) + 1][0]
        if group is groups[0]:
            came, found[3] = lax.optimization_barrier((came, found[3]))
            stay, go = fold(stay, came)
            go, found[2] = lax.optimization_barrier((go, found[2]))
            terms = [stay, exchange(go, "head", n_head, bits[-1])]
        sums[:1] = add_sums(found[0], found[2], sums_shape[:1], sums[:1])
        received[k], cotangents[k], sums[0] = lax.optimization_barrier(
            (received[k], cotangents[k], sums[0])
        )
        sums[1:] = add_sums(found[1], found[3], sums_shape[1:], sums[1:])

    *sums, squares = pl.pallas_call(
        last_kernel,
        out_shape=(*sums_shape, squares_shape),
        in_specs=vmem(4 + 3),
        out_specs=vmem(4),
        input_output_aliases={4: 0, 5: 1, 6: 2},
        compiler_params=params(),
        cost_estimate=free(),
        name="last",
    )(*found, *sums)

    count = (QL * wide_q + 2 * KL * wide_k) * n_head
    limit = max_rms * count**0.5
    squares = add(squares, exchange(squares, "head", n_head, 1))
    squares, terms[1] = lax.optimization_barrier((squares, terms[1]))
    parts = [squares] + [exchange(squares, "head", n_head, 2 * k) for k in range(1, n_head // 2)]
    *scaled, latent_q, latent_kv = pl.pallas_call(
        functools.partial(scale_kernel, limit),
        out_shape=(
            *[struct(w.shape, jnp.bfloat16) for w in weights_shape],
            struct((rows, QL), jnp.float32),
            struct((rows, KL + DR), jnp.float32),
        ),
        in_specs=vmem(2 + 3 + len(parts)),
        out_specs=hbm(5),
        scratch_shapes=list(weights_shape)
        + [
            pltpu.VMEM((rows, QL), jnp.float32),
            pltpu.VMEM((rows, KL + DR), jnp.float32),
            pltpu.SemaphoreType.DMA((2 + (QL + 2 * KL) // 128,)),
        ],
        compiler_params=params(),
        cost_estimate=free(),
        name="scale",
    )(*terms, *sums, *parts)
    return (latent_q, latent_kv, *scaled)


def solution(mesh):
    placed = (
        P("dp", None),
        P("dp", None),
        P("dp", "head"),
        P(None, "head"),
        P(None, "head"),
        P(None, "head"),
    )
    return jax.shard_map(
        functools.partial(per_device, mesh.shape["dp"], mesh.shape["head"]),
        mesh=mesh,
        in_specs=placed,
        out_specs=(
            P(("dp", "head"), None),
            P(("dp", "head"), None),
            P(None, "head"),
            P(None, "head"),
            P(None, "head"),
        ),
        check_vma=False,
    )
```

```python
import functools

import jax
import jax.numpy as jnp
import numpy as np
from jax import lax
from jax.experimental import pallas as pl
from jax.experimental.pallas import tpu as pltpu
from jax.sharding import PartitionSpec as P

QL = 1536
KL = 512
DN = 128
DR = 64
TILE = 128
WIDTH = DN + DR
PAIR = 2 * WIDTH
LATENT = QL + KL + DR

max_rms = 1.0
eps = 1e-06
VMEM_LIMIT = 32 * 2**20

NT = (((1,), (1,)), ((), ()))
TN = (((0,), (0,)), ((), ()))


def dot(left, right, dims=(((1,), (0,)), ((), ()))):
    return lax.dot_general(left, right, dims, preferred_element_type=jnp.float32)


def rotary_tables(length):
    half = DR // 2
    freqs = np.float32(10000.0) ** (
        np.float32(-2.0) * np.arange(half, dtype=np.float32) / np.float32(DR)
    )
    angle = np.arange(length, dtype=np.float32)[:, None] * freqs.astype(np.float32)[None, :]
    cosine, sine = np.cos(angle), np.sin(angle)
    ones, zeros = np.ones((length, DR), np.float32), np.zeros((length, DR), np.float32)
    return np.concatenate([cosine, cosine, ones, -sine, sine, zeros], axis=1)


def swap_halves(tile):
    lane = lax.broadcasted_iota(jnp.int32, tile.shape, 1)
    first = lane % DR < DR // 2
    return jnp.where(
        first, pltpu.roll(tile, TILE - DR // 2, 1), pltpu.roll(tile, DR // 2, 1)
    )


def rounded(values):
    return values.astype(jnp.bfloat16).astype(jnp.float32)


def softmax_grads(scores, grad_probs):
    length = scores.shape[0]
    block = length // 2
    scale = 1.0 / (DN + DR) ** 0.5
    key = lax.broadcasted_iota(jnp.int32, (block, block), 0)
    query = lax.broadcasted_iota(jnp.int32, (block, block), 1)
    allowed = key <= query
    grad_probs = rounded(grad_probs)
    probs_columns, grads_columns = [], []
    for column in range(2):
        columns = slice(column * block, (column + 1) * block)
        parts = [scores[:block, columns], scores[block:, columns]][: column + 1]
        parts[-1] = jnp.where(allowed, parts[-1], -jnp.inf)
        tops = [jnp.max(part, axis=0, keepdims=True) for part in parts]
        top = tops[0] if column == 0 else jnp.maximum(*tops)
        parts = [jnp.exp((part - top) * scale) for part in parts]
        sums = [jnp.sum(part, axis=0, keepdims=True) for part in parts]
        inverse = 1.0 / (sums[0] if column == 0 else sums[0] + sums[1])
        parts = [part * inverse for part in parts]
        grads = [grad_probs[:block, columns], grad_probs[block:, columns]][: column + 1]
        means = [jnp.sum(g * p, axis=0, keepdims=True) for g, p in zip(grads, parts)]
        mean = means[0] if column == 0 else means[0] + means[1]
        grads = [(p * (g - mean) * scale).astype(jnp.bfloat16) for g, p in zip(grads, parts)]
        parts = [p.astype(jnp.bfloat16) for p in parts]
        if column == 0:
            parts.append(jnp.zeros((block, block), jnp.bfloat16))
            grads.append(jnp.zeros((block, block), jnp.bfloat16))
        probs_columns.append(jnp.concatenate(parts, axis=0))
        grads_columns.append(jnp.concatenate(grads, axis=0))
    return jnp.concatenate(probs_columns, axis=1), jnp.concatenate(grads_columns, axis=1)


def backward(length, xq, xkv, grad, weights, table, gq, gkv, qw, kw, vw, rot_out, ready):
    wq, wk, wv = weights
    n_seq = xq.shape[0] // length
    wide = wk.shape[1]
    heads = wide // DN
    low = lax.broadcasted_iota(jnp.int32, (length, TILE), 1) < DR
    spans = [slice(s * length, (s + 1) * length) for s in range(n_seq)]

    ready[0]()
    cos_low, sin_low = table[:, :TILE], table[:, TILE:]
    cos_tiles = (cos_low, pltpu.roll(cos_low, DR, 1))
    sin_tiles = (sin_low, pltpu.roll(sin_low, DR, 1))
    latent = xkv[:, :KL]
    for pair in range(heads // 2):
        columns = slice(2 * DN * pair, 2 * DN * (pair + 1))
        keys = dot(latent, wk[:, columns])
        vw[:, columns] = dot(latent, wv[:, columns]).astype(jnp.bfloat16)
        for span in spans:
            rot = jnp.concatenate(
                [xkv[span, KL : KL + DR].astype(jnp.float32), jnp.zeros((length, DR), jnp.float32)],
                axis=1,
            )
            odd = pltpu.roll(keys[span, DN:], DR, 1)
            tiles = (
                keys[span, :DN],
                rot,
                jnp.where(low, 0.0, odd),
                jnp.where(low, odd, pltpu.roll(rot, DR, 1)),
            )
            for i, tile in enumerate(tiles):
                start = (4 * pair + i) * TILE
                kw[span, start : start + TILE] = tile.astype(jnp.bfloat16)
    ready[1]()
    for pair in range(heads // 2):
        queries = dot(xq[...], wq[:, PAIR * pair : PAIR * (pair + 1)])
        for span in spans:
            for i in range(3):
                part = rounded(queries[span, i * TILE : (i + 1) * TILE])
                if i > 0:
                    part = part * cos_tiles[i - 1] + swap_halves(part) * sin_tiles[i - 1]
                start = PAIR * pair + i * TILE
                qw[span, start : start + TILE] = part.astype(jnp.bfloat16)

    items = [(span, head) for span in spans for head in range(heads)]

    def windows(span, head):
        start = PAIR * (head // 2) + TILE * (head % 2)
        return (
            qw[span, start : start + 2 * TILE],
            kw[span, 2 * TILE * head : 2 * TILE * (head + 1)],
            slice(head * DN, (head + 1) * DN),
        )

    def first_products(span, head):
        query_window, key_window, columns = windows(span, head)
        return (
            dot(key_window, query_window, NT),
            dot(vw[span, columns], grad[span, columns], NT),
        )

    rot_sums = [jnp.zeros((length, TILE), jnp.float32) for _ in spans]
    even_parts = {}

    def last_products(index, probs, grad_scores):
        span, head = items[index]
        query_window, key_window, columns = windows(span, head)
        gkv[span, wide + head * DN : wide + (head + 1) * DN] = dot(probs, grad[span, columns]).astype(
            jnp.bfloat16
        )
        key_part = dot(grad_scores, query_window)
        query_part = dot(grad_scores, key_window, TN)
        seq = index // heads
        if head % 2 == 0:
            gkv[span, columns] = key_part[:, :TILE].astype(jnp.bfloat16)
            if rot_out is not None:
                rot_sums[seq] = rot_sums[seq] + rounded(key_part[:, TILE:])
            even_parts[index + 1] = query_part
            return
        turned = pltpu.roll(key_part[:, TILE:], DR, 1)
        gkv[span, columns] = jnp.where(low, pltpu.roll(key_part[:, :TILE], DR, 1), turned).astype(
            jnp.bfloat16
        )
        if rot_out is not None:
            rot_sums[seq] = rot_sums[seq] + rounded(turned)
        even_part = even_parts.pop(index)
        parts = [
            even_part[:, :TILE],
            even_part[:, TILE:] + query_part[:, :TILE],
            query_part[:, TILE:],
        ]
        for i in range(3):
            part = parts[i]
            if i > 0:
                part = rounded(part)
                part = part * cos_tiles[i - 1] - swap_halves(part) * sin_tiles[i - 1]
            start = PAIR * (head // 2) + i * TILE
            gq[span, start : start + TILE] = part.astype(jnp.bfloat16)

    ahead = [first_products(*item) for item in items[:2]]
    waiting = None
    for index in range(len(items)):
        found = softmax_grads(*ahead.pop(0))
        if index + 2 < len(items):
            ahead.append(first_products(*items[index + 2]))
        if waiting is not None:
            last_products(index - 1, *waiting)
        waiting = found
    last_products(len(items) - 1, *waiting)
    if rot_out is not None:
        rot_out[...] = rot_sums[0]


def raw_grads(parts, left, right, sums, previous):
    wide = right.shape[1] // parts
    total = jnp.zeros((8, TILE), jnp.float32)
    for start in range(0, sums[0].shape[0], KL):
        rows = slice(start, start + KL)
        product = dot(left[:, rows], right[...], TN)
        for part in range(parts):
            block = product[:, part * wide : (part + 1) * wide]
            if previous is not None:
                block = block + previous[part][rows, :]
            sums[part][rows, :] = block
            folded = jnp.sum((block * block).reshape(KL // 8, 8, wide), axis=0)
            for column in range(0, wide, TILE):
                total = total + folded[:, column : column + TILE]
    return total


def load_kernel(place, xq, kvt, grad, packed, cotangent, kv_rows, sem):
    half = packed.shape[0]
    rows = pl.ds(pl.multiple_of(place[1] * half, half), half)
    pieces = ((kvt.at[:, rows], kv_rows), (xq.at[rows], packed.at[:, :QL]), (grad, cotangent))
    copies = [pltpu.make_async_copy(*piece, sem.at[i]) for i, piece in enumerate(pieces)]
    for copy in copies:
        copy.start()
    copies[0].wait()
    for block in range(0, KL + DR, TILE):
        stop = min(block + TILE, KL + DR)
        packed[:, QL + block : QL + stop] = kv_rows[block:stop, :].T
    packed[:, LATENT:] = jnp.zeros((half, TILE - DR), jnp.bfloat16)
    for copy in copies[1:]:
        copy.wait()


def own_kernel(n_head, place, xq_in, kvt_in, grad_in, wq_in, wk_in, wv_in, table_in, *refs):
    wq, wk, wv, table, xq, xkv, gq, gkv, keep, send, *refs = refs
    kvt, grad, qw, kw, vw, term, sem = refs
    pieces = (
        (kvt_in, kvt),
        (table_in, table),
        (wk_in, wk),
        (wv_in, wv),
        (xq_in, xq),
        (wq_in, wq),
        (grad_in, grad),
    )
    copies = [pltpu.make_async_copy(*piece, sem.at[i]) for i, piece in enumerate(pieces)]
    for copy in copies:
        copy.start()

    def latents_ready():
        for copy in copies[:4]:
            copy.wait()
        for block in range(0, KL + DR, TILE):
            stop = min(block + TILE, KL + DR)
            xkv[:, block:stop] = kvt[block:stop, :].T

    def queries_ready():
        for copy in copies[4:]:
            copy.wait()

    length = xq.shape[0]
    rot = term.at[:, QL + KL :]
    ready = (latents_ready, queries_ready)
    backward(length, xq, xkv, grad, (wq, wk, wv), table, gq, gkv, qw, kw, vw, rot, ready)
    wide = wk.shape[1]
    term[:, :QL] = dot(gq[...], wq[...], NT)
    term[:, QL : QL + KL] = dot(gkv[:, :wide], wk[...], NT) + dot(gkv[:, wide:], wv[...], NT)
    rows = length // n_head
    chip, core = place[0], place[1]
    masks = [turned_round(k, n_head // 2) for k in range(n_head // 2)]

    def chosen(which):
        starts = [(2 * jnp.bitwise_xor(chip, mask) + which) * rows for mask in masks]
        return jnp.concatenate([term[pl.ds(pl.multiple_of(i, rows), rows), :] for i in starts])

    keep[...] = chosen(core)
    send[...] = chosen(1 - core).astype(jnp.bfloat16)


def fold_kernel(keep, received, stay, go):
    total = keep[...] + received[...].astype(jnp.float32)
    stay[...] = total[: stay.shape[0], :]
    go[...] = total[stay.shape[0] :, :].astype(jnp.bfloat16)


def far_kernel(n_seq, place, *refs):
    blocks, refs = refs[: 3 * n_seq], refs[3 * n_seq :]
    wq, wk, wv, table, xq, xkv, gq, gkv, grad, qw, kw, vw = refs
    half = blocks[0].shape[0]
    length = 2 * half
    core = place[1]
    for s in range(n_seq):
        mine, other, cotangent = blocks[3 * s : 3 * s + 3]
        for source, side in ((mine, core), (other, 1 - core)):
            rows = pl.ds(pl.multiple_of(s * length + side * half, half), half)
            xq[rows, :] = source[:, :QL]
            xkv[rows, :] = source[:, QL:LATENT]
        grad[s * length : (s + 1) * length, :] = cotangent[...]
    ready = (lambda: None, lambda: None)
    backward(length, xq, xkv, grad, (wq, wk, wv), table, gq, gkv, qw, kw, vw, None, ready)


def sums_kernel(parts, first, left, right, *refs):
    previous, sums = (None, refs) if first else (refs[:parts], refs[parts:])
    raw_grads(parts, left, right, sums, previous)


def last_kernel(xq, xkv, gq, gkv, pq, pk, pv, sq, sk, sv, squares):
    squares[...] = raw_grads(1, xq, gq, (sq,), (pq,)) + raw_grads(2, xkv, gkv, (sk, sv), (pk, pv))


def add_kernel(left, right, *outs):
    total = left[...] + right[...]
    for out in outs:
        out[:8, :] = total
        if out.shape[0] > 8:
            out[8:, :] = jnp.zeros((out.shape[0] - 8, TILE), jnp.float32)


def scale_kernel(limit, local, received, sq, sk, sv, *refs):
    *parts, oq, ok, ov, latent_q, latent_kv, bq, bk, bv, bl, br, sem = refs
    terms = local[...] + received[...].astype(jnp.float32)
    bl[...] = terms[:, :QL]
    br[...] = terms[:, QL:LATENT]
    copies = []
    for buffer, out in ((bl, latent_q), (br, latent_kv)):
        copies.append(pltpu.make_async_copy(buffer, out, sem.at[len(copies)]))
        copies[-1].start()
    total = parts[0][...]
    for part in parts[1:]:
        total = total + part[:8, :]
    total = jnp.sum(total, keepdims=True)
    factor = jnp.minimum(1.0, limit / jnp.sqrt(total + eps))
    for source, buffer, out in ((sq, bq, oq), (sk, bk, ok), (sv, bv, ov)):
        for start in range(0, source.shape[0], 128):
            rows = slice(start, start + 128)
            buffer[rows, :] = (source[rows, :] * factor).astype(jnp.bfloat16)
            copy = pltpu.make_async_copy(buffer.at[rows], out.at[rows], sem.at[len(copies)])
            copy.start()
            copies.append(copy)
    for copy in copies:
        copy.wait()


def vmem(count):
    return [pl.BlockSpec(memory_space=pltpu.VMEM)] * count


def hbm(count):
    return [pl.BlockSpec(memory_space=pltpu.HBM)] * count


def params():
    return pltpu.CompilerParams(vmem_limit_bytes=VMEM_LIMIT)


def free():
    return pl.CostEstimate(flops=0, bytes_accessed=0, transcendentals=0)


def struct(shape, dtype):
    return jax.ShapeDtypeStruct(shape, dtype)


def exchange(value, axis, size, k):
    return lax.ppermute(value, axis, [(i, i ^ k) for i in range(size)])


def far_away(value):
    return pltpu.with_memory_space_constraint(value, pltpu.HBM)


def turned_round(mask, n_dp):
    bits = n_dp.bit_length() - 1
    return sum(((mask >> i) & 1) << (bits - 1 - i) for i in range(bits))


def across(value, n_dp, n_head, mask):
    masks = (mask, turned_round(mask, n_dp))
    pairs = [
        (d * n_head + h, (d ^ masks[h % 2]) * n_head + h) for d in range(n_dp) for h in range(n_head)
    ]
    return lax.ppermute(value, ("dp", "head"), pairs)


def per_device(n_dp, n_head, query_latent, kv_latent, out_grad, query_up, key_up, value_up):
    length = query_latent.shape[0]
    half = length // 2
    wide_q, wide_k = query_up.shape[1], key_up.shape[1]
    heads = wide_k // DN
    index = lax.axis_index("head")
    place = jnp.stack([index // 2, index % 2]).astype(jnp.int32)
    table = jnp.asarray(rotary_tables(length))
    smem = [pl.BlockSpec(memory_space=pltpu.SMEM)]
    inputs = [far_away(value) for value in (query_latent, kv_latent.T, out_grad)]
    width = QL + KL + TILE

    packed, cotangent = pl.pallas_call(
        load_kernel,
        out_shape=(
            pltpu.VMEM((half, width), jnp.bfloat16),
            pltpu.VMEM((length, wide_k), jnp.bfloat16),
        ),
        in_specs=smem + hbm(3),
        out_specs=vmem(2),
        scratch_shapes=[pltpu.VMEM((KL + DR, half), jnp.bfloat16), pltpu.SemaphoreType.DMA((3,))],
        compiler_params=params(),
        cost_estimate=free(),
        name="load",
    )(place, *inputs)
    packed, place = lax.optimization_barrier((packed, place))
    singles = [1 << i for i in reversed(range(n_dp.bit_length() - 1))]
    cotangents = {k: across(cotangent, n_dp, n_head, k) for k in singles}
    received = {k: across(packed, n_dp, n_head, k) for k in singles}

    def rows_shape(rows):
        widths = (QL, KL + DR, wide_q, 2 * wide_k)
        return tuple(pltpu.VMEM((rows, width), jnp.bfloat16) for width in widths)

    def scratch(rows):
        widths = (wide_k, wide_q, 2 * TILE * heads, wide_k)
        return [pltpu.VMEM((rows, width), jnp.bfloat16) for width in widths]

    weights_shape = tuple(
        pltpu.VMEM(shape, jnp.bfloat16) for shape in ((QL, wide_q), (KL, wide_k), (KL, wide_k))
    )
    sums_shape = tuple(pltpu.VMEM(w.shape, jnp.float32) for w in weights_shape)
    *outs, keep, send = pl.pallas_call(
        functools.partial(own_kernel, n_head),
        out_shape=(
            *weights_shape,
            pltpu.VMEM(table.shape, jnp.float32),
            *rows_shape(length),
            struct((half, width), jnp.float32),
            struct((half, width), jnp.bfloat16),
        ),
        in_specs=smem + hbm(7),
        out_specs=vmem(10),
        scratch_shapes=[pltpu.VMEM((KL + DR, length), jnp.bfloat16)]
        + scratch(length)
        + [pltpu.VMEM((length, width), jnp.float32), pltpu.SemaphoreType.DMA((7,))],
        compiler_params=params(),
        cost_estimate=free(),
        name="own",
    )(place, *inputs, *[far_away(value) for value in (query_up, key_up, value_up, table)])
    weights, found = outs[:4], outs[4:]

    rows = length // n_head
    squares_shape = struct((8, TILE), jnp.float32)

    def add_sums(left, right, shapes, sums):
        return list(
            pl.pallas_call(
                functools.partial(sums_kernel, len(shapes), not sums),
                out_shape=shapes,
                in_specs=vmem(2 + len(sums)),
                out_specs=vmem(len(shapes)),
                input_output_aliases={2 + i: i for i in range(len(sums))},
                compiler_params=params(),
                cost_estimate=free(),
                name="sums",
            )(left, right, *sums)
        )

    sums = add_sums(found[0], found[2], sums_shape[:1], [])
    sums += add_sums(found[1], found[3], sums_shape[1:], [])

    def fold(keep, received):
        half_shape = (keep.shape[0] // 2, width)
        return pl.pallas_call(
            fold_kernel,
            out_shape=(struct(half_shape, jnp.float32), struct(half_shape, jnp.bfloat16)),
            in_specs=vmem(2),
            out_specs=vmem(2),
            compiler_params=params(),
            cost_estimate=free(),
            name="fold",
        )(keep, received)

    stay, go = fold(keep, exchange(send, "head", n_head, 1))
    bits = [2 << i for i in range(n_head.bit_length() - 2)]
    for bit in bits[:-2]:
        stay, go = fold(stay, exchange(go, "head", n_head, bit))
    came = exchange(go, "head", n_head, bits[-2])

    values = [received[k] for k in singles]
    *values, sums[0], sums[2] = lax.optimization_barrier((*values, sums[0], sums[2]))
    received = dict(zip(singles, values))
    values = [cotangents[k] for k in singles]
    relayed, *values = lax.optimization_barrier((received, *values))
    cotangents = dict(zip(singles, values))
    for k in range(3, n_dp):
        if k not in received:
            relayed[k] = across(relayed[k & (k - 1)], n_dp, n_head, k & -k)
            received[k] = relayed[k]
            cotangents[k] = across(cotangents[k & (k - 1)], n_dp, n_head, k & -k)

    def swapped(k):
        return exchange(received[turned_round(k, n_dp)], "head", n_head, 1)

    groups = [(1, 2)] + [(k,) for k in range(3, n_dp)]
    for group in groups:
        n_seq = len(group)
        blocks = []
        for k in group:
            blocks += [received[k], swapped(k), cotangents[k]]
        if group is not groups[0]:
            blocks[1], sums[1] = lax.optimization_barrier((blocks[1], sums[1]))
        found = list(
            pl.pallas_call(
                functools.partial(far_kernel, n_seq),
                out_shape=rows_shape(n_seq * length),
                in_specs=smem + vmem(len(blocks) + 4),
                out_specs=vmem(4),
                scratch_shapes=scratch(n_seq * length),
                compiler_params=params(),
                cost_estimate=free(),
                name="far",
            )(place, *blocks, *weights)
        )
        if group is groups[-1]:
            break
        k = groups[groups.index(group) + 1][0]
        if group is groups[0]:
            came, found[3] = lax.optimization_barrier((came, found[3]))
            stay, go = fold(stay, came)
            go, found[2] = lax.optimization_barrier((go, found[2]))
            terms = [stay, exchange(go, "head", n_head, bits[-1])]
        sums[:1] = add_sums(found[0], found[2], sums_shape[:1], sums[:1])
        received[k], cotangents[k], sums[0] = lax.optimization_barrier(
            (received[k], cotangents[k], sums[0])
        )
        sums[1:] = add_sums(found[1], found[3], sums_shape[1:], sums[1:])

    *sums, squares = pl.pallas_call(
        last_kernel,
        out_shape=(*sums_shape, squares_shape),
        in_specs=vmem(4 + 3),
        out_specs=vmem(4),
        input_output_aliases={4: 0, 5: 1, 6: 2},
        compiler_params=params(),
        cost_estimate=free(),
        name="last",
    )(*found, *sums)

    count = (QL * wide_q + 2 * KL * wide_k) * n_head
    limit = max_rms * count**0.5
    near, middle, far = pl.pallas_call(
        add_kernel,
        out_shape=tuple(struct((8 * i, TILE), jnp.float32) for i in (1, 2, 3)),
        in_specs=vmem(2),
        out_specs=vmem(3),
        compiler_params=params(),
        cost_estimate=free(),
        name="add",
    )(squares, exchange(squares, "head", n_head, 1))
    parts = [near]
    for k in range(n_head // 2 - 1, 0, -1):
        value = near if k == 1 else middle if k == 2 else far
        if k == 1:
            value, terms[1] = lax.optimization_barrier((value, terms[1]))
        parts.append(exchange(value, "head", n_head, 2 * k))
    *scaled, latent_q, latent_kv = pl.pallas_call(
        functools.partial(scale_kernel, limit),
        out_shape=(
            *[struct(w.shape, jnp.bfloat16) for w in weights_shape],
            struct((rows, QL), jnp.float32),
            struct((rows, KL + DR), jnp.float32),
        ),
        in_specs=vmem(2 + 3 + len(parts)),
        out_specs=hbm(5),
        scratch_shapes=list(weights_shape)
        + [
            pltpu.VMEM((rows, QL), jnp.float32),
            pltpu.VMEM((rows, KL + DR), jnp.float32),
            pltpu.SemaphoreType.DMA((2 + (QL + 2 * KL) // 128,)),
        ],
        compiler_params=params(),
        cost_estimate=free(),
        name="scale",
    )(*terms, *sums, *parts)
    return (latent_q, latent_kv, *scaled)


def solution(mesh):
    placed = (
        P("dp", None),
        P("dp", None),
        P("dp", "head"),
        P(None, "head"),
        P(None, "head"),
        P(None, "head"),
    )
    return jax.shard_map(
        functools.partial(per_device, mesh.shape["dp"], mesh.shape["head"]),
        mesh=mesh,
        in_specs=placed,
        out_specs=(
            P(("dp", "head"), None),
            P(("dp", "head"), None),
            P(None, "head"),
            P(None, "head"),
            P(None, "head"),
        ),
        check_vma=False,
    )
```

```python
import functools

import jax
import jax.numpy as jnp
import numpy as np
from jax import lax
from jax.experimental import pallas as pl
from jax.experimental.pallas import tpu as pltpu
from jax.sharding import PartitionSpec as P

QL = 1536
KL = 512
DN = 128
DR = 64
TILE = 128
WIDTH = DN + DR
PAIR = 2 * WIDTH
LATENT = QL + KL + DR

max_rms = 1.0
eps = 1e-06
VMEM_LIMIT = 32 * 2**20

NT = (((1,), (1,)), ((), ()))
TN = (((0,), (0,)), ((), ()))


def dot(left, right, dims=(((1,), (0,)), ((), ()))):
    return lax.dot_general(left, right, dims, preferred_element_type=jnp.float32)


def rotary_tables(length):
    half = DR // 2
    freqs = np.float32(10000.0) ** (
        np.float32(-2.0) * np.arange(half, dtype=np.float32) / np.float32(DR)
    )
    angle = np.arange(length, dtype=np.float32)[:, None] * freqs.astype(np.float32)[None, :]
    cosine, sine = np.cos(angle), np.sin(angle)
    ones, zeros = np.ones((length, DR), np.float32), np.zeros((length, DR), np.float32)
    return np.concatenate([cosine, cosine, ones, -sine, sine, zeros], axis=1)


def swap_halves(tile):
    lane = lax.broadcasted_iota(jnp.int32, tile.shape, 1)
    first = lane % DR < DR // 2
    return jnp.where(
        first, pltpu.roll(tile, TILE - DR // 2, 1), pltpu.roll(tile, DR // 2, 1)
    )


def rounded(values):
    return values.astype(jnp.bfloat16).astype(jnp.float32)


def softmax_grads(scores, grad_probs):
    length = scores.shape[0]
    block = length // 2
    scale = 1.0 / (DN + DR) ** 0.5
    key = lax.broadcasted_iota(jnp.int32, (block, block), 0)
    query = lax.broadcasted_iota(jnp.int32, (block, block), 1)
    allowed = key <= query
    grad_probs = rounded(grad_probs)
    probs_columns, grads_columns = [], []
    for column in range(2):
        columns = slice(column * block, (column + 1) * block)
        parts = [scores[:block, columns], scores[block:, columns]][: column + 1]
        parts[-1] = jnp.where(allowed, parts[-1], -jnp.inf)
        tops = [jnp.max(part, axis=0, keepdims=True) for part in parts]
        top = tops[0] if column == 0 else jnp.maximum(*tops)
        parts = [jnp.exp((part - top) * scale) for part in parts]
        sums = [jnp.sum(part, axis=0, keepdims=True) for part in parts]
        inverse = 1.0 / (sums[0] if column == 0 else sums[0] + sums[1])
        parts = [part * inverse for part in parts]
        grads = [grad_probs[:block, columns], grad_probs[block:, columns]][: column + 1]
        means = [jnp.sum(g * p, axis=0, keepdims=True) for g, p in zip(grads, parts)]
        mean = means[0] if column == 0 else means[0] + means[1]
        grads = [(p * (g - mean) * scale).astype(jnp.bfloat16) for g, p in zip(grads, parts)]
        parts = [p.astype(jnp.bfloat16) for p in parts]
        if column == 0:
            parts.append(jnp.zeros((block, block), jnp.bfloat16))
            grads.append(jnp.zeros((block, block), jnp.bfloat16))
        probs_columns.append(jnp.concatenate(parts, axis=0))
        grads_columns.append(jnp.concatenate(grads, axis=0))
    return jnp.concatenate(probs_columns, axis=1), jnp.concatenate(grads_columns, axis=1)


def backward(length, xq, xkv, grad, weights, table, gq, gkv, qw, kw, vw, rot_out, ready):
    wq, wk, wv = weights
    n_seq = xq.shape[0] // length
    wide = wk.shape[1]
    heads = wide // DN
    low = lax.broadcasted_iota(jnp.int32, (length, TILE), 1) < DR
    spans = [slice(s * length, (s + 1) * length) for s in range(n_seq)]

    ready[0]()
    cos_low, sin_low = table[:, :TILE], table[:, TILE:]
    cos_tiles = (cos_low, pltpu.roll(cos_low, DR, 1))
    sin_tiles = (sin_low, pltpu.roll(sin_low, DR, 1))
    latent = xkv[:, :KL]
    for pair in range(heads // 2):
        columns = slice(2 * DN * pair, 2 * DN * (pair + 1))
        keys = dot(latent, wk[:, columns])
        vw[:, columns] = dot(latent, wv[:, columns]).astype(jnp.bfloat16)
        for span in spans:
            rot = jnp.concatenate(
                [xkv[span, KL : KL + DR].astype(jnp.float32), jnp.zeros((length, DR), jnp.float32)],
                axis=1,
            )
            odd = pltpu.roll(keys[span, DN:], DR, 1)
            tiles = (
                keys[span, :DN],
                rot,
                jnp.where(low, 0.0, odd),
                jnp.where(low, odd, pltpu.roll(rot, DR, 1)),
            )
            for i, tile in enumerate(tiles):
                start = (4 * pair + i) * TILE
                kw[span, start : start + TILE] = tile.astype(jnp.bfloat16)
    ready[1]()
    for pair in range(heads // 2):
        queries = dot(xq[...], wq[:, PAIR * pair : PAIR * (pair + 1)])
        for span in spans:
            for i in range(3):
                part = rounded(queries[span, i * TILE : (i + 1) * TILE])
                if i > 0:
                    part = part * cos_tiles[i - 1] + swap_halves(part) * sin_tiles[i - 1]
                start = PAIR * pair + i * TILE
                qw[span, start : start + TILE] = part.astype(jnp.bfloat16)

    items = [(span, head) for span in spans for head in range(heads)]

    def windows(span, head):
        start = PAIR * (head // 2) + TILE * (head % 2)
        return (
            qw[span, start : start + 2 * TILE],
            kw[span, 2 * TILE * head : 2 * TILE * (head + 1)],
            slice(head * DN, (head + 1) * DN),
        )

    def first_products(span, head):
        query_window, key_window, columns = windows(span, head)
        return (
            dot(key_window, query_window, NT),
            dot(vw[span, columns], grad[span, columns], NT),
        )

    rot_sums = [jnp.zeros((length, TILE), jnp.float32) for _ in spans]
    even_parts = {}

    def last_products(index, probs, grad_scores):
        span, head = items[index]
        query_window, key_window, columns = windows(span, head)
        gkv[span, wide + head * DN : wide + (head + 1) * DN] = dot(probs, grad[span, columns]).astype(
            jnp.bfloat16
        )
        key_part = dot(grad_scores, query_window)
        query_part = dot(grad_scores, key_window, TN)
        seq = index // heads
        if head % 2 == 0:
            gkv[span, columns] = key_part[:, :TILE].astype(jnp.bfloat16)
            if rot_out is not None:
                rot_sums[seq] = rot_sums[seq] + rounded(key_part[:, TILE:])
            even_parts[index + 1] = query_part
            return
        turned = pltpu.roll(key_part[:, TILE:], DR, 1)
        gkv[span, columns] = jnp.where(low, pltpu.roll(key_part[:, :TILE], DR, 1), turned).astype(
            jnp.bfloat16
        )
        if rot_out is not None:
            rot_sums[seq] = rot_sums[seq] + rounded(turned)
        even_part = even_parts.pop(index)
        parts = [
            even_part[:, :TILE],
            even_part[:, TILE:] + query_part[:, :TILE],
            query_part[:, TILE:],
        ]
        for i in range(3):
            part = parts[i]
            if i > 0:
                part = rounded(part)
                part = part * cos_tiles[i - 1] - swap_halves(part) * sin_tiles[i - 1]
            start = PAIR * (head // 2) + i * TILE
            gq[span, start : start + TILE] = part.astype(jnp.bfloat16)

    ahead = [first_products(*item) for item in items[:2]]
    waiting = None
    for index in range(len(items)):
        found = softmax_grads(*ahead.pop(0))
        if index + 2 < len(items):
            ahead.append(first_products(*items[index + 2]))
        if waiting is not None:
            last_products(index - 1, *waiting)
        waiting = found
    last_products(len(items) - 1, *waiting)
    if rot_out is not None:
        rot_out[...] = rot_sums[0]


def raw_grads(parts, left, right, sums, previous):
    wide = right.shape[1] // parts
    total = jnp.zeros((8, TILE), jnp.float32)
    for start in range(0, sums[0].shape[0], KL):
        rows = slice(start, start + KL)
        product = dot(left[:, rows], right[...], TN)
        for part in range(parts):
            block = product[:, part * wide : (part + 1) * wide]
            if previous is not None:
                block = block + previous[part][rows, :]
            sums[part][rows, :] = block
            folded = jnp.sum((block * block).reshape(KL // 8, 8, wide), axis=0)
            for column in range(0, wide, TILE):
                total = total + folded[:, column : column + TILE]
    return total


def load_kernel(place, xq, kvt, grad, packed, cotangent, kv_rows, sem):
    half = packed.shape[0]
    rows = pl.ds(pl.multiple_of(place[1] * half, half), half)
    pieces = ((kvt.at[:, rows], kv_rows), (xq.at[rows], packed.at[:, :QL]), (grad, cotangent))
    copies = [pltpu.make_async_copy(*piece, sem.at[i]) for i, piece in enumerate(pieces)]
    for copy in copies:
        copy.start()
    copies[0].wait()
    for block in range(0, KL + DR, TILE):
        stop = min(block + TILE, KL + DR)
        packed[:, QL + block : QL + stop] = kv_rows[block:stop, :].T
    packed[:, LATENT:] = jnp.zeros((half, TILE - DR), jnp.bfloat16)
    for copy in copies[1:]:
        copy.wait()


def own_kernel(n_head, place, xq_in, kvt_in, grad_in, wq_in, wk_in, wv_in, table_in, *refs):
    wq, wk, wv, table, xq, xkv, gq, gkv, keep, send, *refs = refs
    kvt, grad, qw, kw, vw, term, sem = refs
    pieces = (
        (kvt_in, kvt),
        (table_in, table),
        (wk_in, wk),
        (wv_in, wv),
        (xq_in, xq),
        (wq_in, wq),
        (grad_in, grad),
    )
    copies = [pltpu.make_async_copy(*piece, sem.at[i]) for i, piece in enumerate(pieces)]
    for copy in copies:
        copy.start()

    def latents_ready():
        for copy in copies[:4]:
            copy.wait()
        for block in range(0, KL + DR, TILE):
            stop = min(block + TILE, KL + DR)
            xkv[:, block:stop] = kvt[block:stop, :].T

    def queries_ready():
        for copy in copies[4:]:
            copy.wait()

    length = xq.shape[0]
    rot = term.at[:, QL + KL :]
    ready = (latents_ready, queries_ready)
    backward(length, xq, xkv, grad, (wq, wk, wv), table, gq, gkv, qw, kw, vw, rot, ready)
    wide = wk.shape[1]
    term[:, :QL] = dot(gq[...], wq[...], NT)
    term[:, QL : QL + KL] = dot(gkv[:, :wide], wk[...], NT) + dot(gkv[:, wide:], wv[...], NT)
    rows = length // n_head
    chip, core = place[0], place[1]
    masks = [turned_round(k, n_head // 2) for k in range(n_head // 2)]

    def chosen(which):
        starts = [(2 * jnp.bitwise_xor(chip, mask) + which) * rows for mask in masks]
        return jnp.concatenate([term[pl.ds(pl.multiple_of(i, rows), rows), :] for i in starts])

    keep[...] = chosen(core)
    send[...] = chosen(1 - core).astype(jnp.bfloat16)


def fold_kernel(keep, received, stay, go):
    total = keep[...] + received[...].astype(jnp.float32)
    stay[...] = total[: stay.shape[0], :]
    go[...] = total[stay.shape[0] :, :].astype(jnp.bfloat16)


def pad_kernel(cotangent, padded):
    length = cotangent.shape[0]
    padded[:length, :] = cotangent[...]
    padded[length:, :] = jnp.zeros((padded.shape[0] - length, padded.shape[1]), padded.dtype)


def far_kernel(n_seq, place, *refs):
    blocks, refs = refs[: 3 * n_seq], refs[3 * n_seq :]
    wq, wk, wv, table, xq, xkv, gq, gkv, grad, qw, kw, vw = refs
    half = blocks[0].shape[0]
    length = 2 * half
    core = place[1]
    for s in range(n_seq):
        mine, other, cotangent = blocks[3 * s : 3 * s + 3]
        for source, side in ((mine, core), (other, 1 - core)):
            rows = pl.ds(pl.multiple_of(s * length + side * half, half), half)
            xq[rows, :] = source[:, :QL]
            xkv[rows, :] = source[:, QL:LATENT]
        grad[s * length : (s + 1) * length, :] = cotangent[:length, :]
    ready = (lambda: None, lambda: None)
    backward(length, xq, xkv, grad, (wq, wk, wv), table, gq, gkv, qw, kw, vw, None, ready)


def sums_kernel(parts, first, left, right, *refs):
    previous, sums = (None, refs) if first else (refs[:parts], refs[parts:])
    raw_grads(parts, left, right, sums, previous)


def last_kernel(xq, xkv, gq, gkv, pq, pk, pv, sq, sk, sv, squares):
    squares[...] = raw_grads(1, xq, gq, (sq,), (pq,)) + raw_grads(2, xkv, gkv, (sk, sv), (pk, pv))


def add_kernel(left, right, *outs):
    total = left[...] + right[...]
    for out in outs:
        out[:8, :] = total
        if out.shape[0] > 8:
            out[8:, :] = jnp.zeros((out.shape[0] - 8, TILE), jnp.float32)


def scale_kernel(limit, local, received, sq, sk, sv, *refs):
    *parts, oq, ok, ov, latent_q, latent_kv, bq, bk, bv, bl, br, sem = refs
    terms = local[...] + received[...].astype(jnp.float32)
    bl[...] = terms[:, :QL]
    br[...] = terms[:, QL:LATENT]
    copies = []
    for buffer, out in ((bl, latent_q), (br, latent_kv)):
        copies.append(pltpu.make_async_copy(buffer, out, sem.at[len(copies)]))
        copies[-1].start()
    total = parts[0][...]
    for part in parts[1:]:
        total = total + part[:8, :]
    total = jnp.sum(total, keepdims=True)
    factor = jnp.minimum(1.0, limit / jnp.sqrt(total + eps))
    for source, buffer, out in ((sq, bq, oq), (sk, bk, ok), (sv, bv, ov)):
        for start in range(0, source.shape[0], 128):
            rows = slice(start, start + 128)
            buffer[rows, :] = (source[rows, :] * factor).astype(jnp.bfloat16)
            copy = pltpu.make_async_copy(buffer.at[rows], out.at[rows], sem.at[len(copies)])
            copy.start()
            copies.append(copy)
    for copy in copies:
        copy.wait()


def vmem(count):
    return [pl.BlockSpec(memory_space=pltpu.VMEM)] * count


def hbm(count):
    return [pl.BlockSpec(memory_space=pltpu.HBM)] * count


def params():
    return pltpu.CompilerParams(vmem_limit_bytes=VMEM_LIMIT)


def free():
    return pl.CostEstimate(flops=0, bytes_accessed=0, transcendentals=0)


def struct(shape, dtype):
    return jax.ShapeDtypeStruct(shape, dtype)


def exchange(value, axis, size, k):
    return lax.ppermute(value, axis, [(i, i ^ k) for i in range(size)])


def far_away(value):
    return pltpu.with_memory_space_constraint(value, pltpu.HBM)


def turned_round(mask, n_dp):
    bits = n_dp.bit_length() - 1
    return sum(((mask >> i) & 1) << (bits - 1 - i) for i in range(bits))


def across(value, n_dp, n_head, mask):
    masks = (mask, turned_round(mask, n_dp))
    pairs = [
        (d * n_head + h, (d ^ masks[h % 2]) * n_head + h) for d in range(n_dp) for h in range(n_head)
    ]
    return lax.ppermute(value, ("dp", "head"), pairs)


def per_device(n_dp, n_head, query_latent, kv_latent, out_grad, query_up, key_up, value_up):
    length = query_latent.shape[0]
    half = length // 2
    wide_q, wide_k = query_up.shape[1], key_up.shape[1]
    heads = wide_k // DN
    index = lax.axis_index("head")
    place = jnp.stack([index // 2, index % 2]).astype(jnp.int32)
    table = jnp.asarray(rotary_tables(length))
    smem = [pl.BlockSpec(memory_space=pltpu.SMEM)]
    inputs = [far_away(value) for value in (query_latent, kv_latent.T, out_grad)]
    width = QL + KL + TILE

    packed, cotangent = pl.pallas_call(
        load_kernel,
        out_shape=(
            pltpu.VMEM((half, width), jnp.bfloat16),
            pltpu.VMEM((length, wide_k), jnp.bfloat16),
        ),
        in_specs=smem + hbm(3),
        out_specs=vmem(2),
        scratch_shapes=[pltpu.VMEM((KL + DR, half), jnp.bfloat16), pltpu.SemaphoreType.DMA((3,))],
        compiler_params=params(),
        cost_estimate=free(),
        name="load",
    )(place, *inputs)
    packed, place = lax.optimization_barrier((packed, place))
    singles = [1 << i for i in reversed(range(n_dp.bit_length() - 1))]
    cotangents = {k: across(cotangent, n_dp, n_head, k) for k in singles}
    received = {k: across(packed, n_dp, n_head, k) for k in singles}

    def rows_shape(rows):
        widths = (QL, KL + DR, wide_q, 2 * wide_k)
        return tuple(pltpu.VMEM((rows, width), jnp.bfloat16) for width in widths)

    def scratch(rows):
        widths = (wide_k, wide_q, 2 * TILE * heads, wide_k)
        return [pltpu.VMEM((rows, width), jnp.bfloat16) for width in widths]

    weights_shape = tuple(
        pltpu.VMEM(shape, jnp.bfloat16) for shape in ((QL, wide_q), (KL, wide_k), (KL, wide_k))
    )
    sums_shape = tuple(pltpu.VMEM(w.shape, jnp.float32) for w in weights_shape)
    *outs, keep, send = pl.pallas_call(
        functools.partial(own_kernel, n_head),
        out_shape=(
            *weights_shape,
            pltpu.VMEM(table.shape, jnp.float32),
            *rows_shape(length),
            struct((half, width), jnp.float32),
            struct((half, width), jnp.bfloat16),
        ),
        in_specs=smem + hbm(7),
        out_specs=vmem(10),
        scratch_shapes=[pltpu.VMEM((KL + DR, length), jnp.bfloat16)]
        + scratch(length)
        + [pltpu.VMEM((length, width), jnp.float32), pltpu.SemaphoreType.DMA((7,))],
        compiler_params=params(),
        cost_estimate=free(),
        name="own",
    )(place, *inputs, *[far_away(value) for value in (query_up, key_up, value_up, table)])
    weights, found = outs[:4], outs[4:]

    rows = length // n_head
    squares_shape = struct((8, TILE), jnp.float32)

    def add_sums(left, right, shapes, sums):
        return list(
            pl.pallas_call(
                functools.partial(sums_kernel, len(shapes), not sums),
                out_shape=shapes,
                in_specs=vmem(2 + len(sums)),
                out_specs=vmem(len(shapes)),
                input_output_aliases={2 + i: i for i in range(len(sums))},
                compiler_params=params(),
                cost_estimate=free(),
                name="sums",
            )(left, right, *sums)
        )

    sums = add_sums(found[0], found[2], sums_shape[:1], [])
    sums += add_sums(found[1], found[3], sums_shape[1:], [])

    def fold(keep, received):
        half_shape = (keep.shape[0] // 2, width)
        return pl.pallas_call(
            fold_kernel,
            out_shape=(struct(half_shape, jnp.float32), struct(half_shape, jnp.bfloat16)),
            in_specs=vmem(2),
            out_specs=vmem(2),
            compiler_params=params(),
            cost_estimate=free(),
            name="fold",
        )(keep, received)

    stay, go = fold(keep, exchange(send, "head", n_head, 1))
    bits = [2 << i for i in range(n_head.bit_length() - 2)]
    for bit in bits[:-2]:
        stay, go = fold(stay, exchange(go, "head", n_head, bit))
    came = exchange(go, "head", n_head, bits[-2])

    values = [received[k] for k in singles]
    *values, sums[0], sums[2] = lax.optimization_barrier((*values, sums[0], sums[2]))
    received = dict(zip(singles, values))
    values = [cotangents[k] for k in singles]
    relayed, *values = lax.optimization_barrier((received, *values))
    cotangents = dict(zip(singles, values))
    for k in range(3, n_dp):
        if k not in received:
            relayed[k] = across(relayed[k & (k - 1)], n_dp, n_head, k & -k)
            received[k] = relayed[k]
            source = cotangents[k & (k - 1)]
            if k & (k - 1) in singles:
                source = pl.pallas_call(
                    pad_kernel,
                    out_shape=pltpu.VMEM((length + 32, wide_k), jnp.bfloat16),
                    in_specs=vmem(1),
                    out_specs=pl.BlockSpec(memory_space=pltpu.VMEM),
                    compiler_params=params(),
                    cost_estimate=free(),
                    name="pad",
                )(source)
            cotangents[k] = across(source, n_dp, n_head, k & -k)

    def swapped(k):
        return exchange(received[turned_round(k, n_dp)], "head", n_head, 1)

    groups = [(1, 2)] + [(k,) for k in range(3, n_dp)]
    for group in groups:
        n_seq = len(group)
        blocks = []
        for k in group:
            blocks += [received[k], swapped(k), cotangents[k]]
        if group is not groups[0]:
            blocks[1], sums[1] = lax.optimization_barrier((blocks[1], sums[1]))
        found = list(
            pl.pallas_call(
                functools.partial(far_kernel, n_seq),
                out_shape=rows_shape(n_seq * length),
                in_specs=smem + vmem(len(blocks) + 4),
                out_specs=vmem(4),
                scratch_shapes=scratch(n_seq * length),
                compiler_params=params(),
                cost_estimate=free(),
                name="far",
            )(place, *blocks, *weights)
        )
        if group is groups[-1]:
            break
        k = groups[groups.index(group) + 1][0]
        if group is groups[0]:
            came, found[3] = lax.optimization_barrier((came, found[3]))
            stay, go = fold(stay, came)
            go, found[2] = lax.optimization_barrier((go, found[2]))
            terms = [stay, exchange(go, "head", n_head, bits[-1])]
        sums[:1] = add_sums(found[0], found[2], sums_shape[:1], sums[:1])
        received[k], cotangents[k], sums[0] = lax.optimization_barrier(
            (received[k], cotangents[k], sums[0])
        )
        sums[1:] = add_sums(found[1], found[3], sums_shape[1:], sums[1:])

    *sums, squares = pl.pallas_call(
        last_kernel,
        out_shape=(*sums_shape, squares_shape),
        in_specs=vmem(4 + 3),
        out_specs=vmem(4),
        input_output_aliases={4: 0, 5: 1, 6: 2},
        compiler_params=params(),
        cost_estimate=free(),
        name="last",
    )(*found, *sums)

    count = (QL * wide_q + 2 * KL * wide_k) * n_head
    limit = max_rms * count**0.5
    near, middle, far = pl.pallas_call(
        add_kernel,
        out_shape=tuple(struct((8 * i, TILE), jnp.float32) for i in (1, 2, 3)),
        in_specs=vmem(2),
        out_specs=vmem(3),
        compiler_params=params(),
        cost_estimate=free(),
        name="add",
    )(squares, exchange(squares, "head", n_head, 1))
    parts = [near]
    for k in range(n_head // 2 - 1, 0, -1):
        value = near if k == 1 else middle if k == 2 else far
        if k == 1:
            value, terms[1] = lax.optimization_barrier((value, terms[1]))
        parts.append(exchange(value, "head", n_head, 2 * k))
    *scaled, latent_q, latent_kv = pl.pallas_call(
        functools.partial(scale_kernel, limit),
        out_shape=(
            *[struct(w.shape, jnp.bfloat16) for w in weights_shape],
            struct((rows, QL), jnp.float32),
            struct((rows, KL + DR), jnp.float32),
        ),
        in_specs=vmem(2 + 3 + len(parts)),
        out_specs=hbm(5),
        scratch_shapes=list(weights_shape)
        + [
            pltpu.VMEM((rows, QL), jnp.float32),
            pltpu.VMEM((rows, KL + DR), jnp.float32),
            pltpu.SemaphoreType.DMA((2 + (QL + 2 * KL) // 128,)),
        ],
        compiler_params=params(),
        cost_estimate=free(),
        name="scale",
    )(*terms, *sums, *parts)
    return (latent_q, latent_kv, *scaled)


def solution(mesh):
    placed = (
        P("dp", None),
        P("dp", None),
        P("dp", "head"),
        P(None, "head"),
        P(None, "head"),
        P(None, "head"),
    )
    return jax.shard_map(
        functools.partial(per_device, mesh.shape["dp"], mesh.shape["head"]),
        mesh=mesh,
        in_specs=placed,
        out_specs=(
            P(("dp", "head"), None),
            P(("dp", "head"), None),
            P(None, "head"),
            P(None, "head"),
            P(None, "head"),
        ),
        check_vma=False,
    )
```
